32 devices in a mesh: section: 2 (over y), fsdp: 4 (over z), replica: 4 (over x, core).
Axes of the slice: x: 2, y: 2, z: 4, core: 2. Of those that a mesh axis runs over, the one named last changes fastest.
Arguments:
- tokens: bfloat16 [2, 4, 512, 1536], P(None, 'replica', 'fsdp'), may hold values from -6 to 6
- cotangent: bfloat16 [2, 4, 512, 1536], P(None, 'replica', 'fsdp'), may hold values from -6 to 6
- seq_lengths: int32 [2, 4, 4], P(None, 'replica'), may hold values from 1 to 509, as said below
- routes: int32 [2, 2, 4, 512, 4], P('section', None, 'replica', 'fsdp'), may hold values from 0 to 7, all different within a row; in each aligned block of 128 rows (0 to 127, 128 to 255, ..., all dimensions but the last counted through in order) at most 64 rows name the same one
- gains: bfloat16 [2, 2, 1536], P('section', None, 'fsdp'), may hold values from 0.5 to 1.5
- w_query: bfloat16 [2, 1536, 1536], P('section', 'fsdp'), may hold values from -0.15625 to 0.15625
- w_key: bfloat16 [2, 1536, 256], P('section', 'fsdp'), may hold values from -0.15625 to 0.15625
- w_value: bfloat16 [2, 1536, 256], P('section', 'fsdp'), may hold values from -0.15625 to 0.15625
- w_out: bfloat16 [2, 1536, 1536], P('section', 'fsdp'), may hold values from -1.25 to 1.25
- w_router: bfloat16 [2, 1536, 8], P('section', 'fsdp'), may hold values from -0.078125 to 0.078125
- w_gate: bfloat16 [2, 8, 1536, 768], P('section', 'fsdp'), may hold values from -0.15625 to 0.15625
- w_up: bfloat16 [2, 8, 1536, 768], P('section', 'fsdp'), may hold values from -0.15625 to 0.15625
- w_down: bfloat16 [2, 8, 768, 1536], P('section', 'fsdp'), may hold values from -0.21875 to 0.21875
Outputs:
- layer_outputs: bfloat16 [2, 2, 4, 512, 1536], P('section', None, 'replica', 'fsdp')
- input_grads: bfloat16 [2, 2, 4, 512, 1536], P('section', None, 'replica', 'fsdp')
- grad_gains: float32 [2, 2, 1536], P('section', None, 'fsdp')
- grad_query: float32 [2, 1536, 1536], P('section', 'fsdp')
- grad_key: float32 [2, 1536, 256], P('section', 'fsdp')
- grad_value: float32 [2, 1536, 256], P('section', 'fsdp')
- grad_out: float32 [2, 1536, 1536], P('section', 'fsdp')
- grad_router: float32 [2, 1536, 8], P('section', 'fsdp')
- grad_gate: float32 [2, 8, 1536, 768], P('section', 'fsdp')
- grad_up: float32 [2, 8, 1536, 768], P('section', 'fsdp')
- grad_down: float32 [2, 8, 768, 1536], P('section', 'fsdp')
The draws below stay inside these ranges and needn't reach their ends.
Inputs may be any that keep to these rules, and one draw needn't show every extreme that they name: `routes`: each row names 4 different experts; in each aligned block of 128 rows every expert is named by exactly 64 rows. `seq_lengths`: the 4 lengths of a pack are positive and sum to 512; the second sequence of each pack begins among its first 128 tokens and ends among its last 128.
All inputs are finite; a program needn't handle non-finite values.
Results may differ from the reference program's by a relative error of at most 0.028.
Values may be sent and summed in bfloat16 or wider, within the bound.
No kernel may reach another device: no remote copies, remote signals or barrier semaphores. Data moves between devices by JAX's collectives and lax.ppermute only.
A program may use at most 256 MiB of HBM per device.

```python
import math
import jax
import jax.numpy as jnp
import numpy as np
from jax import lax

D = 1536
HEADS = 12
KV_HEADS = 2
HEAD = 128
FF = 768
TOP = 4
MB = 2
NSEG = 4
TOK_DEV = 128
LAYERS = 2
QD = 1536
KVD = 256
EXPERTS = 8
PACK = 512
PACKS = 4
CAP = 64


def draw_seq_lengths(key, part):
    key = jax.random.fold_in(key, 11)
    key_left, key_right, key_cut = jax.random.split(key, 3)
    left_len = jax.random.randint(key_left, (MB, PACKS), 1, TOK_DEV)
    right_len = jax.random.randint(key_right, (MB, PACKS), 2, TOK_DEV)
    left_len = left_len.at[0, 0].set(1)
    right_len = right_len.at[0, 0].set(2)
    cut_len = jax.random.randint(key_cut, (MB, PACKS), 1, right_len)
    longest = PACK - left_len - right_len
    return jnp.stack([left_len, longest, cut_len, right_len - cut_len], axis=-1).astype(jnp.int32)


def block_scale(stream_key, shape, pieces, low, high):
    def one(dim, blocks):
        steps = jax.random.uniform(jax.random.fold_in(jax.random.fold_in(stream_key, 6), dim), (blocks,), jnp.float32, low / len(pieces), high / len(pieces))
        return jnp.repeat(jnp.exp(steps), shape[dim] // blocks).reshape((-1,) + (1,) * (len(shape) - dim - 1))

    factor_of = one(*pieces[0])
    for cut in pieces[1:]:
        factor_of = factor_of * one(*cut)
    return factor_of


def assign_block(stream_key, own, number, rows, count, top, bound, skew):
    sequence = jax.random.permutation(stream_key, count)
    packed, common = shares(count, rows * top, bound, skew, True), shares(count, rows * top, bound, skew, False)
    places = jnp.arange(count)

    def named(sizes, rotation):
        used = int((sizes > 0).sum())
        fixed = max(1, used // 4)
        moved = fixed + (places - fixed + rotation * (used - fixed)) % max(1, count - fixed)
        return jnp.zeros((count,), jnp.int32).at[sequence[jnp.where(places < fixed, places, moved)]].set(jnp.asarray(sizes, jnp.int32))

    sizes = jnp.where(number % 4 == 0, named(packed, number // 4), named(common, number - number // 4 - 1))
    mixed = jax.random.permutation(jax.random.fold_in(own, 3), count)
    giver, receiver = mixed[0:count // 2 * 2:2], mixed[1:count // 2 * 2:2]
    slack = jnp.minimum(sizes[giver] - 1, bound - sizes[receiver]) // 2
    slack = jnp.where((giver == sequence[0]) | (receiver == sequence[0]) | (sizes[receiver] == 0), 0, jnp.maximum(slack, 0))
    moved = jax.random.randint(jax.random.fold_in(own, 4), (count // 2,), 0, 1 << 20) % (slack + 1)
    sizes = sizes.at[giver].add(-moved).at[receiver].add(moved)
    labels = jnp.searchsorted(jnp.cumsum(sizes), jnp.arange(rows * top), side="right").astype(jnp.int32)
    table = labels.reshape(top, rows).T
    table = table[jax.random.permutation(jax.random.fold_in(own, 1), rows)]
    rotation = jax.random.randint(jax.random.fold_in(own, 2), (rows, 1), 0, top)
    return jnp.take_along_axis(table, (jnp.arange(top)[None, :] + rotation) % top, axis=1)


def shares(count, total, most, skew, full):
    weights = [(1 << 20) // math.isqrt(rank ** skew) + 1 for rank in range(1, count + 1)]
    largest = most if full else min(most, max(-(-total // count), total * weights[0] // sum(weights)))
    least = 1 if total - largest >= count - 1 else 0
    counts, surplus = [largest] + [least] * (count - 1), total - largest - least * (count - 1)
    while surplus > 0:
        free = [i for i in range(1, count) if counts[i] < largest] or [i for i in range(1, count) if counts[i] < most]
        mass, left = sum([weights[i] for i in free]), surplus
        for i in free:
            addition = min(most - counts[i], max(1, left * weights[i] // mass), surplus)
            counts[i] = counts[i] + addition
            surplus = surplus - addition
    return np.array(counts)


def normal_values(key, dims, scale, most, cuts=(), kind=jnp.bfloat16):
    level = block_scale(key, dims, cuts, -0.22, 0.18) if cuts else 1.0
    drawn = jax.random.normal(key, dims, jnp.float32) * scale * level
    return jnp.minimum(jnp.maximum(drawn, -most), most).astype(kind)


def setup_inputs(seed: int = 0) -> dict:
    splits = jax.random.split(jax.random.key(seed), 14)
    tokens = normal_values(splits[0], (MB, PACKS, PACK, D), 1.0, 6.0, ((1, 4), (2, 4)))
    cotangent = normal_values(splits[1], (MB, PACKS, PACK, D), 1.0, 6.0, ((1, 4), (2, 4)))
    seq_lengths = draw_seq_lengths(jax.random.fold_in(splits[13], 71), 0)
    routes_keys = jax.random.split(jax.random.fold_in(splits[3], 1), LAYERS * MB * PACKS * PACK // TOK_DEV)
    routes_turns = jax.random.permutation(jax.random.fold_in(splits[3], 3), LAYERS * MB * PACKS * PACK // TOK_DEV)
    routes = jax.vmap(lambda own, number: assign_block(jax.random.fold_in(splits[3], 2), own, number, TOK_DEV, EXPERTS, TOP, CAP, 0))(routes_keys, routes_turns).reshape((LAYERS, MB, PACKS, PACK, TOP))
    gains = jnp.clip(1.0 + 0.1 * jax.random.normal(splits[4], (LAYERS, 2, D), jnp.float32), 0.5, 1.5).astype(jnp.bfloat16)
    w_query = normal_values(splits[5], (LAYERS, D, QD), D ** -0.5, 0.15625, ((0, 2), (1, 4)))
    w_key = normal_values(splits[6], (LAYERS, D, KVD), D ** -0.5, 0.15625, ((0, 2), (1, 4)))
    w_value = normal_values(splits[7], (LAYERS, D, KVD), D ** -0.5, 0.15625, ((0, 2), (1, 4)))
    w_out = normal_values(splits[8], (LAYERS, QD, D), (QD // 64) ** -0.5, 1.25, ((0, 2), (1, 4)))
    w_router = normal_values(splits[9], (LAYERS, D, EXPERTS), (4 * D) ** -0.5, 0.078125, ((0, 2), (1, 4)))
    w_gate = normal_values(splits[10], (LAYERS, EXPERTS, D, FF), D ** -0.5, 0.15625, ((0, 2), (1, 4)))
    w_up = normal_values(splits[11], (LAYERS, EXPERTS, D, FF), D ** -0.5, 0.15625, ((0, 2), (1, 4)))
    w_down = normal_values(splits[12], (LAYERS, EXPERTS, FF, D), FF ** -0.5, 0.21875, ((0, 2), (1, 4)))
    return dict(tokens=tokens, cotangent=cotangent, seq_lengths=seq_lengths, routes=routes, gains=gains, w_query=w_query, w_key=w_key, w_value=w_value, w_out=w_out, w_router=w_router, w_gate=w_gate, w_up=w_up, w_down=w_down)


epsilon = 1e-06
rope_base = 1000000.0
masked_score = -1e+30
highest = lax.Precision.HIGHEST

@jax.custom_vjp
def low(v):
    return lax.optimization_barrier(v.astype(jnp.bfloat16)).astype(jnp.float32)

@jax.custom_vjp
def low_back(v):
    return v

def low_keep(v):
    return (low(v), None)

def low_pass(kept, grad):
    return (grad,)

def back_keep(v):
    return (v, None)

def back_low(kept, grad):
    return (low(grad),)
low.defvjp(low_keep, low_pass)
low_back.defvjp(back_keep, back_low)

def rope_tables(offsets, head_size):
    half_size = head_size // 2
    frequency = rope_base ** (-2.0 * jnp.arange(half_size, dtype=jnp.float32) / head_size)
    angles = offsets[..., None] * frequency
    angles = jnp.concatenate([angles, angles], axis=-1)
    return (jnp.cos(angles)[..., None, :], jnp.sin(angles)[..., None, :])

def rope_turn(values, cosine_table, sine_table):
    half_size = values.shape[-1] // 2
    turned = jnp.concatenate([-values[..., half_size:], values[..., :half_size]], axis=-1)
    return values * cosine_table + turned * sine_table

def pack_layout(lengths, first_row, row_count):
    position = first_row + jnp.arange(row_count, dtype=jnp.int32)
    bounds = jnp.cumsum(lengths).astype(jnp.int32)
    passed = (position[:, None] >= bounds[None, :]).astype(jnp.int32)
    segment = lax.optimization_barrier(jnp.sum(passed, axis=1))
    seq_start = lax.optimization_barrier(jnp.sum(passed * lengths[None, :], axis=1))
    return (position, segment, (position - seq_start).astype(jnp.float32))

def attend_pack(packed_args):
    query_pack, key_pack, value_pack, lengths = packed_args
    position, segment, offsets = pack_layout(lengths, 0, PACK)
    block_rows = min(512, PACK)
    if PACK % block_rows != 0:
        block_rows = PACK
    block_count = PACK // block_rows
    group_count = KV_HEADS
    per_group = HEADS // KV_HEADS

    def one_block(block_args):
        query_block, pos_block, seg_block = block_args
        grouped = query_block.reshape(block_rows, group_count, per_group, HEAD)
        raw_scores = low_back(jnp.einsum('tgha,sga->ghts', grouped, key_pack, precision=highest) * HEAD ** (-0.5))
        allowed = (seg_block[:, None] == segment[None, :]) & (position[None, :] <= pos_block[:, None])
        scores = jnp.where(allowed[None, None], raw_scores, masked_score)
        row_max = lax.optimization_barrier(jnp.max(scores, axis=3, keepdims=True))
        exponent = jnp.exp(scores - row_max)
        probs = exponent / lax.optimization_barrier(jnp.sum(exponent, axis=3, keepdims=True))
        mixed_block = jnp.einsum('ghts,sga->tgha', low(probs), value_pack, precision=highest)
        return mixed_block.reshape(block_rows, HEADS * HEAD)
    block_outs = lax.map(jax.checkpoint(one_block), (query_pack.reshape(block_count, block_rows, HEADS, HEAD), position.reshape(block_count, block_rows), segment.reshape(block_count, block_rows)))
    return block_outs.reshape(PACK, HEADS * HEAD)

def expert_rows(packed_args):
    rows_in, gate_part, up_part, down_part = packed_args
    gate_pre = low_back(jnp.dot(rows_in, gate_part, precision=highest, preferred_element_type=jnp.float32))
    up_pre = low_back(jnp.dot(rows_in, up_part, precision=highest, preferred_element_type=jnp.float32))
    inner_act = low(jax.nn.gelu(gate_pre) * up_pre)
    return low_back(low(jnp.dot(inner_act, down_part, precision=highest, preferred_element_type=jnp.float32)))

def layer_apply(hidden, gain_parts, query_w, key_w, value_w, out_w, router_w, gate_w, up_w, down_w, routes_now, lengths, is_last):
    pack_count = hidden.shape[0]
    norm_scale = lax.rsqrt(lax.optimization_barrier(jnp.mean(hidden * hidden, axis=2, keepdims=True)) + epsilon)
    attn_in = low(hidden * norm_scale * gain_parts[0])
    offsets = jax.vmap(lambda pack_lengths: pack_layout(pack_lengths, 0, PACK)[2])(lengths)
    cosine_table, sine_table = rope_tables(offsets, HEAD)
    query_lin = low_back(jnp.einsum('ptd,de->pte', attn_in, query_w, precision=highest))
    key_lin = low_back(jnp.einsum('ptd,de->pte', attn_in, key_w, precision=highest))
    value_lin = low_back(low(jnp.einsum('ptd,de->pte', attn_in, value_w, precision=highest)))
    query_rot = low(rope_turn(query_lin.reshape(pack_count, PACK, HEADS, HEAD), cosine_table, sine_table))
    key_rot = low(rope_turn(key_lin.reshape(pack_count, PACK, KV_HEADS, HEAD), cosine_table, sine_table))
    value_pack = value_lin.reshape(pack_count, PACK, KV_HEADS, HEAD)
    mixed_out = lax.map(jax.checkpoint(attend_pack), (query_rot, key_rot, value_pack, lengths))
    mixed_low = low_back(low(mixed_out))
    residual_mid = hidden + low_back(jnp.einsum('pte,ed->ptd', mixed_low, out_w, precision=highest))
    scale_two = lax.rsqrt(lax.optimization_barrier(jnp.mean(residual_mid * residual_mid, axis=2, keepdims=True)) + epsilon)
    moe_in = low(residual_mid * scale_two * gain_parts[1])
    logits = jnp.einsum('ptd,de->pte', moe_in, router_w, precision=highest)
    chosen = jnp.take_along_axis(logits, routes_now, axis=2)
    gate_mix = jax.nn.softmax(chosen, axis=2)
    flat_rows = moe_in.reshape(-1, D)
    copies = low_back(jnp.repeat(flat_rows, TOP, axis=0))
    slot_order = jnp.argsort(routes_now.reshape(-1), stable=True).astype(jnp.int32)
    per_expert = copies[slot_order].reshape(EXPERTS, -1, D)
    produced = lax.map(jax.checkpoint(expert_rows), (per_expert, gate_w, up_w, down_w))
    routed = jnp.zeros_like(copies).at[slot_order].set(produced.reshape(-1, D)).reshape(pack_count, PACK, TOP, D)
    result = residual_mid + lax.optimization_barrier(jnp.sum(gate_mix[..., None] * routed, axis=2))
    if is_last:
        return result
    return low_back(low(result))

def reference(tokens, cotangent, seq_lengths, routes, gains, w_query, w_key, w_value, w_out, w_router, w_gate, w_up, w_down):
    weight_list = [part.astype(jnp.float32) for part in (gains, w_query, w_key, w_value, w_out, w_router, w_gate, w_up, w_down)]
    lengths = seq_lengths.reshape(MB * PACKS, NSEG)
    hidden = tokens.astype(jnp.float32).reshape(MB * PACKS, PACK, D)
    back_list = []
    output_list = []
    for layer_index in range(LAYERS):
        routes_now = routes[layer_index].reshape(MB * PACKS, PACK, TOP)

        def apply_layer(layer_in, *weights_now, routes_now=routes_now, is_last=layer_index == LAYERS - 1):
            return layer_apply(layer_in, *weights_now, routes_now, lengths, is_last)
        hidden, back_pass = jax.vjp(apply_layer, hidden, *[part[layer_index] for part in weight_list])
        output_list.append(hidden)
        back_list.append(back_pass)
    gradient = cotangent.astype(jnp.float32).reshape(MB * PACKS, PACK, D)
    input_list = [None] * LAYERS
    grad_list = [None] * LAYERS
    for layer_index in reversed(range(LAYERS)):
        result = back_list[layer_index](gradient)
        gradient = result[0]
        input_list[layer_index] = gradient
        grad_list[layer_index] = result[1:]
    shape_out = (LAYERS, MB, PACKS, PACK, D)
    layer_outputs = jnp.stack(output_list).astype(jnp.bfloat16).reshape(shape_out)
    input_grads = jnp.stack(input_list).astype(jnp.bfloat16).reshape(shape_out)
    stacked = [jnp.stack([grad_list[layer_index][slot] for layer_index in range(LAYERS)]).astype(jnp.float32) for slot in range(9)]
    return (layer_outputs, input_grads, stacked[0], stacked[1], stacked[2], stacked[3], stacked[4], stacked[5], stacked[6], stacked[7], stacked[8])
```

```python
import jax
import jax.numpy as jnp
from jax import lax
from jax.sharding import PartitionSpec as P

HEAD = 128
ROPE_BASE = 1000000.0
EPS = 1e-06
MASKED = -1e30
F32 = jnp.float32
BF16 = jnp.bfloat16
S_AX, F_AX, R_AX = "section", "fsdp", "replica"
HIGHEST = lax.Precision.HIGHEST


def mm(a, b):
    return jnp.dot(a, b, preferred_element_type=F32)


def mm_nt(a, b):
    return lax.dot_general(a, b, (((1,), (1,)), ((), ())), preferred_element_type=F32)


def mm_tn(a, b):
    return lax.dot_general(a, b, (((0,), (0,)), ((), ())), preferred_element_type=F32)


def ein(spec, a, b):
    return jnp.einsum(spec, a, b, preferred_element_type=F32)


def rel_gather(value):
    folds = lax.axis_size(F_AX)
    parts = [value]
    for k in range(1, folds):
        parts.append(lax.ppermute(value, F_AX, [(i, (i + k) % folds) for i in range(folds)]))
    return parts


def rel_scatter(parts):
    folds = lax.axis_size(F_AX)
    total = parts[0].astype(F32)
    for k in range(1, folds):
        got = lax.ppermute(parts[k], F_AX, [(i, (i - k) % folds) for i in range(folds)])
        total = total + got.astype(F32)
    return total


def swap_section(value):
    return lax.ppermute(value, S_AX, [(0, 1), (1, 0)])


def swap_core(value):
    count = lax.axis_size(R_AX)
    return lax.ppermute(value, R_AX, [(i, i ^ 1) for i in range(count)])


def all_chips(value):
    count = lax.axis_size(R_AX) // 2
    mine = lax.axis_index(R_AX) // 2
    buffer = jnp.zeros((count,) + value.shape, value.dtype)
    buffer = lax.dynamic_update_index_in_dim(buffer, value, mine, 0)
    for k in range(1, count):
        pairs = [(2 * i + c, 2 * ((i + k) % count) + c) for i in range(count) for c in range(2)]
        got = lax.ppermute(value, R_AX, pairs)
        buffer = lax.dynamic_update_index_in_dim(buffer, got, (mine - k) % count, 0)
    return buffer


def rope_turn(values, cos, sin):
    half = HEAD // 2
    turned = jnp.concatenate([-values[..., half:], values[..., :half]], axis=-1)
    return values * cos + turned * sin


def rope_back(grads, cos, sin):
    half = HEAD // 2
    scaled = grads * sin
    turned = jnp.concatenate([scaled[..., half:], -scaled[..., :half]], axis=-1)
    return grads * cos + turned


def layout(lengths, position):
    bounds = jnp.cumsum(lengths)
    passed = (position[:, None] >= bounds[None, :]).astype(jnp.int32)
    segment = jnp.sum(passed, axis=1)
    start = jnp.sum(passed * lengths[None, :], axis=1)
    return segment, (position - start).astype(F32)


def gated(gate, up):
    return jax.nn.gelu(gate) * up


def attention_in(hidden, gain, w_qkv, common, kv_width):
    cos, sin = common["cos"], common["sin"]
    rows, width = hidden.shape
    q_width = w_qkv.shape[1] - 2 * kv_width
    scale = lax.rsqrt(jnp.mean(hidden * hidden, axis=1, keepdims=True) + EPS)
    normed = hidden * scale
    attn_in = (normed * gain.astype(F32)).astype(BF16)
    lin = mm(attn_in, w_qkv)
    turned = rope_turn(
        lin[:, : q_width + kv_width].reshape(rows, -1, HEAD), cos, sin
    ).astype(BF16).reshape(rows, -1)
    query = turned[:, :q_width]
    kv = jnp.concatenate([turned[:, q_width:], lin[:, q_width + kv_width :].astype(BF16)], axis=1)
    return dict(scale=scale, normed=normed, attn_in=attn_in, query=query, kv=kv)


def grouped_heads(value, groups):
    rows = value.shape[0]
    return value.reshape(rows, groups, -1, HEAD)


def attend(query, kv_all, allowed, groups):
    keys = kv_all[:, : groups * HEAD].reshape(-1, groups, HEAD)
    values = kv_all[:, groups * HEAD :].reshape(-1, groups, HEAD)
    raw = ein("tgha,sga->ghts", grouped_heads(query, groups), keys) * HEAD ** (-0.5)
    scores = jnp.where(allowed[None, None], raw, MASKED)
    top = jnp.max(scores, axis=3, keepdims=True)
    expo = jnp.exp(scores - top)
    probs = expo / jnp.sum(expo, axis=3, keepdims=True)
    mixed = ein("ghts,sga->tgha", probs.astype(BF16), values)
    return mixed.reshape(query.shape), probs


def attend_back(grad_mixed, mixed, probs, query, kv_all, groups):
    rows = query.shape[0]
    keys = kv_all[:, : groups * HEAD].reshape(-1, groups, HEAD)
    values = kv_all[:, groups * HEAD :].reshape(-1, groups, HEAD)
    grad_grouped = grouped_heads(grad_mixed, groups)
    delta = jnp.sum(
        grad_grouped.astype(F32) * grouped_heads(mixed, groups), axis=3
    )
    delta = jnp.transpose(delta, (1, 2, 0))[..., None]
    grad_probs = ein("tgha,sga->ghts", grad_grouped, values)
    grad_scores = (probs * (grad_probs - delta)).astype(BF16)
    score_scale = HEAD ** (-0.5)
    grad_query = (ein("ghts,sga->tgha", grad_scores, keys) * score_scale).reshape(rows, -1, HEAD)
    grad_key = ein("ghts,tgha->sga", grad_scores, grouped_heads(query, groups)) * score_scale
    grad_value = ein("ghts,tgha->sga", probs.astype(BF16), grad_grouped)
    count = kv_all.shape[0]
    grad_kv = jnp.concatenate(
        [grad_key.reshape(count, -1), grad_value.reshape(count, -1)], axis=1
    ).astype(BF16)
    return grad_query, grad_kv


def route_tables(routes_all, first_expert, local, capacity):
    experts = first_expert + jnp.arange(local, dtype=jnp.int32)
    named = jnp.any(routes_all[:, None] == experts[None, :, None, None], axis=3)
    rank = jnp.cumsum(named.astype(jnp.int32), axis=2) - 1
    slot = jnp.where(named, rank, -1)
    return (slot[:, :, None, :] == jnp.arange(capacity, dtype=jnp.int32)[None, None, :, None])


def pick_gates(moe_in, router, routes_now):
    logits = mm(moe_in, router)
    experts = jnp.arange(router.shape[1], dtype=jnp.int32)
    choose = (routes_now[:, :, None] == experts[None, None, :]).astype(F32)
    mix = jax.nn.softmax(jnp.sum(choose * logits[:, None, :], axis=2), axis=1)
    return choose, mix


def moe_forward(moe_in, router, routes_all, pick, first_expert, experts_w):
    gate_w, up_w, down_w = experts_w
    folds, local, capacity, rows = pick.shape
    width = moe_in.shape[1]
    blocks = jnp.stack(rel_gather(moe_in))
    low = pick.astype(BF16)
    flat = blocks.reshape(folds * rows, width)
    top = routes_all.shape[2]
    choose, mix = pick_gates(flat, router, routes_all.reshape(folds * rows, top))
    dense = jnp.sum(choose * mix[:, :, None], axis=1)
    mine = lax.dynamic_slice_in_dim(dense, first_expert, local, 1).reshape(folds, rows, local)
    gate_rows = jnp.sum(
        pick.astype(F32) * jnp.transpose(mine, (0, 2, 1))[:, :, None, :], axis=3
    )
    gate_rows = jnp.transpose(gate_rows, (1, 0, 2)).reshape(local, folds * capacity, 1)
    picked = ein("flct,ftd->lfcd", low, blocks).astype(BF16).reshape(local, folds * capacity, width)
    gate_pre = ein("lnd,ldf->lnf", picked, gate_w)
    up_pre = ein("lnd,ldf->lnf", picked, up_w)
    inner = gated(gate_pre, up_pre).astype(BF16)
    produced = ein("lnf,lfd->lnd", inner, down_w).astype(BF16)
    weighted = (produced.astype(F32) * gate_rows).astype(BF16)
    partial = ein(
        "flct,lfcd->ftd", low, weighted.reshape(local, folds, capacity, width)
    ).astype(BF16)
    summed = rel_scatter([partial[k] for k in range(folds)])
    kept = dict(
        picked=picked, gate_pre=gate_pre, up_pre=up_pre, produced=produced, gate_rows=gate_rows, low=low
    )
    return summed, kept


def moe_backward(grad_low, kept, experts_w, first_expert, expert_count):
    gate_w, up_w, down_w = experts_w
    low = kept["low"]
    folds, local, capacity, rows = low.shape
    width = grad_low.shape[1]
    blocks = jnp.stack(rel_gather(grad_low))
    picked = ein("flct,ftd->lfcd", low, blocks).reshape(local, folds * capacity, width)
    dots = jnp.sum(picked * kept["produced"].astype(F32), axis=2)
    grad_expert = (kept["gate_rows"] * picked).astype(BF16)
    grad_inner = ein("lnd,lfd->lnf", grad_expert, down_w)
    _, back = jax.vjp(gated, kept["gate_pre"], kept["up_pre"])
    grad_gate, grad_up = back(grad_inner)
    grad_gate, grad_up = grad_gate.astype(BF16), grad_up.astype(BF16)
    grad_rows = (
        ein("lnf,ldf->lnd", grad_gate, gate_w) + ein("lnf,ldf->lnd", grad_up, up_w)
    ).astype(BF16)
    partial = ein(
        "flct,lfcd->ftd", low, grad_rows.reshape(local, folds, capacity, width)
    ).astype(BF16)
    dots = dots.reshape(local, folds, capacity)
    dot_cols = jnp.einsum("flct,lfc->ftl", low.astype(F32), dots, precision=HIGHEST)
    pad = jnp.zeros((folds, rows, HEAD // 2), F32)
    dot_cols = lax.dynamic_update_slice(pad, dot_cols, (0, 0, first_expert))
    high = dot_cols.astype(BF16)
    rest = (dot_cols - high.astype(F32)).astype(BF16)
    packed = jnp.concatenate([partial, high, rest], axis=2)
    summed = rel_scatter([packed[k] for k in range(folds)])
    grad_dots = summed[:, width : width + HEAD // 2] + summed[:, width + HEAD // 2 :]
    return summed[:, :width], grad_dots[:, :expert_count], grad_expert


def layer_forward(layer_in, weights, experts_w, common, routes, pick):
    gains, w_qkv, w_out, router = weights
    groups = common["groups"]
    hidden = layer_in.astype(F32)
    kept = attention_in(hidden, gains[0], w_qkv, common, groups * HEAD)
    kv_all = jnp.concatenate(rel_gather(kept["kv"]), axis=0)
    mixed, probs = attend(kept["query"], kv_all, common["allowed"], groups)
    mixed_low = mixed.astype(BF16)
    residual = hidden + mm(mixed_low, w_out)
    scale_two = lax.rsqrt(jnp.mean(residual * residual, axis=1, keepdims=True) + EPS)
    normed_two = residual * scale_two
    moe_in = (normed_two * gains[1].astype(F32)).astype(BF16)
    choose, mix = pick_gates(moe_in, router, routes[0])
    summed, moe_kept = moe_forward(moe_in, router, routes, pick, common["first"], experts_w)
    out = (residual + summed).astype(BF16)
    kept.update(
        kv_all=kv_all, mixed=mixed, probs=probs, mixed_low=mixed_low, scale_two=scale_two,
        normed_two=normed_two, moe_in=moe_in, choose=choose, mix=mix, moe=moe_kept,
    )
    return out, kept


def layer_backward(grad_low, kept, weights, experts_w, common):
    gains, w_qkv, w_out, router = weights
    groups = common["groups"]
    grad_out = grad_low.astype(F32)
    rows = grad_out.shape[0]
    grad_moe_in, dots, grad_expert = moe_backward(
        grad_low, kept["moe"], experts_w, common["first"], router.shape[1]
    )
    mix, choose = kept["mix"], kept["choose"]
    grad_mix = jnp.sum(choose * dots[:, None, :], axis=2)
    grad_chosen = mix * (grad_mix - jnp.sum(mix * grad_mix, axis=1, keepdims=True))
    grad_logits = jnp.sum(choose * grad_chosen[:, :, None], axis=1)
    moe_in = kept["moe_in"]
    grad_router = jnp.dot(moe_in.astype(F32).T, grad_logits, precision=HIGHEST)
    grad_moe_in = grad_moe_in + jnp.dot(grad_logits, router.astype(F32).T, precision=HIGHEST)
    normed_two = kept["normed_two"]
    grad_norm = grad_moe_in * gains[1].astype(F32)
    grad_gain_two = jnp.sum(grad_moe_in * normed_two, axis=0)
    grad_mid = grad_out + kept["scale_two"] * (
        grad_norm - normed_two * jnp.mean(grad_norm * normed_two, axis=1, keepdims=True)
    )
    grad_attn = grad_mid.astype(BF16)
    grad_w_out = mm_tn(kept["mixed_low"], grad_attn)
    grad_mixed = mm_nt(grad_attn, w_out).astype(BF16)
    grad_query, grad_kv = attend_back(
        grad_mixed, kept["mixed"], kept["probs"], kept["query"], kept["kv_all"], groups
    )
    own = rel_scatter([grad_kv[k * rows : (k + 1) * rows] for k in range(lax.axis_size(F_AX))])
    cos, sin = common["cos"], common["sin"]
    kv_width = groups * HEAD
    grad_lin = jnp.concatenate(
        [
            rope_back(grad_query, cos, sin).reshape(rows, -1),
            rope_back(own[:, :kv_width].reshape(rows, -1, HEAD), cos, sin).reshape(rows, -1),
            own[:, kv_width:],
        ],
        axis=1,
    ).astype(BF16)
    grad_w_qkv = mm_tn(kept["attn_in"], grad_lin)
    grad_attn_in = mm_nt(grad_lin, w_qkv)
    normed = kept["normed"]
    grad_norm = grad_attn_in * gains[0].astype(F32)
    grad_gain_one = jnp.sum(grad_attn_in * normed, axis=0)
    grad_in = grad_mid + kept["scale"] * (
        grad_norm - normed * jnp.mean(grad_norm * normed, axis=1, keepdims=True)
    )
    small = jnp.concatenate(
        [grad_router, grad_gain_one[:, None], grad_gain_two[:, None]], axis=1
    )
    small = jnp.pad(small, ((0, 0), (0, HEAD - small.shape[1])))
    attn_grads = jnp.concatenate([grad_w_qkv, grad_w_out, small], axis=1).astype(BF16)
    return grad_in.astype(BF16), attn_grads, grad_expert


def expert_grads(rows_in, grad_rows, gate_w, up_w, down_w):
    gate_pre = mm(rows_in, gate_w)
    up_pre = mm(rows_in, up_w)
    inner, back = jax.vjp(gated, gate_pre, up_pre)
    grad_gate, grad_up = back(mm_nt(grad_rows, down_w))
    grad_gate, grad_up = grad_gate.astype(BF16), grad_up.astype(BF16)
    return (
        mm_tn(rows_in, grad_gate).astype(BF16),
        mm_tn(rows_in, grad_up).astype(BF16),
        mm_tn(inner.astype(BF16), grad_rows).astype(BF16),
    )


def body(
    tokens, cotangent, seq_lengths, routes, gains, w_query, w_key, w_value, w_out, w_router, w_gate, w_up, w_down
):
    section = lax.axis_index(S_AX)
    is_first = section == 0
    fold_id = lax.axis_index(F_AX)
    replica = lax.axis_index(R_AX)
    core = replica % 2
    folds, replicas = lax.axis_size(F_AX), lax.axis_size(R_AX)
    rows = tokens.shape[2]
    top = routes.shape[4]
    local = w_gate.shape[1]
    expert_count = w_router.shape[2]
    kv_width = w_key.shape[2]
    q_width = w_query.shape[2]
    capacity = rows * top // expert_count

    def own_batch(value):
        return lax.dynamic_index_in_dim(value, section, 0, keepdims=False)

    small = jnp.concatenate([w_router[0], gains[0].T], axis=1)
    small = jnp.pad(small, ((0, 0), (0, HEAD - small.shape[1])))
    first_part = jnp.concatenate([w_query[0], w_key[0], w_value[0], small], axis=1)
    share = first_part.shape[0] // replicas

    def spread(value):
        piece = lax.dynamic_slice_in_dim(value, replica * share, share, 0)
        full = lax.all_gather(piece, (S_AX, F_AX, R_AX), axis=0, tiled=True)
        return full.reshape(2, -1, value.shape[1])

    full_first = spread(first_part)
    full_out = spread(w_out[0])
    split = q_width + 2 * kv_width
    weights = []
    for layer in range(2):
        tail = full_first[layer, :, split:]
        weights.append(
            (
                tail[:, expert_count : expert_count + 2].T,
                full_first[layer, :, :split],
                full_out[layer],
                tail[:, :expert_count],
            )
        )

    def spread_expert(value):
        flat = value.reshape(replicas, -1, value.shape[-1])
        piece = lax.dynamic_index_in_dim(flat, replica, 0, keepdims=False)
        full = lax.all_gather(piece, (S_AX, R_AX), axis=0, tiled=True)
        return full.reshape((2,) + value.shape[1:])

    both_experts = [spread_expert(part) for part in (w_gate, w_up, w_down)]
    experts_w = [tuple(part[layer] for part in both_experts) for layer in range(2)]

    every = lax.all_gather(routes[0, :, 0].reshape(2, rows * top), (S_AX, F_AX), axis=0)
    every = every.reshape(2, folds, 2, rows, top)
    mine = lax.dynamic_index_in_dim(every, section, 2, keepdims=False)
    order = (fold_id - jnp.arange(folds)) % folds
    mine = jnp.take(mine, order, axis=1)
    first = fold_id * local
    picks = [route_tables(mine[layer], first, local, capacity) for layer in range(2)]

    lengths = own_batch(seq_lengths[:, 0])
    position = fold_id * rows + jnp.arange(rows, dtype=jnp.int32)
    key_pos = (order[:, None] * rows + jnp.arange(rows)[None, :]).reshape(-1).astype(jnp.int32)
    segment, offset = layout(lengths, position)
    key_seg, _ = layout(lengths, key_pos)
    freq = ROPE_BASE ** (-2.0 * jnp.arange(HEAD // 2, dtype=F32) / HEAD)
    angles = offset[:, None] * freq
    angles = jnp.concatenate([angles, angles], axis=1)[:, None, :]
    common = dict(
        cos=jnp.cos(angles), sin=jnp.sin(angles), groups=kv_width // HEAD, first=first,
        allowed=(segment[:, None] == key_seg[None, :]) & (key_pos[None, :] <= position[:, None]),
    )

    value = own_batch(tokens[:, 0])
    outs, kept = [], []
    for layer in range(2):
        value, state = layer_forward(
            value, weights[layer], experts_w[layer], common, mine[layer], picks[layer]
        )
        outs.append(value)
        kept.append(state)
    grad = own_batch(cotangent[:, 0])
    grads, attn_grads, expert_rows = [None, None], [None, None], [None, None]
    for layer in (1, 0):
        grad, attn_grads[layer], expert_rows[layer] = layer_backward(
            grad, kept[layer], weights[layer], experts_w[layer], common
        )
        grads[layer] = grad

    def own_layer(pair):
        return jnp.where(is_first, pair[0], pair[1])

    def other_layer(pair):
        return jnp.where(is_first, pair[1], pair[0])

    def by_section(keep, got):
        return jnp.stack([jnp.where(is_first, keep, got), jnp.where(is_first, got, keep)])

    def both_batches(pair):
        return by_section(own_layer(pair), swap_section(other_layer(pair)))

    half = local // 2

    def exchange(pair):
        chip = []
        for value in pair:
            keep = lax.dynamic_slice_in_dim(value, core * half, half, 0)
            give = lax.dynamic_slice_in_dim(value, (1 - core) * half, half, 0)
            got = swap_core(give)
            chip.append(
                jnp.concatenate(
                    [jnp.where(core == 0, keep, got), jnp.where(core == 0, got, keep)], axis=1
                )
            )
        batches = both_batches(chip)
        whole = all_chips(batches)
        return jnp.moveaxis(whole, 2, 0).reshape(half, -1, whole.shape[-1])

    x_rows = exchange([state["moe"]["picked"] for state in kept])
    g_rows = exchange(expert_rows)
    mine_w = [lax.dynamic_slice_in_dim(part[0], core * half, half, 0) for part in (w_gate, w_up, w_down)]
    made = [
        expert_grads(x_rows[i], g_rows[i], mine_w[0][i], mine_w[1][i], mine_w[2][i]) for i in range(half)
    ]
    expert_out = []
    for slot in range(3):
        keep = jnp.stack([one[slot] for one in made])
        got = swap_core(keep)
        both = jnp.concatenate(
            [jnp.where(core == 0, keep, got), jnp.where(core == 0, got, keep)], axis=0
        )
        expert_out.append(both.astype(F32)[None])

    shards = []
    for layer in range(2):
        piece = lax.psum_scatter(
            attn_grads[layer], (F_AX, S_AX, R_AX), scatter_dimension=0, tiled=True
        )
        shards.append(lax.all_gather(piece, (S_AX, R_AX), axis=0, tiled=True))
    shard = own_layer(shards).astype(F32)
    out_at = split + q_width
    small = shard[:, shard.shape[1] - HEAD :]
    layer_outputs = both_batches(outs)
    input_grads = both_batches(grads)
    return (
        layer_outputs[None, :, None],
        input_grads[None, :, None],
        small[:, expert_count : expert_count + 2].T[None],
        shard[None, :, :q_width],
        shard[None, :, q_width : q_width + kv_width],
        shard[None, :, q_width + kv_width : split],
        shard[None, :, split : shard.shape[1] - HEAD],
        small[None, :, :expert_count],
        expert_out[0],
        expert_out[1],
        expert_out[2],
    )


def solution(mesh):
    acts = P(None, R_AX, F_AX, None)
    rows = P(S_AX, F_AX, None)
    expert = P(S_AX, F_AX, None, None)
    stacked = P(S_AX, None, R_AX, F_AX, None)
    gain = P(S_AX, None, F_AX)
    return jax.shard_map(
        body,
        mesh=mesh,
        in_specs=(acts, acts, P(None, R_AX, None), stacked, gain)
        + (rows,) * 5
        + (expert,) * 3,
        out_specs=(stacked, stacked, gain) + (rows,) * 5 + (expert,) * 3,
        check_vma=False,
    )
```

```python
import functools

import jax
import jax.numpy as jnp
from jax import lax
from jax.experimental import pallas as pl
from jax.experimental.pallas import tpu as pltpu
from jax.sharding import PartitionSpec as P

HEAD = 128
ROPE_BASE = 1000000.0
EPS = 1e-06
MASKED = -1e30
F32 = jnp.float32
BF16 = jnp.bfloat16
S_AX, F_AX, R_AX = "section", "fsdp", "replica"
HIGHEST = lax.Precision.HIGHEST
LANES = 128
GELU_C = 0.7978845608028654
GELU_A = 0.044715


def dot(a, b):
    return lax.dot_general(a, b, (((1,), (0,)), ((), ())), preferred_element_type=F32)


def dot_nt(a, b):
    return lax.dot_general(a, b, (((1,), (1,)), ((), ())), preferred_element_type=F32)


def dot_tn(a, b):
    return lax.dot_general(a, b, (((0,), (0,)), ((), ())), preferred_element_type=F32)


def gelu_parts(x):
    t = jnp.tanh(GELU_C * (x + GELU_A * x * x * x))
    value = 0.5 * x * (1.0 + t)
    slope = 0.5 * (1.0 + t) + 0.5 * x * (1.0 - t * t) * GELU_C * (1.0 + 3.0 * GELU_A * x * x)
    return value, slope


def lane_is(shape, number):
    return lax.broadcasted_iota(jnp.int32, shape, 1) == number


def masked_mix(logits, mask):
    kept = jnp.where(mask > 0.0, logits, -1e30)
    expo = jnp.exp(kept - jnp.max(kept, axis=1, keepdims=True)) * mask
    return expo / jnp.sum(expo, axis=1, keepdims=True)


def one_hot(slots_ref, block, step, capacity):
    rows = slots_ref.shape[2]
    place = lax.broadcasted_iota(jnp.int32, (capacity, rows), 0)
    return place == slots_ref[block, step : step + 1, :]


def weight_copies(scalars, own, pieces, buffers, sems):
    own_g, own_u, own_d = own
    parts = len(pieces[0][0])
    ff = own_g.shape[2] // parts
    is_own, flip = scalars[0], scalars[1]
    waits = {}
    for step in range(len(pieces[0])):
        for part in range(parts):
            expert = step ^ flip
            cols = pl.ds(part * ff, ff)
            sources = (own_g.at[expert, :, cols], own_u.at[expert, :, cols], own_d.at[expert, cols, :])
            for kind in range(3):
                target = buffers[kind].at[step, part]
                sem = sems.at[kind, step, part]

                @pl.when(is_own == 1)
                def _(source=sources[kind], target=target, sem=sem):
                    pltpu.make_async_copy(source, target, sem).start()

                @pl.when(is_own == 0)
                def _(source=pieces[kind][step][part], target=target, sem=sem):
                    pltpu.make_async_copy(source, target, sem).start()

                waits[kind, step, part] = pltpu.make_async_copy(
                    pieces[kind][step][part], target, sem
                )
    return waits


def split_refs(refs, counts):
    out, at = [], 0
    for count in counts:
        out.append(refs[at : at + count])
        at += count
    return out


def moe_fwd_kernel(folds, local, parts, capacity, *refs):
    (scalars, slots, mask, router), blocks, own, flat, outs, partials, scratch = split_refs(
        refs, (4, folds, 3, 3 * local * parts, 5, folds, 4)
    )
    scalars_ref = scalars
    picked_ref, gate_ref, up_ref, made_ref, grows_ref = outs
    buf_g, buf_u, buf_d, sems = scratch
    pieces = [
        [[flat[(kind * local + step) * parts + part] for part in range(parts)] for step in range(local)]
        for kind in range(3)
    ]
    waits = weight_copies(scalars_ref, own, pieces, (buf_g, buf_u, buf_d), sems)
    rows = blocks[0].shape[0]
    width = blocks[0].shape[1]
    ff = buf_g.shape[3]
    for k in range(folds):
        mix = masked_mix(dot(blocks[k][...], router[...]), mask[k])
        for step in range(local):
            pick = one_hot(slots, k, step, capacity)
            at = pl.ds(k * capacity, capacity)
            picked_ref[step, at, :] = dot(
                jnp.where(pick, 1.0, 0.0).astype(BF16), blocks[k][...]
            ).astype(BF16)
            grows_ref[step, at, :] = lax.dot_general(
                jnp.where(pick, 1.0, 0.0), mix, (((1,), (0,)), ((), ())),
                precision=HIGHEST, preferred_element_type=F32,
            )
    for step in range(local):
        for part in range(parts):
            for kind in range(3):
                waits[kind, step, part].wait()
            cols = pl.ds(part * ff, ff)
            x = picked_ref[step]
            gate = dot(x, buf_g[step, part])
            up = dot(x, buf_u[step, part])
            gate_ref[step, :, cols] = gate
            up_ref[step, :, cols] = up
            inner = (gelu_parts(gate)[0] * up).astype(BF16)
            term = dot(inner, buf_d[step, part])
            made = term if part == 0 else made + term
        made_ref[step] = made.astype(BF16)
    for k in range(folds):
        at = pl.ds(k * capacity, capacity)
        picks, weighted = [], []
        for step in range(local):
            gates = grows_ref[step, at, :]
            own_lane = lane_is(gates.shape, scalars_ref[2 + step])
            factor = jnp.sum(jnp.where(own_lane, gates, 0.0), axis=1, keepdims=True)
            picks.append(jnp.where(one_hot(slots, k, step, capacity), 1.0, 0.0).astype(BF16))
            weighted.append((made_ref[step, at, :].astype(F32) * factor).astype(BF16))
        partials[k][...] = dot_tn(
            jnp.concatenate(picks, axis=0), jnp.concatenate(weighted, axis=0)
        ).astype(BF16)


def moe_bwd_kernel(folds, local, parts, capacity, *refs):
    (scalars, slots, gate_ref, up_ref, made_ref, grows_ref), blocks, own, flat, (ge_ref,), partials, scratch = split_refs(
        refs, (6, folds, 3, 3 * local * parts, 1, folds, 6)
    )
    buf_g, buf_u, buf_d, sems, dx_ref, dots_ref = scratch
    pieces = [
        [[flat[(kind * local + step) * parts + part] for part in range(parts)] for step in range(local)]
        for kind in range(3)
    ]
    waits = weight_copies(scalars, own, pieces, (buf_g, buf_u, buf_d), sems)
    ff = buf_g.shape[3]
    for step in range(local):
        for k in range(folds):
            at = pl.ds(k * capacity, capacity)
            pick = jnp.where(one_hot(slots, k, step, capacity), 1.0, 0.0).astype(BF16)
            dout = dot(pick, blocks[k][...])
            gates = grows_ref[step, at, :]
            own_lane = lane_is(gates.shape, scalars[2 + step])
            factor = jnp.sum(jnp.where(own_lane, gates, 0.0), axis=1, keepdims=True)
            value = jnp.sum(dout * made_ref[step, at, :].astype(F32), axis=1, keepdims=True)
            lane = lax.broadcasted_iota(jnp.int32, gates.shape, 1)
            number = scalars[2 + step]
            dots_ref[step, at, :] = jnp.where(
                (lane == number) | (lane == number + LANES // 2), value, 0.0
            )
            ge_ref[step, at, :] = (dout * factor).astype(BF16)
    for step in range(local):
        ge = ge_ref[step]
        for part in range(parts):
            for kind in range(3):
                waits[kind, step, part].wait()
            cols = pl.ds(part * ff, ff)
            grad_inner = dot_nt(ge, buf_d[step, part])
            gate = gate_ref[step, :, cols]
            up = up_ref[step, :, cols]
            value, slope = gelu_parts(gate)
            grad_gate = (grad_inner * up * slope).astype(BF16)
            grad_up = (grad_inner * value).astype(BF16)
            term = dot_nt(grad_gate, buf_g[step, part]) + dot_nt(grad_up, buf_u[step, part])
            total = term if part == 0 else total + term
        dx_ref[step] = total.astype(BF16)
    for k in range(folds):
        at = pl.ds(k * capacity, capacity)
        hot = [one_hot(slots, k, step, capacity) for step in range(local)]
        picks = jnp.concatenate([jnp.where(one, 1.0, 0.0) for one in hot], axis=0)
        width = ge_ref.shape[2]
        partials[k][:, :width] = dot_tn(
            picks.astype(BF16), jnp.concatenate([dx_ref[step, at, :] for step in range(local)], axis=0)
        ).astype(BF16)
        dots = lax.dot_general(
            picks, jnp.concatenate([dots_ref[step, at, :] for step in range(local)], axis=0),
            (((0,), (0,)), ((), ())), precision=HIGHEST, preferred_element_type=F32,
        )
        high = dots.astype(BF16).astype(F32)
        lane = lax.broadcasted_iota(jnp.int32, dots.shape, 1)
        partials[k][:, width:] = jnp.where(lane < LANES // 2, high, dots - high).astype(BF16)


def vmem(count):
    return [pl.BlockSpec(memory_space=pltpu.VMEM)] * count


def anywhere(count):
    return [pl.BlockSpec(memory_space=pl.ANY)] * count


def weight_scratch(own, local, parts):
    width, ff = own[0].shape[1], own[0].shape[2] // parts
    return [
        pltpu.VMEM((local, parts, width, ff), BF16),
        pltpu.VMEM((local, parts, width, ff), BF16),
        pltpu.VMEM((local, parts, ff, width), BF16),
        pltpu.SemaphoreType.DMA((3, local, parts)),
    ]


def cost(rows, width, ff, products):
    return pl.CostEstimate(
        flops=2 * rows * width * ff * products, bytes_accessed=2 * 3 * width * ff * 2 + 8 * rows * width,
        transcendentals=rows * ff,
    )


def moe_fwd_call(scalars, slots, mask, router, blocks, own, flat, folds, local, rows, parts, width, ff, capacity):
    picked_rows = folds * capacity
    shapes = [
        jax.ShapeDtypeStruct((local, picked_rows, width), BF16),
        jax.ShapeDtypeStruct((local, picked_rows, ff), F32),
        jax.ShapeDtypeStruct((local, picked_rows, ff), F32),
        jax.ShapeDtypeStruct((local, picked_rows, width), BF16),
        jax.ShapeDtypeStruct((local, picked_rows, LANES), F32),
    ] + [jax.ShapeDtypeStruct((rows, width), BF16)] * folds
    out = pl.pallas_call(
        functools.partial(moe_fwd_kernel, folds, local, parts, capacity),
        out_shape=shapes,
        in_specs=[pl.BlockSpec(memory_space=pltpu.SMEM)]
        + vmem(3 + folds) + anywhere(3 + len(flat)),
        out_specs=vmem(len(shapes)),
        scratch_shapes=weight_scratch(own, local, parts),
        cost_estimate=cost(local * picked_rows, width, ff, 3),
        compiler_params=pltpu.CompilerParams(vmem_limit_bytes=56 << 20),
    )(scalars, slots, mask, router, *blocks, *own, *flat)
    return out[:5], out[5:]


def moe_bwd_call(scalars, slots, kept, blocks, own, flat, folds, local, rows, parts, width, ff, capacity):
    _, gate_pre, up_pre, made, gate_rows = kept
    picked_rows = folds * capacity
    shapes = [jax.ShapeDtypeStruct((local, picked_rows, width), BF16)] + [
        jax.ShapeDtypeStruct((rows, width + LANES), BF16)
    ] * folds
    out = pl.pallas_call(
        functools.partial(moe_bwd_kernel, folds, local, parts, capacity),
        out_shape=shapes,
        in_specs=[pl.BlockSpec(memory_space=pltpu.SMEM)]
        + vmem(5 + folds) + anywhere(3 + len(flat)),
        out_specs=vmem(len(shapes)),
        scratch_shapes=weight_scratch(own, local, parts)
        + [pltpu.VMEM((local, picked_rows, width), BF16), pltpu.VMEM((local, picked_rows, LANES), F32)],
        cost_estimate=cost(local * picked_rows, width, ff, 3),
        compiler_params=pltpu.CompilerParams(vmem_limit_bytes=56 << 20),
    )(scalars, slots, gate_pre, up_pre, made, gate_rows, *blocks, *own, *flat)
    return out[0], out[1:]


def mm(a, b):
    return jnp.dot(a, b, preferred_element_type=F32)


def mm_nt(a, b):
    return lax.dot_general(a, b, (((1,), (1,)), ((), ())), preferred_element_type=F32)


def mm_tn(a, b):
    return lax.dot_general(a, b, (((0,), (0,)), ((), ())), preferred_element_type=F32)


def ein(spec, a, b):
    return jnp.einsum(spec, a, b, preferred_element_type=F32)


def rel_gather(value):
    folds = lax.axis_size(F_AX)
    parts = [value]
    for k in range(1, folds):
        parts.append(lax.ppermute(value, F_AX, [(i, (i + k) % folds) for i in range(folds)]))
    return parts


def rel_scatter(parts):
    folds = lax.axis_size(F_AX)
    total = parts[0].astype(F32)
    for k in range(1, folds):
        got = lax.ppermute(parts[k], F_AX, [(i, (i - k) % folds) for i in range(folds)])
        total = total + got.astype(F32)
    return total


def swap_section(value):
    return lax.ppermute(value, S_AX, [(0, 1), (1, 0)])


def swap_core(value):
    count = lax.axis_size(R_AX)
    return lax.ppermute(value, R_AX, [(i, i ^ 1) for i in range(count)])


def rope_turn(values, cos, sin):
    half = HEAD // 2
    turned = jnp.concatenate([-values[..., half:], values[..., :half]], axis=-1)
    return values * cos + turned * sin


def rope_back(grads, cos, sin):
    half = HEAD // 2
    scaled = grads * sin
    turned = jnp.concatenate([scaled[..., half:], -scaled[..., :half]], axis=-1)
    return grads * cos + turned


def layout(lengths, position):
    bounds = jnp.cumsum(lengths)
    passed = (position[:, None] >= bounds[None, :]).astype(jnp.int32)
    segment = jnp.sum(passed, axis=1)
    start = jnp.sum(passed * lengths[None, :], axis=1)
    return segment, (position - start).astype(F32)


def gated(gate, up):
    return jax.nn.gelu(gate) * up


def attention_in(hidden, gain, w_qkv, common, kv_width):
    cos, sin = common["cos"], common["sin"]
    rows, width = hidden.shape
    q_width = w_qkv.shape[1] - 2 * kv_width
    scale = lax.rsqrt(jnp.mean(hidden * hidden, axis=1, keepdims=True) + EPS)
    normed = hidden * scale
    attn_in = (normed * gain.astype(F32)).astype(BF16)
    lin = mm(attn_in, w_qkv)
    turned = rope_turn(
        lin[:, : q_width + kv_width].reshape(rows, -1, HEAD), cos, sin
    ).astype(BF16).reshape(rows, -1)
    query = turned[:, :q_width]
    kv = jnp.concatenate([turned[:, q_width:], lin[:, q_width + kv_width :].astype(BF16)], axis=1)
    return dict(scale=scale, normed=normed, attn_in=attn_in, query=query, kv=kv)


def grouped_heads(value, groups):
    rows = value.shape[0]
    return value.reshape(rows, groups, -1, HEAD)


def attend(query, kv_all, allowed, groups):
    keys = kv_all[:, : groups * HEAD].reshape(-1, groups, HEAD)
    values = kv_all[:, groups * HEAD :].reshape(-1, groups, HEAD)
    raw = ein("tgha,sga->ghts", grouped_heads(query, groups), keys) * HEAD ** (-0.5)
    scores = jnp.where(allowed[None, None], raw, MASKED)
    top = jnp.max(scores, axis=3, keepdims=True)
    expo = jnp.exp(scores - top)
    probs = expo / jnp.sum(expo, axis=3, keepdims=True)
    mixed = ein("ghts,sga->tgha", probs.astype(BF16), values)
    return mixed.reshape(query.shape), probs


def attend_back(grad_mixed, mixed, probs, query, kv_all, groups):
    rows = query.shape[0]
    keys = kv_all[:, : groups * HEAD].reshape(-1, groups, HEAD)
    values = kv_all[:, groups * HEAD :].reshape(-1, groups, HEAD)
    grad_grouped = grouped_heads(grad_mixed, groups)
    delta = jnp.sum(
        grad_grouped.astype(F32) * grouped_heads(mixed, groups), axis=3
    )
    delta = jnp.transpose(delta, (1, 2, 0))[..., None]
    grad_probs = ein("tgha,sga->ghts", grad_grouped, values)
    grad_scores = (probs * (grad_probs - delta)).astype(BF16)
    score_scale = HEAD ** (-0.5)
    grad_query = (ein("ghts,sga->tgha", grad_scores, keys) * score_scale).reshape(rows, -1, HEAD)
    grad_key = ein("ghts,tgha->sga", grad_scores, grouped_heads(query, groups)) * score_scale
    grad_value = ein("ghts,tgha->sga", probs.astype(BF16), grad_grouped)
    count = kv_all.shape[0]
    grad_kv = jnp.concatenate(
        [grad_key.reshape(count, -1), grad_value.reshape(count, -1)], axis=1
    ).astype(BF16)
    return grad_query, grad_kv


def moe_forward(moe_in, router, mask, slots, scalars, experts_w, size):
    outs, partials = moe_fwd_call(
        scalars, slots, mask, router, rel_gather(moe_in), *experts_w, **size
    )
    return rel_scatter(partials), outs


def moe_backward(grad_low, kept, slots, scalars, experts_w, size, tie, send_rows):
    blocks, tied = lax.optimization_barrier((rel_gather(grad_low), tie))
    grad_expert, partials = moe_bwd_call(scalars, slots, kept, blocks, *experts_w, **size)
    sent = send_rows(grad_expert)
    summed = rel_scatter(partials)
    width = grad_low.shape[1]
    tail = summed[:, width:]
    half = LANES // 2
    dots = tail[:, :half] + tail[:, half:]
    return summed[:, :width], jnp.pad(dots, ((0, 0), (0, half))), sent, tied


def layer_forward(layer_in, weights, experts_w, common, mask, slots, scalars):
    gains, w_qkv, w_out, router = weights
    groups = common["groups"]
    hidden = layer_in.astype(F32)
    kept = attention_in(hidden, gains[0], w_qkv, common, groups * HEAD)
    kv_all = jnp.concatenate(rel_gather(kept["kv"]), axis=0)
    mixed, probs = attend(kept["query"], kv_all, common["allowed"], groups)
    mixed_low = mixed.astype(BF16)
    residual = hidden + mm(mixed_low, w_out)
    scale_two = lax.rsqrt(jnp.mean(residual * residual, axis=1, keepdims=True) + EPS)
    normed_two = residual * scale_two
    moe_in = (normed_two * gains[1].astype(F32)).astype(BF16)
    mix = masked_mix(mm(moe_in, router), mask[0])
    summed, moe_kept = moe_forward(moe_in, router, mask, slots, scalars, experts_w, common["size"])
    out = (residual + summed).astype(BF16)
    kept.update(
        kv_all=kv_all, mixed=mixed, probs=probs, mixed_low=mixed_low, scale_two=scale_two,
        normed_two=normed_two, moe_in=moe_in, mix=mix, moe=moe_kept,
    )
    return out, kept


def layer_backward(grad_low, kept, weights, experts_w, common, slots, scalars, tie, late_tie, send_rows):
    gains, w_qkv, w_out, router = weights
    groups = common["groups"]
    grad_out = grad_low.astype(F32)
    rows = grad_out.shape[0]
    grad_moe_in, dots, sent, tied = moe_backward(
        grad_low, kept["moe"], slots, scalars, experts_w, common["size"], tie, send_rows
    )
    mix = kept["mix"]
    grad_logits = mix * (dots - jnp.sum(mix * dots, axis=1, keepdims=True))
    moe_in = kept["moe_in"]
    count = common["experts"]
    grad_router = lax.dot_general(
        grad_logits[:, :count], moe_in.astype(F32), (((0,), (0,)), ((), ())), precision=HIGHEST
    )
    grad_moe_in = grad_moe_in + jnp.dot(grad_logits, router.astype(F32).T, precision=HIGHEST)
    normed_two = kept["normed_two"]
    grad_norm = grad_moe_in * gains[1].astype(F32)
    grad_gain_two = jnp.sum(grad_moe_in * normed_two, axis=0)
    grad_mid = grad_out + kept["scale_two"] * (
        grad_norm - normed_two * jnp.mean(grad_norm * normed_two, axis=1, keepdims=True)
    )
    grad_attn = grad_mid.astype(BF16)
    grad_mixed = mm_nt(grad_attn, w_out).astype(BF16)
    grad_query, grad_kv = attend_back(
        grad_mixed, kept["mixed"], kept["probs"], kept["query"], kept["kv_all"], groups
    )
    grad_kv, late_tied, sent = lax.optimization_barrier((grad_kv, late_tie, sent))
    own = rel_scatter([grad_kv[k * rows : (k + 1) * rows] for k in range(lax.axis_size(F_AX))])
    cos, sin = common["cos"], common["sin"]
    kv_width = groups * HEAD
    grad_lin = jnp.concatenate(
        [
            rope_back(grad_query, cos, sin).reshape(rows, -1),
            rope_back(own[:, :kv_width].reshape(rows, -1, HEAD), cos, sin).reshape(rows, -1),
            own[:, kv_width:],
        ],
        axis=1,
    ).astype(BF16)
    grad_attn_in = mm_nt(grad_lin, w_qkv)
    normed = kept["normed"]
    grad_norm = grad_attn_in * gains[0].astype(F32)
    grad_in = grad_mid + kept["scale"] * (
        grad_norm - normed * jnp.mean(grad_norm * normed, axis=1, keepdims=True)
    )
    small = jnp.concatenate([grad_router, grad_gain_two[None]], axis=0)
    return grad_in.astype(BF16), grad_attn, grad_lin, small.astype(BF16), sent, tied, late_tied


def expert_grads(rows_in, grad_rows, gate_w, up_w, down_w):
    gate_pre = mm(rows_in, gate_w)
    up_pre = mm(rows_in, up_w)
    inner, back = jax.vjp(gated, gate_pre, up_pre)
    grad_gate, grad_up = back(mm_nt(grad_rows, down_w))
    grad_gate, grad_up = grad_gate.astype(BF16), grad_up.astype(BF16)
    return (
        mm_tn(rows_in, grad_gate).astype(BF16),
        mm_tn(rows_in, grad_up).astype(BF16),
        mm_tn(inner.astype(BF16), grad_rows).astype(BF16),
    )


def body(
    tokens, cotangent, seq_lengths, routes, gains, w_query, w_key, w_value, w_out, w_router, w_gate, w_up, w_down
):
    section = lax.axis_index(S_AX)
    is_first = section == 0
    fold_id = lax.axis_index(F_AX)
    replica = lax.axis_index(R_AX)
    core = replica % 2
    folds, replicas = lax.axis_size(F_AX), lax.axis_size(R_AX)
    rows = tokens.shape[2]
    top = routes.shape[4]
    local = w_gate.shape[1]
    expert_count = w_router.shape[2]
    kv_width = w_key.shape[2]
    q_width = w_query.shape[2]
    capacity = rows * top // expert_count

    def own_batch(value):
        return lax.dynamic_index_in_dim(value, section, 0, keepdims=False)

    def swap_xor(value, bit):
        return lax.ppermute(value, R_AX, [(i, i ^ bit) for i in range(replicas)])

    flat_routes = routes[0, :, 0].reshape(2, rows * top)
    give = lax.dynamic_index_in_dim(flat_routes, 1 - section, 0, keepdims=False)
    keep = own_batch(flat_routes)
    got = swap_section(give)
    pair = jnp.stack([jnp.where(is_first, keep, got), jnp.where(is_first, got, keep)])
    mine = jnp.stack(rel_gather(pair), axis=1).reshape(2, folds, rows, top)
    first = fold_id * local
    flip = (replica // 2) % 2
    lanes = jnp.arange(LANES, dtype=jnp.int32)
    masks = jnp.any(mine[..., None] == lanes, axis=3)
    numbers = first + (jnp.arange(local, dtype=jnp.int32) ^ flip)
    named = jnp.any(mine[:, :, None] == numbers[None, None, :, None, None], axis=4)
    before = (jnp.arange(rows)[:, None] < jnp.arange(rows)[None, :]).astype(BF16)
    rank = ein("lfet,tu->lfeu", named.astype(BF16), before).astype(jnp.int32)
    slots_all = jnp.where(named, rank, -1)
    masks = masks.astype(F32)
    scalars = [
        jnp.concatenate([jnp.stack([(section == layer).astype(jnp.int32), flip]), numbers]).astype(jnp.int32)
        for layer in range(2)
    ]

    small = jnp.concatenate([w_router[0], gains[0].T], axis=1)
    small = jnp.pad(small, ((0, 0), (0, HEAD - small.shape[1])))
    shard = jnp.concatenate([w_query[0], w_key[0], w_value[0], small, w_out[0]], axis=1)
    share = shard.shape[0] // (2 * replicas)
    keep = lax.dynamic_slice_in_dim(shard, (section * replicas + replica) * share, share, 0)
    give = lax.dynamic_slice_in_dim(shard, ((1 - section) * replicas + replica) * share, share, 0)
    got = swap_section(give)
    split = q_width + 2 * kv_width
    weights = []
    for layer in range(2):
        piece = jnp.where(section == layer, keep, got)
        axes = (F_AX, S_AX, R_AX)
        head = lax.all_gather(piece[:, : split + LANES], axes, axis=0, tiled=True)
        out_w = lax.all_gather(piece[:, split + LANES :], axes, axis=0, tiled=True)
        tail = head[:, split:]
        weights.append((tail[:, expert_count : expert_count + 2].T, head[:, :split], out_w, tail))

    part_ff = w_gate.shape[3] // 2
    at = core * part_ff
    flat = []
    for part, axis in ((w_gate, 1), (w_up, 1), (w_down, 0)):
        chosen = lax.dynamic_index_in_dim(part[0], flip, 0, keepdims=False)
        piece = lax.dynamic_slice_in_dim(chosen, at, part_ff, axis)
        same = swap_section(piece)
        cross = swap_xor(same, 2)
        flat += [same, swap_core(same), cross, swap_core(cross)]
    experts_w = ((w_gate[0], w_up[0], w_down[0]), flat)
    size = dict(
        folds=folds, local=local, rows=rows, parts=2, width=tokens.shape[3], ff=w_gate.shape[3],
        capacity=capacity,
    )

    lengths = own_batch(seq_lengths[:, 0])
    position = fold_id * rows + jnp.arange(rows, dtype=jnp.int32)
    order = (fold_id - jnp.arange(folds)) % folds
    key_pos = (order[:, None] * rows + jnp.arange(rows)[None, :]).reshape(-1).astype(jnp.int32)
    segment, offset = layout(lengths, position)
    key_seg, _ = layout(lengths, key_pos)
    freq = ROPE_BASE ** (-2.0 * jnp.arange(HEAD // 2, dtype=F32) / HEAD)
    angles = offset[:, None] * freq
    angles = jnp.concatenate([angles, angles], axis=1)[:, None, :]
    common = dict(
        cos=jnp.cos(angles), sin=jnp.sin(angles), groups=kv_width // HEAD, size=size,
        experts=expert_count,
        allowed=(segment[:, None] == key_seg[None, :]) & (key_pos[None, :] <= position[:, None]),
    )

    value = own_batch(tokens[:, 0])
    outs, kept = [], []
    for layer in range(2):
        value, state = layer_forward(
            value, weights[layer], experts_w, common, masks[layer], slots_all[layer], scalars[layer]
        )
        outs.append(value)
        kept.append(state)

    def own_layer(pair):
        return jnp.where(is_first, pair[0], pair[1])

    def other_layer(pair):
        return jnp.where(is_first, pair[1], pair[0])

    def by_section(keep, got):
        return jnp.stack([jnp.where(is_first, keep, got), jnp.where(is_first, got, keep)])

    def both_batches(pair):
        return by_section(own_layer(pair), swap_section(other_layer(pair)))

    half = local // 2

    def chip_rows(pair):
        chip = []
        for value in pair:
            keep = lax.dynamic_slice_in_dim(value, (core ^ flip) * half, half, 0)
            give = lax.dynamic_slice_in_dim(value, (1 - (core ^ flip)) * half, half, 0)
            got = swap_core(give)
            chip.append(
                jnp.concatenate(
                    [jnp.where(core == 0, keep, got), jnp.where(core == 0, got, keep)], axis=1
                )
            )
        return chip

    chips = replicas // 2

    def all_x(value):
        return [swap_xor(value, bit) for bit in range(2, replicas, 2)]

    def by_order(value, others):
        whole = jnp.zeros((chips,) + value.shape, value.dtype)
        for at, part in enumerate([value] + others):
            whole = lax.dynamic_update_index_in_dim(whole, part, (replica // 2) ^ at, 0)
        return whole

    same_core = [[2 * i + c for i in range(chips)] for c in range(2)]

    def flat_rows(whole):
        return jnp.moveaxis(whole, 2, 0).reshape(half, -1, whole.shape[-1])

    x_rows = both_batches(chip_rows([state["moe"][0] for state in kept]))
    def both_rows(pair):
        return jnp.concatenate([own_layer(pair), swap_section(other_layer(pair))], axis=0)

    def own_columns(value):
        width = value.shape[1] // replicas
        whole = jnp.zeros((replicas, value.shape[0], width), value.dtype)
        for bit in range(replicas):
            piece = lax.dynamic_slice_in_dim(value, (replica ^ bit) * width, width, 1)
            got = piece if bit == 0 else swap_xor(piece, bit)
            whole = lax.dynamic_update_index_in_dim(whole, got, replica ^ bit, 0)
        return whole

    def weight_gradient(left, right, extra):
        total = mm_tn(left, right).astype(BF16)
        step = total.shape[0] // folds
        blocks = []
        for k in range(folds):
            goal = (fold_id - k) % folds
            block = lax.dynamic_slice_in_dim(total, goal * step, step, 0)
            if extra is not None:
                more = lax.dynamic_index_in_dim(extra, goal, 0, keepdims=False)
                block = jnp.concatenate([block, more], axis=0)
            blocks.append(block)
        mine = rel_scatter(blocks).astype(BF16)
        height, width = mine.shape
        whole = jnp.zeros((replicas, height, width), BF16)
        for bit in range(0, replicas, 2):
            same = mine if bit == 0 else swap_xor(mine, bit)
            for other, part in enumerate((same, swap_core(same))):
                whole = lax.dynamic_update_index_in_dim(whole, part, replica ^ (bit + other), 0)
        return whole

    left_rows = both_rows(
        [jnp.concatenate([state["attn_in"], state["mixed_low"]], axis=1) for state in kept]
    )
    grad = own_batch(cotangent[:, 0])
    grads, grad_attn, grad_lin = [None, None], [None, None], [None, None]
    smalls, expert_rows = [None, None], [None, None]
    tie = ()
    held = []

    def send_first(value):
        held.append(chip_rows([value])[0])
        return ()

    def send_both(value):
        chip = (chip_rows([value])[0], held[0])
        mine = own_layer(chip)
        return by_order(mine, all_x(mine)), swap_section(other_layer(chip))

    for layer in (1, 0):
        late_tie = (x_rows, left_rows) if layer == 1 else ()
        (grad, grad_attn[layer], grad_lin[layer], smalls[layer], expert_rows[layer], tied, late_tied) = layer_backward(
            grad, kept[layer], weights[layer], experts_w, common, slots_all[layer], scalars[layer], tie, late_tie,
            send_first if layer == 1 else send_both,
        )
        if layer == 1:
            x_rows, left_rows = late_tied
            x_rows = lax.all_gather(x_rows, R_AX, axis=0, axis_index_groups=same_core)
            left_rows = lax.all_gather(left_rows, R_AX, axis=0, tiled=True)
            tie = (x_rows, left_rows)
        else:
            x_rows, left_rows = tied
        grads[layer] = grad
    x_rows = flat_rows(x_rows)
    model = tokens.shape[3]
    piece = model // (folds * replicas)
    count = smalls[0].shape[0]
    tall = -(-count // 16) * 16
    with_small = []
    for layer in range(2):
        value = smalls[layer].reshape(count, folds, replicas, piece)
        value = jnp.transpose(value, (0, 2, 1, 3)).reshape(count, model)
        with_small.append(jnp.concatenate([grad_attn[layer], jnp.pad(value, ((0, tall - count), (0, 0)))], axis=0))
    right = own_columns(both_rows(with_small))
    right = right.reshape(replicas, 2, rows + tall, right.shape[2])
    extra = jnp.sum(right[:, :, rows:].astype(F32), axis=(0, 1)).reshape(tall, folds, piece)
    extra = jnp.pad(
        jnp.transpose(extra, (1, 0, 2)), ((0, 0), (0, 0), (0, right.shape[3] - piece))
    ).astype(BF16)
    out_shard = weight_gradient(
        left_rows[:, model:], right[:, :, :rows].reshape(-1, right.shape[3]), extra
    )
    def side_by_side(value):
        return jnp.concatenate([value[j].astype(F32) for j in range(replicas)], axis=1)

    small = side_by_side(out_shard[:, gains.shape[2] :, :piece])
    out_shard = side_by_side(out_shard[:, : gains.shape[2]])
    right = own_columns(both_rows(grad_lin))
    shard = weight_gradient(left_rows[:, :model], right.reshape(-1, right.shape[2]), None)
    shard = side_by_side(shard)
    own_w = jnp.concatenate([w_query[0], w_key[0], w_value[0]], axis=1).astype(F32)
    gain_one = jnp.sum(shard * own_w, axis=1) / gains[0, 0].astype(F32)
    mine, got = expert_rows[0]
    got = by_order(got, all_x(got))
    batches = [jnp.where(is_first, mine, got), jnp.where(is_first, got, mine)]
    g_rows = flat_rows(jnp.stack(batches, axis=1))
    mine_w = [lax.dynamic_slice_in_dim(part[0], core * half, half, 0) for part in (w_gate, w_up, w_down)]
    made = [
        expert_grads(x_rows[i], g_rows[i], mine_w[0][i], mine_w[1][i], mine_w[2][i]) for i in range(half)
    ]
    expert_out = []
    for slot in range(3):
        keep = jnp.stack([one[slot] for one in made])
        got = swap_core(keep)
        both = jnp.concatenate(
            [jnp.where(core == 0, keep, got), jnp.where(core == 0, got, keep)], axis=0
        )
        expert_out.append(both.astype(F32)[None])

    layer_outputs = both_batches(outs)
    input_grads = both_batches(grads)
    return (
        layer_outputs[None, :, None],
        input_grads[None, :, None],
        jnp.stack([gain_one, small[expert_count]])[None],
        shard[None, :, :q_width],
        shard[None, :, q_width : q_width + kv_width],
        shard[None, :, q_width + kv_width : split],
        out_shard[None],
        small[:expert_count].T[None],
        expert_out[0],
        expert_out[1],
        expert_out[2],
    )


def solution(mesh):
    acts = P(None, R_AX, F_AX, None)
    rows = P(S_AX, F_AX, None)
    expert = P(S_AX, F_AX, None, None)
    stacked = P(S_AX, None, R_AX, F_AX, None)
    gain = P(S_AX, None, F_AX)
    return jax.shard_map(
        body,
        mesh=mesh,
        in_specs=(acts, acts, P(None, R_AX, None), stacked, gain)
        + (rows,) * 5
        + (expert,) * 3,
        out_specs=(stacked, stacked, gain) + (rows,) * 5 + (expert,) * 3,
        check_vma=False,
    )
```

```python
import functools

import jax
import jax.numpy as jnp
from jax import lax
from jax.experimental import pallas as pl
from jax.experimental.pallas import tpu as pltpu
from jax.sharding import PartitionSpec as P

HEAD = 128
ROPE_BASE = 1000000.0
EPS = 1e-06
MASKED = -1e30
F32 = jnp.float32
BF16 = jnp.bfloat16
S_AX, F_AX, R_AX = "section", "fsdp", "replica"
HIGHEST = lax.Precision.HIGHEST
LANES = 128
GELU_C = 0.7978845608028654
GELU_A = 0.044715


def dot(a, b):
    return lax.dot_general(a, b, (((1,), (0,)), ((), ())), preferred_element_type=F32)


def dot_nt(a, b):
    return lax.dot_general(a, b, (((1,), (1,)), ((), ())), preferred_element_type=F32)


def dot_tn(a, b):
    return lax.dot_general(a, b, (((0,), (0,)), ((), ())), preferred_element_type=F32)


def gelu_parts(x):
    t = jnp.tanh(GELU_C * (x + GELU_A * x * x * x))
    value = 0.5 * x * (1.0 + t)
    slope = 0.5 * (1.0 + t) + 0.5 * x * (1.0 - t * t) * GELU_C * (1.0 + 3.0 * GELU_A * x * x)
    return value, slope


def lane_is(shape, number):
    return lax.broadcasted_iota(jnp.int32, shape, 1) == number


def masked_mix(logits, mask):
    kept = jnp.where(mask > 0.0, logits, -1e30)
    expo = jnp.exp(kept - jnp.max(kept, axis=1, keepdims=True)) * mask
    return expo / jnp.sum(expo, axis=1, keepdims=True)


def one_hot(slots_ref, block, step, capacity):
    rows = slots_ref.shape[2]
    place = lax.broadcasted_iota(jnp.int32, (capacity, rows), 0)
    return place == slots_ref[block, step : step + 1, :]


def route_mask(tile, at, top):
    lane = lax.broadcasted_iota(jnp.int32, tile.shape, 1).astype(F32)
    named = tile.astype(F32)
    hit = lane == named[:, at : at + 1]
    for k in range(1, top):
        hit = hit | (lane == named[:, at + k : at + k + 1])
    return jnp.where(hit, 1.0, 0.0)


def weight_copies(scalars, own, pieces, buffers, sems):
    own_g, own_u, own_d = own
    parts = len(pieces[0][0])
    ff = own_g.shape[2] // parts
    is_own, flip = scalars[0], scalars[1]
    waits = {}
    for step in range(len(pieces[0])):
        for part in range(parts):
            expert = step ^ flip
            cols = pl.ds(part * ff, ff)
            sources = (own_g.at[expert, :, cols], own_u.at[expert, :, cols], own_d.at[expert, cols, :])
            for kind in range(3):
                target = buffers[kind].at[step, part]
                sem = sems.at[kind, step, part]

                @pl.when(is_own == 1)
                def _(source=sources[kind], target=target, sem=sem):
                    pltpu.make_async_copy(source, target, sem).start()

                @pl.when(is_own == 0)
                def _(source=pieces[kind][step][part], target=target, sem=sem):
                    pltpu.make_async_copy(source, target, sem).start()

                waits[kind, step, part] = pltpu.make_async_copy(
                    pieces[kind][step][part], target, sem
                )
    return waits


def split_refs(refs, counts):
    out, at = [], 0
    for count in counts:
        out.append(refs[at : at + count])
        at += count
    return out


def moe_fwd_kernel(folds, local, parts, capacity, routes_at, top, *refs):
    (scalars, router), tiles, blocks, own, flat, outs, partials, scratch = split_refs(
        refs, (2, folds, folds, 3, 3 * local * parts, 7, folds, 4)
    )
    scalars_ref = scalars
    picked_ref, gate_ref, up_ref, made_ref, grows_ref, slots, mix_ref = outs
    buf_g, buf_u, buf_d, sems = scratch
    pieces = [
        [[flat[(kind * local + step) * parts + part] for part in range(parts)] for step in range(local)]
        for kind in range(3)
    ]
    waits = weight_copies(scalars_ref, own, pieces, (buf_g, buf_u, buf_d), sems)
    rows = blocks[0].shape[0]
    width = blocks[0].shape[1]
    ff = buf_g.shape[3]
    square = (rows, rows)
    earlier = jnp.where(
        lax.broadcasted_iota(jnp.int32, square, 0) < lax.broadcasted_iota(jnp.int32, square, 1), 1.0, 0.0
    ).astype(BF16)
    same = jnp.where(
        lax.broadcasted_iota(jnp.int32, square, 0) == lax.broadcasted_iota(jnp.int32, square, 1), 1.0, 0.0
    ).astype(BF16)
    for k in range(folds):
        mask = route_mask(tiles[k][...], routes_at, top)
        mix = masked_mix(dot(blocks[k][...], router[...]), mask)
        if k == 0:
            mix_ref[...] = mix
        low = mask.astype(BF16)
        rank = dot_tn(low, earlier)
        named = dot_tn(low, same)
        place = jnp.where(named > 0.5, rank, -1.0)
        number = lax.broadcasted_iota(jnp.int32, place.shape, 0)
        for step in range(local):
            row = jnp.sum(jnp.where(number == scalars_ref[2 + step], place, 0.0), axis=0, keepdims=True)
            slots[k, step : step + 1, :] = row.astype(jnp.int32)
        for step in range(local):
            pick = one_hot(slots, k, step, capacity)
            at = pl.ds(k * capacity, capacity)
            picked_ref[step, at, :] = dot(
                jnp.where(pick, 1.0, 0.0).astype(BF16), blocks[k][...]
            ).astype(BF16)
            grows_ref[step, at, :] = lax.dot_general(
                jnp.where(pick, 1.0, 0.0), mix, (((1,), (0,)), ((), ())),
                precision=HIGHEST, preferred_element_type=F32,
            )
    for step in range(local):
        for part in range(parts):
            for kind in range(3):
                waits[kind, step, part].wait()
            cols = pl.ds(part * ff, ff)
            x = picked_ref[step]
            gate = dot(x, buf_g[step, part])
            up = dot(x, buf_u[step, part])
            gate_ref[step, :, cols] = gate
            up_ref[step, :, cols] = up
            inner = (gelu_parts(gate)[0] * up).astype(BF16)
            term = dot(inner, buf_d[step, part])
            made = term if part == 0 else made + term
        made_ref[step] = made.astype(BF16)
    for k in range(folds):
        at = pl.ds(k * capacity, capacity)
        picks, weighted = [], []
        for step in range(local):
            gates = grows_ref[step, at, :]
            own_lane = lane_is(gates.shape, scalars_ref[2 + step])
            factor = jnp.sum(jnp.where(own_lane, gates, 0.0), axis=1, keepdims=True)
            picks.append(jnp.where(one_hot(slots, k, step, capacity), 1.0, 0.0).astype(BF16))
            weighted.append((made_ref[step, at, :].astype(F32) * factor).astype(BF16))
        partials[k][...] = dot_tn(
            jnp.concatenate(picks, axis=0), jnp.concatenate(weighted, axis=0)
        ).astype(BF16)


def moe_bwd_kernel(folds, local, parts, capacity, *refs):
    (scalars, slots, gate_ref, up_ref, made_ref, grows_ref), blocks, own, flat, (ge_ref,), partials, scratch = split_refs(
        refs, (6, folds, 3, 3 * local * parts, 1, folds, 6)
    )
    buf_g, buf_u, buf_d, sems, dx_ref, dots_ref = scratch
    pieces = [
        [[flat[(kind * local + step) * parts + part] for part in range(parts)] for step in range(local)]
        for kind in range(3)
    ]
    waits = weight_copies(scalars, own, pieces, (buf_g, buf_u, buf_d), sems)
    ff = buf_g.shape[3]
    for step in range(local):
        for k in range(folds):
            at = pl.ds(k * capacity, capacity)
            pick = jnp.where(one_hot(slots, k, step, capacity), 1.0, 0.0).astype(BF16)
            dout = dot(pick, blocks[k][...])
            gates = grows_ref[step, at, :]
            own_lane = lane_is(gates.shape, scalars[2 + step])
            factor = jnp.sum(jnp.where(own_lane, gates, 0.0), axis=1, keepdims=True)
            value = jnp.sum(dout * made_ref[step, at, :].astype(F32), axis=1, keepdims=True)
            lane = lax.broadcasted_iota(jnp.int32, gates.shape, 1)
            number = scalars[2 + step]
            dots_ref[step, at, :] = jnp.where(
                (lane == number) | (lane == number + LANES // 2), value, 0.0
            )
            ge_ref[step, at, :] = (dout * factor).astype(BF16)
    for step in range(local):
        ge = ge_ref[step]
        for part in range(parts):
            for kind in range(3):
                waits[kind, step, part].wait()
            cols = pl.ds(part * ff, ff)
            grad_inner = dot_nt(ge, buf_d[step, part])
            gate = gate_ref[step, :, cols]
            up = up_ref[step, :, cols]
            value, slope = gelu_parts(gate)
            grad_gate = (grad_inner * up * slope).astype(BF16)
            grad_up = (grad_inner * value).astype(BF16)
            term = dot_nt(grad_gate, buf_g[step, part]) + dot_nt(grad_up, buf_u[step, part])
            total = term if part == 0 else total + term
        dx_ref[step] = total.astype(BF16)
    for k in range(folds):
        at = pl.ds(k * capacity, capacity)
        hot = [one_hot(slots, k, step, capacity) for step in range(local)]
        picks = jnp.concatenate([jnp.where(one, 1.0, 0.0) for one in hot], axis=0)
        width = ge_ref.shape[2]
        partials[k][:, :width] = dot_tn(
            picks.astype(BF16), jnp.concatenate([dx_ref[step, at, :] for step in range(local)], axis=0)
        ).astype(BF16)
        dots = lax.dot_general(
            picks, jnp.concatenate([dots_ref[step, at, :] for step in range(local)], axis=0),
            (((0,), (0,)), ((), ())), precision=HIGHEST, preferred_element_type=F32,
        )
        high = dots.astype(BF16).astype(F32)
        lane = lax.broadcasted_iota(jnp.int32, dots.shape, 1)
        partials[k][:, width:] = jnp.where(lane < LANES // 2, high, dots - high).astype(BF16)


def vmem(count):
    return [pl.BlockSpec(memory_space=pltpu.VMEM)] * count


def anywhere(count):
    return [pl.BlockSpec(memory_space=pl.ANY)] * count


def weight_scratch(own, local, parts):
    width, ff = own[0].shape[1], own[0].shape[2] // parts
    return [
        pltpu.VMEM((local, parts, width, ff), BF16),
        pltpu.VMEM((local, parts, width, ff), BF16),
        pltpu.VMEM((local, parts, ff, width), BF16),
        pltpu.SemaphoreType.DMA((3, local, parts)),
    ]


def cost(rows, width, ff, products):
    return pl.CostEstimate(
        flops=2 * rows * width * ff * products, bytes_accessed=2 * 3 * width * ff * 2 + 8 * rows * width,
        transcendentals=rows * ff,
    )


def moe_fwd_call(
    scalars, tiles, routes_at, router, blocks, own, flat, folds, local, rows, parts, width, ff, capacity, top
):
    picked_rows = folds * capacity
    shapes = [
        jax.ShapeDtypeStruct((local, picked_rows, width), BF16),
        jax.ShapeDtypeStruct((local, picked_rows, ff), F32),
        jax.ShapeDtypeStruct((local, picked_rows, ff), F32),
        jax.ShapeDtypeStruct((local, picked_rows, width), BF16),
        jax.ShapeDtypeStruct((local, picked_rows, LANES), F32),
        jax.ShapeDtypeStruct((folds, local, rows), jnp.int32),
        jax.ShapeDtypeStruct((rows, LANES), F32),
    ] + [jax.ShapeDtypeStruct((rows, width), BF16)] * folds
    out = pl.pallas_call(
        functools.partial(moe_fwd_kernel, folds, local, parts, capacity, routes_at, top),
        out_shape=shapes,
        in_specs=[pl.BlockSpec(memory_space=pltpu.SMEM)]
        + vmem(1 + 2 * folds) + anywhere(3 + len(flat)),
        out_specs=vmem(len(shapes)),
        scratch_shapes=weight_scratch(own, local, parts),
        cost_estimate=cost(local * picked_rows, width, ff, 3),
        compiler_params=pltpu.CompilerParams(vmem_limit_bytes=56 << 20),
    )(scalars, router, *tiles, *blocks, *own, *flat)
    return out[:7], out[7:]


def moe_bwd_call(scalars, kept, blocks, own, flat, folds, local, rows, parts, width, ff, capacity, top):
    _, gate_pre, up_pre, made, gate_rows, slots, _ = kept
    picked_rows = folds * capacity
    shapes = [jax.ShapeDtypeStruct((local, picked_rows, width), BF16)] + [
        jax.ShapeDtypeStruct((rows, width + LANES), BF16)
    ] * folds
    out = pl.pallas_call(
        functools.partial(moe_bwd_kernel, folds, local, parts, capacity),
        out_shape=shapes,
        in_specs=[pl.BlockSpec(memory_space=pltpu.SMEM)]
        + vmem(5 + folds) + anywhere(3 + len(flat)),
        out_specs=vmem(len(shapes)),
        scratch_shapes=weight_scratch(own, local, parts)
        + [pltpu.VMEM((local, picked_rows, width), BF16), pltpu.VMEM((local, picked_rows, LANES), F32)],
        cost_estimate=cost(local * picked_rows, width, ff, 3),
        compiler_params=pltpu.CompilerParams(vmem_limit_bytes=56 << 20),
    )(scalars, slots, gate_pre, up_pre, made, gate_rows, *blocks, *own, *flat)
    return out[0], out[1:]


def mm(a, b):
    return jnp.dot(a, b, preferred_element_type=F32)


def mm_nt(a, b):
    return lax.dot_general(a, b, (((1,), (1,)), ((), ())), preferred_element_type=F32)


def mm_shares(a, shares):
    if shares.ndim == 2:
        return mm_nt(a, shares)
    width = shares.shape[2]
    return sum(mm_nt(a[:, j * width : (j + 1) * width], shares[j]) for j in range(shares.shape[0]))


def mm_tn(a, b):
    return lax.dot_general(a, b, (((0,), (0,)), ((), ())), preferred_element_type=F32)


def ein(spec, a, b):
    return jnp.einsum(spec, a, b, preferred_element_type=F32)


def rel_gather(value):
    folds = lax.axis_size(F_AX)
    parts = [value]
    for k in range(1, folds):
        parts.append(lax.ppermute(value, F_AX, [(i, (i + k) % folds) for i in range(folds)]))
    return parts


def rel_scatter(parts):
    folds = lax.axis_size(F_AX)
    total = parts[0].astype(F32)
    for k in range(1, folds):
        got = lax.ppermute(parts[k], F_AX, [(i, (i - k) % folds) for i in range(folds)])
        total = total + got.astype(F32)
    return total


def send_back(parts):
    folds = lax.axis_size(F_AX)
    return [parts[0]] + [
        lax.ppermute(parts[k], F_AX, [(i, (i - k) % folds) for i in range(folds)]) for k in range(1, folds)
    ]


def add_up(parts):
    total = parts[0].astype(F32)
    for part in parts[1:]:
        total = total + part.astype(F32)
    return total


def swap_section(value):
    return lax.ppermute(value, S_AX, [(0, 1), (1, 0)])


def swap_core(value):
    count = lax.axis_size(R_AX)
    return lax.ppermute(value, R_AX, [(i, i ^ 1) for i in range(count)])


def rope_turn(values, cos, sin):
    half = HEAD // 2
    turned = jnp.concatenate([-values[..., half:], values[..., :half]], axis=-1)
    return values * cos + turned * sin


def rope_back(grads, cos, sin):
    half = HEAD // 2
    scaled = grads * sin
    turned = jnp.concatenate([scaled[..., half:], -scaled[..., :half]], axis=-1)
    return grads * cos + turned


def layout(lengths, position):
    bounds = jnp.cumsum(lengths)
    passed = (position[:, None] >= bounds[None, :]).astype(jnp.int32)
    segment = jnp.sum(passed, axis=1)
    start = jnp.sum(passed * lengths[None, :], axis=1)
    return segment, (position - start).astype(F32)


def gated(gate, up):
    return jax.nn.gelu(gate) * up


def attention_in(hidden, gain):
    scale = lax.rsqrt(jnp.mean(hidden * hidden, axis=1, keepdims=True) + EPS)
    normed = hidden * scale
    return scale, normed, (normed * gain.astype(F32)).astype(BF16)


def turn_heads(lin, common, kv_width):
    rows = lin.shape[0]
    q_width = lin.shape[1] - 2 * kv_width
    turned = rope_turn(
        lin[:, : q_width + kv_width].astype(F32).reshape(rows, -1, HEAD), common["cos"], common["sin"]
    ).astype(BF16).reshape(rows, -1)
    kv = jnp.concatenate([turned[:, q_width:], lin[:, q_width + kv_width :].astype(BF16)], axis=1)
    return turned[:, :q_width], kv


def grouped_heads(value, groups):
    rows = value.shape[0]
    return value.reshape(rows, groups, -1, HEAD)


def attend(query, kv_all, allowed, groups):
    keys = kv_all[:, : groups * HEAD].reshape(-1, groups, HEAD)
    values = kv_all[:, groups * HEAD :].reshape(-1, groups, HEAD)
    raw = ein("tgha,sga->ghts", grouped_heads(query, groups), keys) * HEAD ** (-0.5)
    scores = jnp.where(allowed[None, None], raw, MASKED)
    top = jnp.max(scores, axis=3, keepdims=True)
    expo = jnp.exp(scores - top)
    probs = expo / jnp.sum(expo, axis=3, keepdims=True)
    mixed = ein("ghts,sga->tgha", probs.astype(BF16), values)
    return mixed.reshape(query.shape), probs


def attend_back(grad_mixed, mixed, probs, query, kv_all, groups):
    rows = query.shape[0]
    keys = kv_all[:, : groups * HEAD].reshape(-1, groups, HEAD)
    values = kv_all[:, groups * HEAD :].reshape(-1, groups, HEAD)
    grad_grouped = grouped_heads(grad_mixed, groups)
    delta = jnp.sum(
        grad_grouped.astype(F32) * grouped_heads(mixed, groups), axis=3
    )
    delta = jnp.transpose(delta, (1, 2, 0))[..., None]
    grad_probs = ein("tgha,sga->ghts", grad_grouped, values)
    grad_scores = (probs * (grad_probs - delta)).astype(BF16)
    score_scale = HEAD ** (-0.5)
    grad_query = (ein("ghts,sga->tgha", grad_scores, keys) * score_scale).reshape(rows, -1, HEAD)
    grad_key = ein("ghts,tgha->sga", grad_scores, grouped_heads(query, groups)) * score_scale
    grad_value = ein("ghts,tgha->sga", probs.astype(BF16), grad_grouped)
    count = kv_all.shape[0]
    grad_kv = jnp.concatenate(
        [grad_key.reshape(count, -1), grad_value.reshape(count, -1)], axis=1
    ).astype(BF16)
    return grad_query, grad_kv


def moe_forward(router, tiles, routes_at, scalars, experts_w, size, blocks):
    outs, partials = moe_fwd_call(
        scalars, tiles, routes_at, router, blocks, *experts_w, **size
    )
    return partials, outs


def moe_backward(blocks, kept, scalars, experts_w, size, tie, hooks):
    blocks, tied = lax.optimization_barrier((blocks, tie))
    grad_expert, partials = moe_bwd_call(scalars, kept, blocks, *experts_w, **size)
    sent = hooks["rows"](grad_expert)
    summed, sent = lax.optimization_barrier((rel_scatter(partials), sent))
    width = blocks[0].shape[1]
    tail = summed[:, width:]
    half = LANES // 2
    dots = tail[:, :half] + tail[:, half:]
    return summed[:, :width], jnp.pad(dots, ((0, 0), (0, half))), sent, tied


def layer_forward(layer_in, weights, experts_w, common, tiles, routes_at, scalars, tie, projected=None, out_product=None):
    gains, w_qkv, w_out, router = weights
    groups = common["groups"]
    hidden = layer_in.astype(F32)
    scale, normed, attn_in = attention_in(hidden, gains[0])
    lin = mm(attn_in, w_qkv) if projected is None else projected
    lin, tied_lin = lax.optimization_barrier((lin, tie.get("lin", ())))
    query, kv = turn_heads(lin, common, groups * HEAD)
    kv_all, tied_kv = lax.optimization_barrier(
        (jnp.concatenate(rel_gather(kv), axis=0), tie.get("kv", ()))
    )
    mixed, probs = attend(query, kv_all, common["allowed"], groups)
    mixed_low = mixed.astype(BF16)
    more = tie["mixed"](tied_lin, tied_kv, attn_in, mixed_low) if "mixed" in tie else ()
    mixed_low, more = lax.optimization_barrier((mixed_low, more))
    if out_product is None:
        residual = hidden + mm(mixed_low, w_out)
    else:
        residual = hidden + out_product(mixed_low).astype(F32)
    scale_two = lax.rsqrt(jnp.mean(residual * residual, axis=1, keepdims=True) + EPS)
    normed_two = residual * scale_two
    moe_in = (normed_two * gains[1].astype(F32)).astype(BF16)
    if "moe" in tie:
        moe_in, experts_w, more = tie["moe"](moe_in, experts_w, more)
    blocks, tied = lax.optimization_barrier((rel_gather(moe_in), more))
    parts, moe_kept = moe_forward(router, tiles, routes_at, scalars, experts_w, common["size"], blocks)
    finish = lambda got: (residual + add_up(got)).astype(BF16)
    out = finish(send_back(parts)) if "last" not in tie else (parts, finish)
    kept = dict(
        scale=scale, normed=normed, attn_in=attn_in, query=query, kv=kv,
        kv_all=kv_all, mixed=mixed, probs=probs, mixed_low=mixed_low, scale_two=scale_two,
        normed_two=normed_two, moe_in=moe_in, mix=moe_kept[6], moe=moe_kept,
    )
    return out, kept, experts_w, tied


def layer_backward(grad_low, kept, weights, experts_w, common, scalars, tie, hooks):
    gains, w_qkv, w_out, router = weights
    groups = common["groups"]
    grad_out = grad_low.astype(F32)
    rows = grad_out.shape[0]
    blocks = hooks["blocks"] if "blocks" in hooks else rel_gather(grad_low)
    grad_moe_in, dots, sent, tied = moe_backward(
        blocks, kept["moe"], scalars, experts_w, common["size"], tie, hooks
    )
    mix = kept["mix"]
    grad_logits = mix * (dots - jnp.sum(mix * dots, axis=1, keepdims=True))
    moe_in = kept["moe_in"]
    count = common["experts"]
    high = grad_logits.astype(BF16)
    rest = (grad_logits - high.astype(F32)).astype(BF16)
    both = mm_tn(jnp.concatenate([high[:, :count], rest[:, :count]], axis=1), moe_in)
    grad_router = both[:count] + both[count:]
    grad_moe_in = grad_moe_in + mm_nt(high, router) + mm_nt(rest, router)
    normed_two = kept["normed_two"]
    grad_norm = grad_moe_in * gains[1].astype(F32)
    grad_gain_two = jnp.sum(grad_moe_in * normed_two, axis=0)
    grad_mid = grad_out + kept["scale_two"] * (
        grad_norm - normed_two * jnp.mean(grad_norm * normed_two, axis=1, keepdims=True)
    )
    grad_attn = grad_mid.astype(BF16)
    small = jnp.concatenate([grad_router, grad_gain_two[None]], axis=0).astype(BF16)
    crossed = hooks["attn"](grad_attn, small, sent)
    grad_mixed = mm_shares(grad_attn, w_out).astype(BF16)
    grad_query, grad_kv = attend_back(
        grad_mixed, kept["mixed"], kept["probs"], kept["query"], kept["kv_all"], groups
    )
    grad_kv, crossed = lax.optimization_barrier((grad_kv, crossed))
    later = hooks["later"](sent, crossed)
    own = rel_scatter([grad_kv[k * rows : (k + 1) * rows] for k in range(lax.axis_size(F_AX))])
    own, later = lax.optimization_barrier((own, later))
    cos, sin = common["cos"], common["sin"]
    kv_width = groups * HEAD
    grad_lin = jnp.concatenate(
        [
            rope_back(grad_query, cos, sin).reshape(rows, -1),
            rope_back(own[:, :kv_width].reshape(rows, -1, HEAD), cos, sin).reshape(rows, -1),
            own[:, kv_width:],
        ],
        axis=1,
    ).astype(BF16)
    grad_attn_in = mm_shares(grad_lin, w_qkv)
    normed = kept["normed"]
    grad_norm = grad_attn_in * gains[0].astype(F32)
    grad_in = grad_mid + kept["scale"] * (
        grad_norm - normed * jnp.mean(grad_norm * normed, axis=1, keepdims=True)
    )
    return grad_in.astype(BF16), grad_lin, later, tied


def expert_middle(rows_in, grad_rows, gate_w, up_w, down_w):
    value, slope = gelu_parts(mm(rows_in, gate_w))
    up_pre = mm(rows_in, up_w)
    grad_inner = mm_nt(grad_rows, down_w)
    return (
        (value * up_pre).astype(BF16),
        (grad_inner * up_pre * slope).astype(BF16),
        (grad_inner * value).astype(BF16),
    )


def body(
    tokens, cotangent, seq_lengths, routes, gains, w_query, w_key, w_value, w_out, w_router, w_gate, w_up, w_down
):
    section = lax.axis_index(S_AX)
    is_first = section == 0
    fold_id = lax.axis_index(F_AX)
    replica = lax.axis_index(R_AX)
    core = replica % 2
    flip = (replica // 2) % 2
    folds, replicas = lax.axis_size(F_AX), lax.axis_size(R_AX)
    rows = tokens.shape[2]
    top = routes.shape[4]
    local = w_gate.shape[1]
    expert_count = w_router.shape[2]
    kv_width = w_key.shape[2]
    q_width = w_query.shape[2]
    capacity = rows * top // expert_count

    def own_batch(value):
        return lax.dynamic_index_in_dim(value, section, 0, keepdims=False)

    def swap_xor(value, bit):
        return lax.ppermute(value, R_AX, [(i, i ^ bit) for i in range(replicas)])

    def own_layer(pair):
        return jnp.where(is_first, pair[0], pair[1])

    def other_layer(pair):
        return jnp.where(is_first, pair[1], pair[0])

    def by_section(keep, got):
        return jnp.stack([jnp.where(is_first, keep, got), jnp.where(is_first, got, keep)])

    def both_batches(pair):
        return by_section(own_layer(pair), swap_section(other_layer(pair)))

    split = q_width + 2 * kv_width
    routes_at = HEAD // 4

    def widened(pieces):
        weights_part, routes_part = pieces
        routes_part = jnp.pad(routes_part.astype(BF16), ((0, weights_part.shape[0] - rows), (0, 0)))
        gap = jnp.zeros((weights_part.shape[0], routes_at - weights_part.shape[1]), BF16)
        whole = jnp.concatenate([weights_part, gap, routes_part], axis=1)
        return jnp.pad(whole, ((0, 0), (0, HEAD - whole.shape[1])))

    small = jnp.concatenate([w_router[0], gains[0].T], axis=1)
    my_routes = own_batch(routes[0, :, 0])
    give_routes = lax.dynamic_index_in_dim(routes[0, :, 0], 1 - section, 0, keepdims=False)
    joined = jnp.concatenate([w_query[0], w_key[0], w_value[0]], axis=1)
    depth = joined.shape[0]

    def column_share(value):
        width = value.shape[1] // replicas
        return lax.dynamic_slice_in_dim(value, replica * width, width, 1)

    def stacked_parts(parts):
        whole = jnp.zeros((folds,) + parts[0].shape, parts[0].dtype)
        for k, part in enumerate(parts):
            whole = lax.dynamic_update_index_in_dim(whole, part, (fold_id - k) % folds, 0)
        return whole.reshape((-1,) + parts[0].shape[1:])

    def stacked_rows(value):
        return stacked_parts(rel_gather(value))

    def of_first(value):
        return jnp.where(is_first, value, swap_section(value))

    def share_back(value):
        whole = jnp.zeros(value.shape, value.dtype)
        for bit in range(replicas):
            got = value[bit] if bit == 0 else swap_xor(value[bit], bit)
            whole = lax.dynamic_update_index_in_dim(whole, got, replica ^ bit, 0)
        return jnp.concatenate([whole[j] for j in range(replicas)], axis=1)

    def group_rows(value):
        parts = []
        for bit in range(0, replicas, 2):
            same = value if bit == 0 else swap_xor(value, bit)
            parts += [same, swap_core(same)]
        return parts

    my_tokens = own_batch(tokens[:, 0])
    token_group = jnp.concatenate(group_rows(my_tokens), axis=0)
    head_own = column_share(joined)
    lin_width = head_own.shape[1]
    head_swap = swap_section(jnp.concatenate([head_own, widened((small, give_routes))], axis=1))
    got_routes = head_swap[:rows, lin_width + routes_at : lin_width + routes_at + top].astype(jnp.int32)
    both_routes = jnp.where(
        is_first,
        jnp.concatenate([my_routes, got_routes], axis=1),
        jnp.concatenate([got_routes, my_routes], axis=1),
    )
    tail_cols = jnp.where(is_first, small, head_swap[:, lin_width : lin_width + small.shape[1]])
    head_got = jnp.concatenate(
        [jnp.where(is_first, head_own, head_swap[:, :lin_width]), widened((tail_cols, both_routes))], axis=1
    )
    part_ff = w_gate.shape[3] // 2
    pieces = []
    for part, axis in ((w_gate, 1), (w_up, 1), (w_down, 0)):
        chosen = lax.dynamic_index_in_dim(part[0], flip, 0, keepdims=False)
        pieces.append(lax.dynamic_slice_in_dim(chosen, core * part_ff, part_ff, axis))
    pieces, head_got = lax.optimization_barrier((pieces, head_got))
    crossed_y = [swap_section(pieces[0]), None, None]
    last_grad = own_batch(cotangent[:, 0])
    head_got, last_blocks = lax.optimization_barrier((head_got, rel_gather(last_grad)))
    head_parts, crossed_y[0] = lax.optimization_barrier((rel_gather(head_got), crossed_y[0]))
    head_block = stacked_parts(head_parts)
    tiles = [part[:rows, lin_width:] for part in head_parts]
    crossed_y[1:] = [swap_section(value) for value in pieces[1:]]
    first = fold_id * local
    numbers = first + (jnp.arange(local, dtype=jnp.int32) ^ flip)
    scalars = [
        jnp.concatenate([jnp.stack([(section == layer).astype(jnp.int32), flip]), numbers]).astype(jnp.int32)
        for layer in range(2)
    ]
    first_tail = head_block[:, lin_width:]
    out_block = of_first(column_share(w_out[0]))
    head_block, out_block = lax.optimization_barrier((head_block, out_block))
    out_block = stacked_rows(out_block)
    group_in = attention_in(token_group.astype(F32), first_tail[:, expert_count])[2]
    first_lin = share_back(
        mm(group_in, head_block[:, :lin_width]).astype(BF16).reshape(replicas, rows, lin_width)
    )

    def first_out(mixed_low):
        group = jnp.concatenate(group_rows(mixed_low), axis=0)
        made = mm(group, out_block).astype(BF16)
        return share_back(made.reshape(replicas, rows, -1))

    shard = jnp.concatenate([joined, jnp.pad(small, ((0, 0), (0, HEAD - small.shape[1]))), w_out[0]], axis=1)
    share = depth // (2 * replicas)
    keep = lax.dynamic_slice_in_dim(shard, (section * replicas + replica) * share, share, 0)
    give = lax.dynamic_slice_in_dim(shard, ((1 - section) * replicas + replica) * share, share, 0)
    give, _ = lax.optimization_barrier((give, head_got))
    got = swap_section(give)

    def whole_weights(layer, keep, got):
        piece = jnp.where(section == layer, keep, got)
        full = lax.all_gather(piece, (F_AX, S_AX, R_AX), axis=0, tiled=True)
        tail = full[:, split : split + LANES]
        return tail[:, expert_count : expert_count + 2].T, full[:, :split], full[:, split + LANES :], tail

    first_w = (
        first_tail[:, expert_count : expert_count + 2].T, None, None, first_tail
    )
    size = dict(
        folds=folds, local=local, rows=rows, parts=2, width=tokens.shape[3], ff=w_gate.shape[3],
        capacity=capacity, top=top,
    )

    lengths = own_batch(seq_lengths[:, 0])
    position = fold_id * rows + jnp.arange(rows, dtype=jnp.int32)
    order = (fold_id - jnp.arange(folds)) % folds
    key_pos = (order[:, None] * rows + jnp.arange(rows)[None, :]).reshape(-1).astype(jnp.int32)
    segment, offset = layout(lengths, position)
    key_seg, _ = layout(lengths, key_pos)
    freq = ROPE_BASE ** (-2.0 * jnp.arange(HEAD // 2, dtype=F32) / HEAD)
    angles = offset[:, None] * freq
    angles = jnp.concatenate([angles, angles], axis=1)[:, None, :]
    common = dict(
        cos=jnp.cos(angles), sin=jnp.sin(angles), groups=kv_width // HEAD, size=size,
        experts=expert_count,
        allowed=(segment[:, None] == key_seg[None, :]) & (key_pos[None, :] <= position[:, None]),
    )

    def first_mixed(tied_lin, tied, attn_in, mixed_low):
        gate_x, up_y = tied
        held["second"] = whole_weights(1, *tied_lin)
        return (crossed_y[0], up_y, crossed_y[2]), (gate_x,)

    def first_moe(moe_in, own, more):
        same, cross, moe_in = lax.optimization_barrier((*more, moe_in))
        cross = [*cross, swap_xor(same[1], 2), swap_xor(same[2], 2)]
        flat = []
        for one, two in zip(same, cross):
            flat += [one, swap_core(one), two, swap_core(two)]
        return moe_in, (own, flat), ()

    held = {}
    first_value, first_kept, experts_w, _ = layer_forward(
        my_tokens, first_w, (w_gate[0], w_up[0], w_down[0]), common, tiles, routes_at, scalars[0],
        dict(lin=(keep, got), kv=(swap_xor(crossed_y[0], 2), crossed_y[1]), mixed=first_mixed, moe=first_moe),
        first_lin, first_out,
    )
    head_share, out_share, _ = lax.optimization_barrier(
        (head_block[:, :lin_width], out_block, first_kept["moe"][1])
    )
    weights_first = (
        first_w[0], lax.all_gather(head_share, R_AX, axis=0), lax.all_gather(out_share, R_AX, axis=0), first_tail
    )

    second_w = held["second"]

    def left_pair(attn_in, mixed_low):
        pair = (
            jnp.concatenate([first_kept["attn_in"], first_kept["mixed_low"]], axis=1),
            jnp.concatenate([attn_in, mixed_low], axis=1),
        )
        return own_layer(pair), swap_section(other_layer(pair))

    second_value, second_kept, _, tied = layer_forward(
        first_value, second_w, experts_w, common, tiles, routes_at + top, scalars[1],
        dict(
            mixed=lambda one, two, attn_in, mixed_low: (attn_in, mixed_low),
            moe=lambda moe_in, own, more: (moe_in, own, (left_pair(*more), weights_first)),
            last=True,
        ),
    )
    left_rows, weights_first = tied
    second_parts, second_finish = second_value
    left_rows = jnp.concatenate(left_rows, axis=0)
    kept, weights = [first_kept, second_kept], [weights_first, second_w]

    half = local // 2

    def chip_rows(pair):
        chip = []
        for value in pair:
            keep = lax.dynamic_slice_in_dim(value, (core ^ flip) * half, half, 0)
            give = lax.dynamic_slice_in_dim(value, (1 - (core ^ flip)) * half, half, 0)
            got = swap_core(give)
            chip.append(
                jnp.concatenate(
                    [jnp.where(core == 0, keep, got), jnp.where(core == 0, got, keep)], axis=1
                )
            )
        return chip

    chips = replicas // 2

    def all_x(value):
        return [swap_xor(value, bit) for bit in range(2, replicas, 2)]

    def by_order(value, others):
        whole = jnp.zeros((chips,) + value.shape, value.dtype)
        for at, part in enumerate([value] + others):
            whole = lax.dynamic_update_index_in_dim(whole, part, (replica // 2) ^ at, 0)
        return whole

    def flat_rows(whole):
        return jnp.moveaxis(whole, 1, 0).reshape(half, -1, whole.shape[-1])

    x_chip = chip_rows([state["moe"][0] for state in kept])
    x_mine, x_give = own_layer(x_chip), other_layer(x_chip)
    def both_rows(pair):
        return jnp.concatenate([own_layer(pair), swap_section(other_layer(pair))], axis=0)

    def own_columns(value):
        width = value.shape[1] // replicas
        parts = []
        for bit in range(replicas):
            piece = lax.dynamic_slice_in_dim(value, (replica ^ bit) * width, width, 1)
            parts.append(piece if bit == 0 else swap_xor(piece, bit))
        return jnp.stack(parts)

    def fold_sum(left, right, extra, tie):
        total = mm_tn(left, right).astype(BF16)
        if extra is not None:
            total = total.reshape(folds, -1, total.shape[1])
            total = jnp.concatenate([total, extra], axis=1).reshape(-1, total.shape[2])
        mine = lax.psum_scatter(total, F_AX, scatter_dimension=0, tiled=True)
        whole = jnp.zeros((replicas,) + mine.shape, BF16)
        for bit, part in enumerate(group_rows(mine)):
            whole = lax.dynamic_update_index_in_dim(whole, part, replica ^ bit, 0)
        return whole, tie

    def side_by_side(value):
        return jnp.concatenate([value[j].astype(F32) for j in range(replicas)], axis=1)

    left_whole = group_rows(left_rows)
    model = tokens.shape[3]
    piece = model // (folds * replicas)
    count = expert_count + 1
    tall = -(-count // 16) * 16

    def with_small(grad_attn, small):
        value = small.reshape(count, folds, replicas, piece)
        value = jnp.transpose(value, (0, 2, 1, 3)).reshape(count, model)
        return jnp.concatenate([grad_attn, jnp.pad(value, ((0, tall - count), (0, 0)))], axis=0)

    def last_rows(grad_expert):
        held["rows"] = chip_rows([grad_expert])[0]
        return left_whole, stacked_parts(second_parts), swap_section(x_give)

    def last_attn(grad_attn, small, sent):
        held["attn"] = with_small(grad_attn, small)
        return all_x(x_mine)

    def first_rows(grad_expert):
        chip = (chip_rows([grad_expert])[0], held["rows"])
        mine = own_layer(chip)
        return mine, all_x(mine), swap_section(other_layer(chip))

    def first_attn(grad_attn, small, sent):
        return both_rows((with_small(grad_attn, small), held["attn"])), sent

    def first_later(sent, crossed):
        right_out, (mine, mine_x, got) = crossed
        held["got_x"] = all_x(got)
        g_own = by_order(mine, mine_x)
        return g_own, [expert_middle(x_own[i], flat_rows(g_own)[i], *[w[i] for w in mine_w]) for i in range(half)], got, own_columns(right_out)

    grads, grad_lin = [None, None], [None, None]
    grads[1], grad_lin[1], ((left_whole, second_stack, x_got), x_mine_x, x_got_x), _ = layer_backward(
        last_grad, kept[1], weights[1], experts_w, common, scalars[1], (),
        dict(rows=last_rows, attn=last_attn, later=lambda sent, crossed: (sent, crossed, all_x(sent[2])), blocks=last_blocks),
    )
    second_sum = lax.psum_scatter(second_stack, F_AX, scatter_dimension=0, tiled=True)
    outs = [first_value, second_finish([second_sum])]
    x_own = flat_rows(by_order(x_mine, x_mine_x))
    x_own = [x_own[i] for i in range(half)]
    mine_w = [lax.dynamic_slice_in_dim(part[0], core * half, half, 0) for part in (w_gate, w_up, w_down)]
    grads[0], grad_lin[0], later, _ = layer_backward(
        grads[1], kept[0], weights[0], experts_w, common, scalars[0], (),
        dict(rows=first_rows, attn=first_attn, later=first_later),
    )
    g_own, middle_own, got, right_out = later
    left_whole = jnp.concatenate(left_whole, axis=0)
    lin_rows = both_rows(grad_lin)
    got_x = held["got_x"]
    lin_rows, outs = lax.optimization_barrier((lin_rows, outs))
    right = own_columns(lin_rows)
    g_got, x_got = by_order(got, got_x), by_order(x_got, x_got_x)
    right, g_got, x_got = lax.optimization_barrier((right, g_got, x_got))
    x_got = [flat_rows(x_got)[i] for i in range(half)]
    g_own, g_got = [[flat_rows(value)[i] for i in range(half)] for value in (g_own, g_got)]
    middle_got = [expert_middle(x_got[i], g_got[i], *[w[i] for w in mine_w]) for i in range(half)]

    right_out = right_out.reshape(replicas, 2, rows + tall, -1)
    extra = jnp.sum(right_out[:, :, rows:].astype(F32), axis=(0, 1)).reshape(tall, folds, piece)
    extra = jnp.pad(
        jnp.transpose(extra, (1, 0, 2)), ((0, 0), (0, 0), (0, right_out.shape[3] - piece))
    ).astype(BF16)
    right_out = right_out[:, :, :rows].reshape(-1, right_out.shape[3])
    out_shard, _ = fold_sum(left_whole[:, model:], right_out, extra, ())
    shard, middle_got = fold_sum(left_whole[:, :model], right.reshape(-1, right.shape[2]), None, middle_got)
    made = []
    for i in range(half):
        inner, gate, up = zip(middle_own[i], middle_got[i])
        made.append(
            (
                (mm_tn(x_own[i], gate[0]) + mm_tn(x_got[i], gate[1])).astype(BF16),
                (mm_tn(x_own[i], up[0]) + mm_tn(x_got[i], up[1])).astype(BF16),
                (mm_tn(inner[0], g_own[i]) + mm_tn(inner[1], g_got[i])).astype(BF16),
            )
        )
    small = side_by_side(out_shard[:, depth:, :piece])
    out_shard = side_by_side(out_shard[:, :depth])
    shard = side_by_side(shard)
    gain_one = jnp.sum(shard * joined.astype(F32), axis=1) / gains[0, 0].astype(F32)
    expert_out = []
    for slot in range(3):
        keep = jnp.stack([one[slot] for one in made])
        got = swap_core(keep)
        both = jnp.concatenate(
            [jnp.where(core == 0, keep, got), jnp.where(core == 0, got, keep)], axis=0
        )
        expert_out.append(both.astype(F32)[None])
    layer_outputs = both_batches(outs)
    input_grads = both_batches(grads)
    return (
        layer_outputs[None, :, None],
        input_grads[None, :, None],
        jnp.stack([gain_one, small[expert_count]])[None],
        shard[None, :, :q_width],
        shard[None, :, q_width : q_width + kv_width],
        shard[None, :, q_width + kv_width : split],
        out_shard[None],
        small[:expert_count].T[None],
        expert_out[0],
        expert_out[1],
        expert_out[2],
    )


def solution(mesh):
    acts = P(None, R_AX, F_AX, None)
    rows = P(S_AX, F_AX, None)
    expert = P(S_AX, F_AX, None, None)
    stacked = P(S_AX, None, R_AX, F_AX, None)
    gain = P(S_AX, None, F_AX)
    return jax.shard_map(
        body,
        mesh=mesh,
        in_specs=(acts, acts, P(None, R_AX, None), stacked, gain)
        + (rows,) * 5
        + (expert,) * 3,
        out_specs=(stacked, stacked, gain) + (rows,) * 5 + (expert,) * 3,
        check_vma=False,
    )
```

```python
import functools

import jax
import jax.numpy as jnp
from jax import lax
from jax.experimental import pallas as pl
from jax.experimental.pallas import tpu as pltpu
from jax.sharding import PartitionSpec as P

HEAD = 128
ROPE_BASE = 1000000.0
EPS = 1e-06
MASKED = -1e30
F32 = jnp.float32
BF16 = jnp.bfloat16
S_AX, F_AX, R_AX = "section", "fsdp", "replica"
HIGHEST = lax.Precision.HIGHEST
LANES = 128
GELU_C = 0.7978845608028654
GELU_A = 0.044715


def dot(a, b):
    return lax.dot_general(a, b, (((1,), (0,)), ((), ())), preferred_element_type=F32)


def dot_nt(a, b):
    return lax.dot_general(a, b, (((1,), (1,)), ((), ())), preferred_element_type=F32)


def dot_tn(a, b):
    return lax.dot_general(a, b, (((0,), (0,)), ((), ())), preferred_element_type=F32)


def gelu_parts(x):
    t = jnp.tanh(GELU_C * (x + GELU_A * x * x * x))
    value = 0.5 * x * (1.0 + t)
    slope = 0.5 * (1.0 + t) + 0.5 * x * (1.0 - t * t) * GELU_C * (1.0 + 3.0 * GELU_A * x * x)
    return value, slope


def lane_is(shape, number):
    return lax.broadcasted_iota(jnp.int32, shape, 1) == number


def masked_mix(logits, mask):
    kept = jnp.where(mask > 0.0, logits, -1e30)
    expo = jnp.exp(kept - jnp.max(kept, axis=1, keepdims=True)) * mask
    return expo / jnp.sum(expo, axis=1, keepdims=True)


def one_hot(slots_ref, block, step, capacity):
    rows = slots_ref.shape[2]
    place = lax.broadcasted_iota(jnp.int32, (capacity, rows), 0)
    return place == slots_ref[block, step : step + 1, :]


def route_mask(tile, at, top):
    lane = lax.broadcasted_iota(jnp.int32, tile.shape, 1).astype(F32)
    named = tile.astype(F32)
    hit = lane == named[:, at : at + 1]
    for k in range(1, top):
        hit = hit | (lane == named[:, at + k : at + k + 1])
    return jnp.where(hit, 1.0, 0.0)


def weight_copies(scalars, own, pieces, buffers, sems):
    own_g, own_u, own_d = own
    parts = len(pieces[0][0])
    ff = own_g.shape[2] // parts
    is_own, flip = scalars[0], scalars[1]
    waits = {}
    for step in range(len(pieces[0])):
        for part in range(parts):
            expert = step ^ flip
            cols = pl.ds(part * ff, ff)
            sources = (own_g.at[expert, :, cols], own_u.at[expert, :, cols], own_d.at[expert, cols, :])
            for kind in range(3):
                target = buffers[kind].at[step, part]
                sem = sems.at[kind, step, part]

                @pl.when(is_own == 1)
                def _(source=sources[kind], target=target, sem=sem):
                    pltpu.make_async_copy(source, target, sem).start()

                @pl.when(is_own == 0)
                def _(source=pieces[kind][step][part], target=target, sem=sem):
                    pltpu.make_async_copy(source, target, sem).start()

                waits[kind, step, part] = pltpu.make_async_copy(
                    pieces[kind][step][part], target, sem
                )
    return waits


def split_refs(refs, counts):
    out, at = [], 0
    for count in counts:
        out.append(refs[at : at + count])
        at += count
    return out


def moe_fwd_kernel(folds, local, parts, capacity, routes_at, top, *refs):
    (scalars, router), tiles, blocks, own, flat, outs, partials, scratch = split_refs(
        refs, (2, folds, folds, 3, 3 * local * parts, 7, folds, 4)
    )
    scalars_ref = scalars
    picked_ref, gate_ref, up_ref, made_ref, grows_ref, slots, mix_ref = outs
    buf_g, buf_u, buf_d, sems = scratch
    pieces = [
        [[flat[(kind * local + step) * parts + part] for part in range(parts)] for step in range(local)]
        for kind in range(3)
    ]
    waits = weight_copies(scalars_ref, own, pieces, (buf_g, buf_u, buf_d), sems)
    rows = blocks[0].shape[0]
    width = blocks[0].shape[1]
    ff = buf_g.shape[3]
    square = (rows, rows)
    earlier = jnp.where(
        lax.broadcasted_iota(jnp.int32, square, 0) < lax.broadcasted_iota(jnp.int32, square, 1), 1.0, 0.0
    ).astype(BF16)
    same = jnp.where(
        lax.broadcasted_iota(jnp.int32, square, 0) == lax.broadcasted_iota(jnp.int32, square, 1), 1.0, 0.0
    ).astype(BF16)
    for k in range(folds):
        mask = route_mask(tiles[k][...], routes_at, top)
        mix = masked_mix(dot(blocks[k][...], router[...]), mask)
        if k == 0:
            mix_ref[...] = mix
        low = mask.astype(BF16)
        rank = dot_tn(low, earlier)
        named = dot_tn(low, same)
        place = jnp.where(named > 0.5, rank, -1.0)
        number = lax.broadcasted_iota(jnp.int32, place.shape, 0)
        for step in range(local):
            row = jnp.sum(jnp.where(number == scalars_ref[2 + step], place, 0.0), axis=0, keepdims=True)
            slots[k, step : step + 1, :] = row.astype(jnp.int32)
        for step in range(local):
            pick = one_hot(slots, k, step, capacity)
            at = pl.ds(k * capacity, capacity)
            picked_ref[step, at, :] = dot(
                jnp.where(pick, 1.0, 0.0).astype(BF16), blocks[k][...]
            ).astype(BF16)
            grows_ref[step, at, :] = lax.dot_general(
                jnp.where(pick, 1.0, 0.0), mix, (((1,), (0,)), ((), ())),
                precision=HIGHEST, preferred_element_type=F32,
            )
    for step in range(local):
        for part in range(parts):
            for kind in range(3):
                waits[kind, step, part].wait()
            cols = pl.ds(part * ff, ff)
            x = picked_ref[step]
            gate = dot(x, buf_g[step, part])
            up = dot(x, buf_u[step, part])
            gate_ref[step, :, cols] = gate
            up_ref[step, :, cols] = up
            inner = (gelu_parts(gate)[0] * up).astype(BF16)
            term = dot(inner, buf_d[step, part])
            made = term if part == 0 else made + term
        made_ref[step] = made.astype(BF16)
    for k in range(folds):
        at = pl.ds(k * capacity, capacity)
        picks, weighted = [], []
        for step in range(local):
            gates = grows_ref[step, at, :]
            own_lane = lane_is(gates.shape, scalars_ref[2 + step])
            factor = jnp.sum(jnp.where(own_lane, gates, 0.0), axis=1, keepdims=True)
            picks.append(jnp.where(one_hot(slots, k, step, capacity), 1.0, 0.0).astype(BF16))
            weighted.append((made_ref[step, at, :].astype(F32) * factor).astype(BF16))
        partials[k][...] = dot_tn(
            jnp.concatenate(picks, axis=0), jnp.concatenate(weighted, axis=0)
        ).astype(BF16)


def moe_bwd_kernel(folds, local, parts, capacity, *refs):
    (scalars, slots, gate_ref, up_ref, made_ref, grows_ref), blocks, own, flat, (ge_ref,), partials, scratch = split_refs(
        refs, (6, folds, 3, 3 * local * parts, 1, folds, 6)
    )
    buf_g, buf_u, buf_d, sems, dx_ref, dots_ref = scratch
    pieces = [
        [[flat[(kind * local + step) * parts + part] for part in range(parts)] for step in range(local)]
        for kind in range(3)
    ]
    waits = weight_copies(scalars, own, pieces, (buf_g, buf_u, buf_d), sems)
    ff = buf_g.shape[3]
    for step in range(local):
        for k in range(folds):
            at = pl.ds(k * capacity, capacity)
            pick = jnp.where(one_hot(slots, k, step, capacity), 1.0, 0.0).astype(BF16)
            dout = dot(pick, blocks[k][...])
            gates = grows_ref[step, at, :]
            own_lane = lane_is(gates.shape, scalars[2 + step])
            factor = jnp.sum(jnp.where(own_lane, gates, 0.0), axis=1, keepdims=True)
            value = jnp.sum(dout * made_ref[step, at, :].astype(F32), axis=1, keepdims=True)
            lane = lax.broadcasted_iota(jnp.int32, gates.shape, 1)
            number = scalars[2 + step]
            dots_ref[step, at, :] = jnp.where(
                (lane == number) | (lane == number + LANES // 2), value, 0.0
            )
            ge_ref[step, at, :] = (dout * factor).astype(BF16)
    for step in range(local):
        ge = ge_ref[step]
        for part in range(parts):
            for kind in range(3):
                waits[kind, step, part].wait()
            cols = pl.ds(part * ff, ff)
            grad_inner = dot_nt(ge, buf_d[step, part])
            gate = gate_ref[step, :, cols]
            up = up_ref[step, :, cols]
            value, slope = gelu_parts(gate)
            grad_gate = (grad_inner * up * slope).astype(BF16)
            grad_up = (grad_inner * value).astype(BF16)
            term = dot_nt(grad_gate, buf_g[step, part]) + dot_nt(grad_up, buf_u[step, part])
            total = term if part == 0 else total + term
        dx_ref[step] = total.astype(BF16)
    for k in range(folds):
        at = pl.ds(k * capacity, capacity)
        hot = [one_hot(slots, k, step, capacity) for step in range(local)]
        picks = jnp.concatenate([jnp.where(one, 1.0, 0.0) for one in hot], axis=0)
        width = ge_ref.shape[2]
        partials[k][:, :width] = dot_tn(
            picks.astype(BF16), jnp.concatenate([dx_ref[step, at, :] for step in range(local)], axis=0)
        ).astype(BF16)
        dots = lax.dot_general(
            picks, jnp.concatenate([dots_ref[step, at, :] for step in range(local)], axis=0),
            (((0,), (0,)), ((), ())), precision=HIGHEST, preferred_element_type=F32,
        )
        high = dots.astype(BF16).astype(F32)
        lane = lax.broadcasted_iota(jnp.int32, dots.shape, 1)
        partials[k][:, width:] = jnp.where(lane < LANES // 2, high, dots - high).astype(BF16)


def vmem(count):
    return [pl.BlockSpec(memory_space=pltpu.VMEM)] * count


def anywhere(count):
    return [pl.BlockSpec(memory_space=pl.ANY)] * count


def weight_scratch(own, local, parts):
    width, ff = own[0].shape[1], own[0].shape[2] // parts
    return [
        pltpu.VMEM((local, parts, width, ff), BF16),
        pltpu.VMEM((local, parts, width, ff), BF16),
        pltpu.VMEM((local, parts, ff, width), BF16),
        pltpu.SemaphoreType.DMA((3, local, parts)),
    ]


def cost(rows, width, ff, products):
    return pl.CostEstimate(
        flops=2 * rows * width * ff * products, bytes_accessed=2 * 3 * width * ff * 2 + 8 * rows * width,
        transcendentals=rows * ff,
    )


def moe_fwd_call(
    scalars, tiles, routes_at, router, blocks, own, flat, folds, local, rows, parts, width, ff, capacity, top, tile_at
):
    router, router_at = router
    picked_rows = folds * capacity
    shapes = [
        jax.ShapeDtypeStruct((local, picked_rows, width), BF16),
        jax.ShapeDtypeStruct((local, picked_rows, ff), F32),
        jax.ShapeDtypeStruct((local, picked_rows, ff), F32),
        jax.ShapeDtypeStruct((local, picked_rows, width), BF16),
        jax.ShapeDtypeStruct((local, picked_rows, LANES), F32),
        jax.ShapeDtypeStruct((folds, local, rows), jnp.int32),
        jax.ShapeDtypeStruct((rows, LANES), F32),
    ] + [jax.ShapeDtypeStruct((rows, width), BF16)] * folds
    out = pl.pallas_call(
        functools.partial(moe_fwd_kernel, folds, local, parts, capacity, routes_at, top),
        out_shape=shapes,
        in_specs=[
            pl.BlockSpec(memory_space=pltpu.SMEM),
            pl.BlockSpec((router.shape[0], LANES), lambda i: (0, router_at)),
        ]
        + [pl.BlockSpec((rows, LANES), lambda i: (0, tile_at))] * folds
        + vmem(folds) + anywhere(3 + len(flat)),
        grid=(1,),
        out_specs=vmem(len(shapes)),
        scratch_shapes=weight_scratch(own, local, parts),
        cost_estimate=cost(local * picked_rows, width, ff, 3),
        compiler_params=pltpu.CompilerParams(vmem_limit_bytes=56 << 20),
    )(scalars, router, *tiles, *blocks, *own, *flat)
    return out[:7], out[7:]


def moe_bwd_call(scalars, kept, blocks, own, flat, folds, local, rows, parts, width, ff, capacity, top, tile_at):
    _, gate_pre, up_pre, made, gate_rows, slots, _ = kept
    picked_rows = folds * capacity
    shapes = [jax.ShapeDtypeStruct((local, picked_rows, width), BF16)] + [
        jax.ShapeDtypeStruct((rows, width + LANES), BF16)
    ] * folds
    out = pl.pallas_call(
        functools.partial(moe_bwd_kernel, folds, local, parts, capacity),
        out_shape=shapes,
        in_specs=[pl.BlockSpec(memory_space=pltpu.SMEM)]
        + vmem(5 + folds) + anywhere(3 + len(flat)),
        out_specs=vmem(len(shapes)),
        scratch_shapes=weight_scratch(own, local, parts)
        + [pltpu.VMEM((local, picked_rows, width), BF16), pltpu.VMEM((local, picked_rows, LANES), F32)],
        cost_estimate=cost(local * picked_rows, width, ff, 3),
        compiler_params=pltpu.CompilerParams(vmem_limit_bytes=56 << 20),
    )(scalars, slots, gate_pre, up_pre, made, gate_rows, *blocks, *own, *flat)
    return out[0], out[1:]


def mm(a, b):
    return jnp.dot(a, b, preferred_element_type=F32)


def mm_nt(a, b):
    return lax.dot_general(a, b, (((1,), (1,)), ((), ())), preferred_element_type=F32)


def mm_shares(a, shares):
    if shares.ndim == 2:
        return mm_nt(a, shares)
    width = shares.shape[2]
    return sum(mm_nt(a[:, j * width : (j + 1) * width], shares[j]) for j in range(shares.shape[0]))


def mm_tn(a, b):
    return lax.dot_general(a, b, (((0,), (0,)), ((), ())), preferred_element_type=F32)


def ein(spec, a, b):
    return jnp.einsum(spec, a, b, preferred_element_type=F32)


def rel_gather(value):
    folds = lax.axis_size(F_AX)
    parts = [value]
    for k in range(1, folds):
        parts.append(lax.ppermute(value, F_AX, [(i, (i + k) % folds) for i in range(folds)]))
    return parts


def rel_scatter(parts):
    folds = lax.axis_size(F_AX)
    total = parts[0].astype(F32)
    for k in range(1, folds):
        got = lax.ppermute(parts[k], F_AX, [(i, (i - k) % folds) for i in range(folds)])
        total = total + got.astype(F32)
    return total


def send_back(parts):
    folds = lax.axis_size(F_AX)
    return [parts[0]] + [
        lax.ppermute(parts[k], F_AX, [(i, (i - k) % folds) for i in range(folds)]) for k in range(1, folds)
    ]


def add_up(parts):
    total = parts[0].astype(F32)
    for part in parts[1:]:
        total = total + part.astype(F32)
    return total


def swap_section(value):
    return lax.ppermute(value, S_AX, [(0, 1), (1, 0)])


def swap_core(value):
    count = lax.axis_size(R_AX)
    return lax.ppermute(value, R_AX, [(i, i ^ 1) for i in range(count)])


def rope_turn(values, cos, sin):
    half = HEAD // 2
    turned = jnp.concatenate([-values[..., half:], values[..., :half]], axis=-1)
    return values * cos + turned * sin


def rope_back(grads, cos, sin):
    half = HEAD // 2
    scaled = grads * sin
    turned = jnp.concatenate([scaled[..., half:], -scaled[..., :half]], axis=-1)
    return grads * cos + turned


def layout(lengths, position):
    bounds = jnp.cumsum(lengths)
    passed = (position[:, None] >= bounds[None, :]).astype(jnp.int32)
    segment = jnp.sum(passed, axis=1)
    start = jnp.sum(passed * lengths[None, :], axis=1)
    return segment, (position - start).astype(F32)


def gated(gate, up):
    return jax.nn.gelu(gate) * up


def attention_in(hidden, gain):
    scale = lax.rsqrt(jnp.mean(hidden * hidden, axis=1, keepdims=True) + EPS)
    normed = hidden * scale
    return scale, normed, (normed * gain.astype(F32)).astype(BF16)


def turn_heads(lin, common, kv_width):
    rows = lin.shape[0]
    q_width = lin.shape[1] - 2 * kv_width
    turned = rope_turn(
        lin[:, : q_width + kv_width].astype(F32).reshape(rows, -1, HEAD), common["cos"], common["sin"]
    ).astype(BF16).reshape(rows, -1)
    kv = jnp.concatenate([turned[:, q_width:], lin[:, q_width + kv_width :].astype(BF16)], axis=1)
    return turned[:, :q_width], kv


def grouped_heads(value, groups):
    rows = value.shape[0]
    return value.reshape(rows, groups, -1, HEAD)


def attend(query, kv_all, allowed, groups):
    keys = kv_all[:, : groups * HEAD].reshape(-1, groups, HEAD)
    values = kv_all[:, groups * HEAD :].reshape(-1, groups, HEAD)
    raw = ein("tgha,sga->ghts", grouped_heads(query, groups), keys) * HEAD ** (-0.5)
    scores = jnp.where(allowed[None, None], raw, MASKED)
    top = jnp.max(scores, axis=3, keepdims=True)
    expo = jnp.exp(scores - top)
    probs = expo / jnp.sum(expo, axis=3, keepdims=True)
    mixed = ein("ghts,sga->tgha", probs.astype(BF16), values)
    return mixed.reshape(query.shape), probs


def attend_back(grad_mixed, mixed, probs, query, kv_all, groups):
    rows = query.shape[0]
    keys = kv_all[:, : groups * HEAD].reshape(-1, groups, HEAD)
    values = kv_all[:, groups * HEAD :].reshape(-1, groups, HEAD)
    grad_grouped = grouped_heads(grad_mixed, groups)
    delta = jnp.sum(
        grad_grouped.astype(F32) * grouped_heads(mixed, groups), axis=3
    )
    delta = jnp.transpose(delta, (1, 2, 0))[..., None]
    grad_probs = ein("tgha,sga->ghts", grad_grouped, values)
    grad_scores = (probs * (grad_probs - delta)).astype(BF16)
    score_scale = HEAD ** (-0.5)
    grad_query = (ein("ghts,sga->tgha", grad_scores, keys) * score_scale).reshape(rows, -1, HEAD)
    grad_key = ein("ghts,tgha->sga", grad_scores, grouped_heads(query, groups)) * score_scale
    grad_value = ein("ghts,tgha->sga", probs.astype(BF16), grad_grouped)
    count = kv_all.shape[0]
    grad_kv = jnp.concatenate(
        [grad_key.reshape(count, -1), grad_value.reshape(count, -1)], axis=1
    ).astype(BF16)
    return grad_query, grad_kv


def moe_forward(router, tiles, routes_at, scalars, experts_w, size, blocks):
    outs, partials = moe_fwd_call(
        scalars, tiles, routes_at, router, blocks, *experts_w, **size
    )
    return partials, outs


def moe_backward(blocks, kept, scalars, experts_w, size, tie, hooks):
    blocks, tied = lax.optimization_barrier((blocks, tie))
    grad_expert, partials = moe_bwd_call(scalars, kept, blocks, *experts_w, **size)
    sent = hooks["rows"](grad_expert)
    summed, sent = lax.optimization_barrier((rel_scatter(partials), sent))
    width = blocks[0].shape[1]
    tail = summed[:, width:]
    half = LANES // 2
    dots = tail[:, :half] + tail[:, half:]
    return summed[:, :width], jnp.pad(dots, ((0, 0), (0, half))), sent, tied


def layer_forward(layer_in, weights, experts_w, common, tiles, routes_at, scalars, tie, projected=None, out_product=None):
    gains, w_qkv, w_out, router = weights
    groups = common["groups"]
    hidden = layer_in.astype(F32)
    scale, normed, attn_in = attention_in(hidden, gains[0])
    lin = mm(attn_in, w_qkv) if projected is None else projected
    lin, tied_lin = lax.optimization_barrier((lin, tie.get("lin", ())))
    query, kv = turn_heads(lin, common, groups * HEAD)
    kv_all, tied_kv = lax.optimization_barrier(
        (jnp.concatenate(rel_gather(kv), axis=0), tie.get("kv", ()))
    )
    mixed, probs = attend(query, kv_all, common["allowed"], groups)
    mixed_low = mixed.astype(BF16)
    more = tie["mixed"](tied_lin, tied_kv, attn_in, mixed_low) if "mixed" in tie else ()
    mixed_low, more = lax.optimization_barrier((mixed_low, more))
    if out_product is None:
        residual = hidden + mm(mixed_low, w_out)
    else:
        residual = hidden + out_product(mixed_low).astype(F32)
    scale_two = lax.rsqrt(jnp.mean(residual * residual, axis=1, keepdims=True) + EPS)
    normed_two = residual * scale_two
    moe_in = (normed_two * gains[1].astype(F32)).astype(BF16)
    if "moe" in tie:
        moe_in, experts_w, more = tie["moe"](moe_in, experts_w, more)
    blocks, tied = lax.optimization_barrier((rel_gather(moe_in), more))
    parts, moe_kept = moe_forward(tie["router"], tiles, routes_at, scalars, experts_w, common["size"], blocks)
    finish = lambda got: (residual + add_up(got)).astype(BF16)
    out = finish(send_back(parts)) if "last" not in tie else (parts, finish)
    kept = dict(
        scale=scale, normed=normed, attn_in=attn_in, query=query, kv=kv,
        kv_all=kv_all, mixed=mixed, probs=probs, mixed_low=mixed_low, scale_two=scale_two,
        normed_two=normed_two, moe_in=moe_in, mix=moe_kept[6], moe=moe_kept,
    )
    return out, kept, experts_w, tied


def layer_backward(grad_low, kept, weights, experts_w, common, scalars, tie, hooks):
    gains, w_qkv, w_out, router = weights
    groups = common["groups"]
    grad_out = grad_low.astype(F32)
    rows = grad_out.shape[0]
    blocks = hooks["blocks"] if "blocks" in hooks else rel_gather(grad_low)
    grad_moe_in, dots, sent, tied = moe_backward(
        blocks, kept["moe"], scalars, experts_w, common["size"], tie, hooks
    )
    mix = kept["mix"]
    grad_logits = mix * (dots - jnp.sum(mix * dots, axis=1, keepdims=True))
    moe_in = kept["moe_in"]
    count = common["experts"]
    high = grad_logits.astype(BF16)
    rest = (grad_logits - high.astype(F32)).astype(BF16)
    both = mm_tn(jnp.concatenate([high[:, :count], rest[:, :count]], axis=1), moe_in)
    grad_router = both[:count] + both[count:]
    grad_moe_in = grad_moe_in + mm_nt(high, router) + mm_nt(rest, router)
    normed_two = kept["normed_two"]
    grad_norm = grad_moe_in * gains[1].astype(F32)
    grad_gain_two = jnp.sum(grad_moe_in * normed_two, axis=0)
    grad_mid = grad_out + kept["scale_two"] * (
        grad_norm - normed_two * jnp.mean(grad_norm * normed_two, axis=1, keepdims=True)
    )
    grad_attn = grad_mid.astype(BF16)
    small = jnp.concatenate([grad_router, grad_gain_two[None]], axis=0).astype(BF16)
    crossed = hooks["attn"](grad_attn, small, sent)
    grad_mixed = mm_shares(grad_attn, w_out).astype(BF16)
    grad_query, grad_kv = attend_back(
        grad_mixed, kept["mixed"], kept["probs"], kept["query"], kept["kv_all"], groups
    )
    grad_kv, crossed = lax.optimization_barrier((grad_kv, crossed))
    later = hooks["later"](sent, crossed)
    own = rel_scatter([grad_kv[k * rows : (k + 1) * rows] for k in range(lax.axis_size(F_AX))])
    own, later = lax.optimization_barrier((own, later))
    cos, sin = common["cos"], common["sin"]
    kv_width = groups * HEAD
    grad_lin = jnp.concatenate(
        [
            rope_back(grad_query, cos, sin).reshape(rows, -1),
            rope_back(own[:, :kv_width].reshape(rows, -1, HEAD), cos, sin).reshape(rows, -1),
            own[:, kv_width:],
        ],
        axis=1,
    ).astype(BF16)
    grad_attn_in = mm_shares(grad_lin, w_qkv)
    normed = kept["normed"]
    grad_norm = grad_attn_in * gains[0].astype(F32)
    grad_in = grad_mid + kept["scale"] * (
        grad_norm - normed * jnp.mean(grad_norm * normed, axis=1, keepdims=True)
    )
    return grad_in.astype(BF16), grad_lin, later, tied


def expert_middle(rows_in, grad_rows, gate_w, up_w, down_w):
    value, slope = gelu_parts(mm(rows_in, gate_w))
    up_pre = mm(rows_in, up_w)
    grad_inner = mm_nt(grad_rows, down_w)
    return (
        (value * up_pre).astype(BF16),
        (grad_inner * up_pre * slope).astype(BF16),
        (grad_inner * value).astype(BF16),
    )


def body(
    tokens, cotangent, seq_lengths, routes, gains, w_query, w_key, w_value, w_out, w_router, w_gate, w_up, w_down
):
    section = lax.axis_index(S_AX)
    is_first = section == 0
    fold_id = lax.axis_index(F_AX)
    replica = lax.axis_index(R_AX)
    core = replica % 2
    flip = (replica // 2) % 2
    folds, replicas = lax.axis_size(F_AX), lax.axis_size(R_AX)
    rows = tokens.shape[2]
    top = routes.shape[4]
    local = w_gate.shape[1]
    expert_count = w_router.shape[2]
    kv_width = w_key.shape[2]
    q_width = w_query.shape[2]
    capacity = rows * top // expert_count

    def own_batch(value):
        return lax.dynamic_index_in_dim(value, section, 0, keepdims=False)

    def swap_xor(value, bit):
        return lax.ppermute(value, R_AX, [(i, i ^ bit) for i in range(replicas)])

    def own_layer(pair):
        return jnp.where(is_first, pair[0], pair[1])

    def other_layer(pair):
        return jnp.where(is_first, pair[1], pair[0])

    def by_section(keep, got):
        return jnp.stack([jnp.where(is_first, keep, got), jnp.where(is_first, got, keep)])

    def both_batches(pair):
        return by_section(own_layer(pair), swap_section(other_layer(pair)))

    split = q_width + 2 * kv_width
    routes_at = HEAD // 4

    def widened(pieces):
        weights_part, routes_part = pieces
        routes_part = jnp.pad(routes_part.astype(BF16), ((0, weights_part.shape[0] - rows), (0, 0)))
        gap = jnp.zeros((weights_part.shape[0], routes_at - weights_part.shape[1]), BF16)
        whole = jnp.concatenate([weights_part, gap, routes_part], axis=1)
        return jnp.pad(whole, ((0, 0), (0, HEAD - whole.shape[1])))

    small = jnp.concatenate([w_router[0], gains[0].T], axis=1)
    my_routes = own_batch(routes[0, :, 0])
    give_routes = lax.dynamic_index_in_dim(routes[0, :, 0], 1 - section, 0, keepdims=False)
    joined = jnp.concatenate([w_query[0], w_key[0], w_value[0]], axis=1)
    depth = joined.shape[0]

    def column_share(value):
        width = value.shape[1] // replicas
        return lax.dynamic_slice_in_dim(value, replica * width, width, 1)

    def stacked_parts(parts):
        whole = jnp.zeros((folds,) + parts[0].shape, parts[0].dtype)
        for k, part in enumerate(parts):
            whole = lax.dynamic_update_index_in_dim(whole, part, (fold_id - k) % folds, 0)
        return whole.reshape((-1,) + parts[0].shape[1:])

    def stacked_rows(value):
        return stacked_parts(rel_gather(value))

    def of_first(value):
        return jnp.where(is_first, value, swap_section(value))

    def share_back(value):
        whole = jnp.zeros(value.shape, value.dtype)
        for bit in range(replicas):
            got = value[bit] if bit == 0 else swap_xor(value[bit], bit)
            whole = lax.dynamic_update_index_in_dim(whole, got, replica ^ bit, 0)
        return jnp.concatenate([whole[j] for j in range(replicas)], axis=1)

    def group_rows(value):
        parts = []
        for bit in range(0, replicas, 2):
            same = value if bit == 0 else swap_xor(value, bit)
            parts += [same, swap_core(same)]
        return parts

    my_tokens = own_batch(tokens[:, 0])
    token_group = jnp.concatenate(group_rows(my_tokens), axis=0)
    head_own = column_share(joined)
    lin_width = head_own.shape[1]
    head_swap = swap_section(jnp.concatenate([head_own, widened((small, give_routes))], axis=1))
    got_routes = head_swap[:rows, lin_width + routes_at : lin_width + routes_at + top].astype(jnp.int32)
    both_routes = jnp.where(
        is_first,
        jnp.concatenate([my_routes, got_routes], axis=1),
        jnp.concatenate([got_routes, my_routes], axis=1),
    )
    tail_cols = jnp.where(is_first, small, head_swap[:, lin_width : lin_width + small.shape[1]])
    head_got = jnp.concatenate(
        [jnp.where(is_first, head_own, head_swap[:, :lin_width]), widened((tail_cols, both_routes))], axis=1
    )
    part_ff = w_gate.shape[3] // 2
    pieces = []
    for part, axis in ((w_gate, 1), (w_up, 1), (w_down, 0)):
        chosen = lax.dynamic_index_in_dim(part[0], flip, 0, keepdims=False)
        pieces.append(lax.dynamic_slice_in_dim(chosen, core * part_ff, part_ff, axis))
    pieces, head_got = lax.optimization_barrier((pieces, head_got))
    crossed_y = [swap_section(pieces[0]), None, None]
    last_grad = own_batch(cotangent[:, 0])
    head_got, last_blocks = lax.optimization_barrier((head_got, rel_gather(last_grad)))
    head_parts, crossed_y[0] = lax.optimization_barrier((rel_gather(head_got), crossed_y[0]))
    head_block = stacked_parts(head_parts)
    tiles = head_parts
    crossed_y[1:] = [swap_section(value) for value in pieces[1:]]
    first = fold_id * local
    numbers = first + (jnp.arange(local, dtype=jnp.int32) ^ flip)
    scalars = [
        jnp.concatenate([jnp.stack([(section == layer).astype(jnp.int32), flip]), numbers]).astype(jnp.int32)
        for layer in range(2)
    ]
    first_tail = head_block[:, lin_width:]
    out_block = of_first(column_share(w_out[0]))
    head_block, out_block = lax.optimization_barrier((head_block, out_block))
    out_block = stacked_rows(out_block)
    group_in = attention_in(token_group.astype(F32), first_tail[:, expert_count])[2]
    first_lin = share_back(
        mm(group_in, head_block[:, :lin_width]).astype(BF16).reshape(replicas, rows, lin_width)
    )

    def first_out(mixed_low):
        group = jnp.concatenate(group_rows(mixed_low), axis=0)
        made = mm(group, out_block).astype(BF16)
        return share_back(made.reshape(replicas, rows, -1))

    shard = jnp.concatenate([joined, jnp.pad(small, ((0, 0), (0, HEAD - small.shape[1]))), w_out[0]], axis=1)
    share = depth // (2 * replicas)
    keep = lax.dynamic_slice_in_dim(shard, (section * replicas + replica) * share, share, 0)
    give = lax.dynamic_slice_in_dim(shard, ((1 - section) * replicas + replica) * share, share, 0)
    give, _ = lax.optimization_barrier((give, head_got))
    got = swap_section(give)

    def whole_weights(layer, keep, got):
        piece = jnp.where(section == layer, keep, got)
        full = lax.all_gather(piece, (F_AX, S_AX, R_AX), axis=0, tiled=True)
        tail = full[:, split : split + LANES]
        held["full"] = full
        return tail[:, expert_count : expert_count + 2].T, full[:, :split], full[:, split + LANES :], tail

    first_w = (
        first_tail[:, expert_count : expert_count + 2].T, None, None, first_tail
    )
    size = dict(
        folds=folds, local=local, rows=rows, parts=2, width=tokens.shape[3], ff=w_gate.shape[3],
        capacity=capacity, top=top, tile_at=lin_width // LANES,
    )

    lengths = own_batch(seq_lengths[:, 0])
    position = fold_id * rows + jnp.arange(rows, dtype=jnp.int32)
    order = (fold_id - jnp.arange(folds)) % folds
    key_pos = (order[:, None] * rows + jnp.arange(rows)[None, :]).reshape(-1).astype(jnp.int32)
    segment, offset = layout(lengths, position)
    key_seg, _ = layout(lengths, key_pos)
    freq = ROPE_BASE ** (-2.0 * jnp.arange(HEAD // 2, dtype=F32) / HEAD)
    angles = offset[:, None] * freq
    angles = jnp.concatenate([angles, angles], axis=1)[:, None, :]
    common = dict(
        cos=jnp.cos(angles), sin=jnp.sin(angles), groups=kv_width // HEAD, size=size,
        experts=expert_count,
        allowed=(segment[:, None] == key_seg[None, :]) & (key_pos[None, :] <= position[:, None]),
    )

    def first_mixed(tied_lin, tied, attn_in, mixed_low):
        gate_x, up_y = tied
        held["second"] = whole_weights(1, *tied_lin)
        return (crossed_y[0], up_y), (gate_x,)

    def first_moe(moe_in, own, more):
        same, cross = more
        same, cross, moe_in = lax.optimization_barrier(((*same, crossed_y[2]), cross, moe_in))
        cross = [*cross, swap_xor(same[1], 2), swap_xor(same[2], 2)]
        flat = []
        for one, two in zip(same, cross):
            flat += [one, swap_core(one), two, swap_core(two)]
        return moe_in, (own, flat), ()

    held = {}
    first_value, first_kept, experts_w, _ = layer_forward(
        my_tokens, first_w, (w_gate[0], w_up[0], w_down[0]), common, tiles, routes_at, scalars[0],
        dict(router=(head_block, lin_width // LANES), lin=(keep, got), kv=(swap_xor(crossed_y[0], 2), crossed_y[1]), mixed=first_mixed, moe=first_moe),
        first_lin, first_out,
    )
    head_share, out_share, _ = lax.optimization_barrier(
        (head_block[:, :lin_width], out_block, first_kept["moe"][1])
    )
    weights_first = (
        first_w[0], lax.all_gather(head_share, R_AX, axis=0), lax.all_gather(out_share, R_AX, axis=0), first_tail
    )

    second_w = held["second"]

    def left_pair(attn_in, mixed_low):
        pair = (
            jnp.concatenate([first_kept["attn_in"], first_kept["mixed_low"]], axis=1),
            jnp.concatenate([attn_in, mixed_low], axis=1),
        )
        return own_layer(pair), swap_section(other_layer(pair))

    second_value, second_kept, _, tied = layer_forward(
        first_value, second_w, experts_w, common, tiles, routes_at + top, scalars[1],
        dict(
            mixed=lambda one, two, attn_in, mixed_low: (attn_in, mixed_low),
            moe=lambda moe_in, own, more: (moe_in, own, (left_pair(*more), weights_first)),
            last=True, router=(held["full"], split // LANES),
        ),
    )
    left_rows, weights_first = tied
    second_parts, second_finish = second_value
    left_rows = jnp.concatenate(left_rows, axis=0)
    kept, weights = [first_kept, second_kept], [weights_first, second_w]

    half = local // 2

    def chip_rows(pair):
        chip = []
        for value in pair:
            keep = lax.dynamic_slice_in_dim(value, (core ^ flip) * half, half, 0)
            give = lax.dynamic_slice_in_dim(value, (1 - (core ^ flip)) * half, half, 0)
            got = swap_core(give)
            chip.append(jnp.concatenate([keep, got], axis=1))
        return chip

    chips = replicas // 2

    def all_x(value):
        return [swap_xor(value, bit) for bit in range(2, replicas, 2)]

    def by_order(value, others):
        whole = jnp.zeros((chips,) + value.shape, value.dtype)
        for at, part in enumerate([value] + others):
            whole = lax.dynamic_update_index_in_dim(whole, part, (replica // 2) ^ at, 0)
        return whole

    def flat_rows(whole):
        return jnp.moveaxis(whole, 1, 0).reshape(half, -1, whole.shape[-1])

    x_chip = chip_rows([state["moe"][0] for state in kept])
    x_mine, x_give = own_layer(x_chip), other_layer(x_chip)
    def both_rows(pair):
        return jnp.concatenate([own_layer(pair), swap_section(other_layer(pair))], axis=0)

    def own_columns(value):
        width = value.shape[1] // replicas
        parts = []
        for bit in range(replicas):
            piece = lax.dynamic_slice_in_dim(value, (replica ^ bit) * width, width, 1)
            parts.append(piece if bit == 0 else swap_xor(piece, bit))
        return jnp.stack(parts)

    def fold_sum(left, right, extra):
        total = mm_tn(left, right).astype(BF16)
        if extra is not None:
            total = total.reshape(folds, -1, total.shape[1])
            total = jnp.concatenate([total, extra], axis=1).reshape(-1, total.shape[2])
        return total

    def late_part(total, tie):
        if tie == ():
            mine = lax.psum_scatter(total, F_AX, scatter_dimension=0, tiled=True)
        else:
            step = total.shape[0] // folds
            mine = rel_scatter(
                [
                    lax.dynamic_slice_in_dim(total, ((fold_id - k) % folds) * step, step, 0)
                    for k in range(folds)
                ]
            ).astype(BF16)
            mine, tie = lax.optimization_barrier((mine, tie))
        whole = jnp.zeros((replicas,) + mine.shape, BF16)
        for bit, part in enumerate(group_rows(mine)):
            whole = lax.dynamic_update_index_in_dim(whole, part, replica ^ bit, 0)
        return whole, tie

    def side_by_side(value):
        return jnp.concatenate([value[j].astype(F32) for j in range(replicas)], axis=1)

    left_whole = group_rows(left_rows)
    model = tokens.shape[3]
    piece = model // (folds * replicas)
    count = expert_count + 1
    tall = -(-count // 16) * 16

    def with_small(grad_attn, small):
        value = small.reshape(count, folds, replicas, piece)
        value = jnp.transpose(value, (0, 2, 1, 3)).reshape(count, model)
        return jnp.concatenate([grad_attn, jnp.pad(value, ((0, tall - count), (0, 0)))], axis=0)

    def last_rows(grad_expert):
        held["rows"] = chip_rows([grad_expert])[0]
        return left_whole, stacked_parts(second_parts)

    def last_attn(grad_attn, small, sent):
        held["attn"] = with_small(grad_attn, small)
        return swap_section(x_give), sent[1]

    def first_rows(grad_expert):
        chip = (chip_rows([grad_expert])[0], held["rows"])
        mine = own_layer(chip)
        return mine, all_x(mine), swap_section(other_layer(chip)), x_own, second_stack

    def first_attn(grad_attn, small, sent):
        *sent, stack = sent
        held["second_sum"] = lax.psum_scatter(stack, F_AX, scatter_dimension=0, tiled=True)
        return both_rows((with_small(grad_attn, small), held["attn"])), sent

    def first_later(sent, crossed):
        right_out, (mine, mine_x, got, x_own) = crossed
        g_own = by_order(mine, mine_x)
        return x_own, g_own, [expert_middle(x_own[i], flat_rows(g_own)[i], *[w[i] for w in mine_w]) for i in range(half)], got, own_columns(right_out)

    grads, grad_lin = [None, None], [None, None]
    grads[1], grad_lin[1], ((left_whole, _), (x_got, second_stack), x_mine_x), _ = layer_backward(
        last_grad, kept[1], weights[1], experts_w, common, scalars[1], (),
        dict(rows=last_rows, attn=last_attn, later=lambda sent, crossed: (sent, crossed, all_x(x_mine)), blocks=last_blocks),
    )
    x_own = flat_rows(by_order(x_mine, x_mine_x))
    x_own = [x_own[i] for i in range(half)]
    mine_w = [lax.dynamic_slice_in_dim(part[0], core * half, half, 0) for part in (w_gate, w_up, w_down)]
    grads[0], grad_lin[0], later, x_got_x = layer_backward(
        grads[1], kept[0], weights[0], experts_w, common, scalars[0], all_x(x_got),
        dict(rows=first_rows, attn=first_attn, later=first_later),
    )
    x_own, g_own, middle_own, got, right_out = later
    left_whole = jnp.concatenate(left_whole, axis=0)
    right_out = right_out.reshape(replicas, 2, rows + tall, -1)
    extra = jnp.sum(right_out[:, :, rows:].astype(F32), axis=(0, 1)).reshape(tall, folds, piece)
    extra = jnp.pad(
        jnp.transpose(extra, (1, 0, 2)), ((0, 0), (0, 0), (0, right_out.shape[3] - piece))
    ).astype(BF16)
    right_out = right_out[:, :, :rows].reshape(-1, right_out.shape[3])
    out_shard, _ = late_part(fold_sum(left_whole[:, model:], right_out, extra), ())
    lin_rows, second_sum = lax.optimization_barrier((both_rows(grad_lin), held["second_sum"]))
    right, got = lax.optimization_barrier((own_columns(lin_rows), got))
    got_x = all_x(got)
    g_got, x_got = by_order(got, got_x), by_order(x_got, x_got_x)
    shard = fold_sum(left_whole[:, :model], right.reshape(-1, right.shape[2]), None)
    shard, (middle_own, x_own, first_value, grads) = lax.optimization_barrier(
        (shard, (middle_own, x_own, first_value, grads))
    )
    x_got = [flat_rows(x_got)[i] for i in range(half)]
    g_own, g_got = [[flat_rows(value)[i] for i in range(half)] for value in (g_own, g_got)]
    middle_got = [expert_middle(x_got[i], g_got[i], *[w[i] for w in mine_w]) for i in range(half)]

    shard, middle_got = late_part(shard, middle_got)
    made = []
    for i in range(half):
        inner, gate, up = zip(middle_own[i], middle_got[i])
        made.append(
            (
                (mm_tn(x_own[i], gate[0]) + mm_tn(x_got[i], gate[1])).astype(BF16),
                (mm_tn(x_own[i], up[0]) + mm_tn(x_got[i], up[1])).astype(BF16),
                (mm_tn(inner[0], g_own[i]) + mm_tn(inner[1], g_got[i])).astype(BF16),
            )
        )
    made, second_sum = lax.optimization_barrier((made, second_sum))
    outs = [first_value, second_finish([second_sum])]
    small = side_by_side(out_shard[:, depth:, :piece])
    out_shard = side_by_side(out_shard[:, :depth])
    shard = side_by_side(shard)
    gain_one = jnp.sum(shard * joined.astype(F32), axis=1) / gains[0, 0].astype(F32)
    expert_out = []
    for slot in range(3):
        keep = jnp.stack([one[slot] for one in made])
        got = swap_core(keep)
        both = jnp.concatenate(
            [jnp.where(core == 0, keep, got), jnp.where(core == 0, got, keep)], axis=0
        )
        expert_out.append(both.astype(F32)[None])
    layer_outputs = both_batches(outs)
    input_grads = both_batches(grads)
    return (
        layer_outputs[None, :, None],
        input_grads[None, :, None],
        jnp.stack([gain_one, small[expert_count]])[None],
        shard[None, :, :q_width],
        shard[None, :, q_width : q_width + kv_width],
        shard[None, :, q_width + kv_width : split],
        out_shard[None],
        small[:expert_count].T[None],
        expert_out[0],
        expert_out[1],
        expert_out[2],
    )


def solution(mesh):
    acts = P(None, R_AX, F_AX, None)
    rows = P(S_AX, F_AX, None)
    expert = P(S_AX, F_AX, None, None)
    stacked = P(S_AX, None, R_AX, F_AX, None)
    gain = P(S_AX, None, F_AX)
    return jax.shard_map(
        body,
        mesh=mesh,
        in_specs=(acts, acts, P(None, R_AX, None), stacked, gain)
        + (rows,) * 5
        + (expert,) * 3,
        out_specs=(stacked, stacked, gain) + (rows,) * 5 + (expert,) * 3,
        check_vma=False,
    )
```

```python
import functools

import jax
import jax.numpy as jnp
from jax import lax
from jax.experimental import pallas as pl
from jax.experimental.pallas import tpu as pltpu
from jax.sharding import PartitionSpec as P

HEAD = 128
ROPE_BASE = 1000000.0
EPS = 1e-06
MASKED = -1e30
F32 = jnp.float32
BF16 = jnp.bfloat16
S_AX, F_AX, R_AX = "section", "fsdp", "replica"
HIGHEST = lax.Precision.HIGHEST
LANES = 128
GELU_C = 0.7978845608028654
GELU_A = 0.044715


def dot(a, b):
    return lax.dot_general(a, b, (((1,), (0,)), ((), ())), preferred_element_type=F32)


def dot_nt(a, b):
    return lax.dot_general(a, b, (((1,), (1,)), ((), ())), preferred_element_type=F32)


def dot_tn(a, b):
    return lax.dot_general(a, b, (((0,), (0,)), ((), ())), preferred_element_type=F32)


def gelu_parts(x):
    t = jnp.tanh(GELU_C * (x + GELU_A * x * x * x))
    value = 0.5 * x * (1.0 + t)
    slope = 0.5 * (1.0 + t) + 0.5 * x * (1.0 - t * t) * GELU_C * (1.0 + 3.0 * GELU_A * x * x)
    return value, slope


def lane_is(shape, number):
    return lax.broadcasted_iota(jnp.int32, shape, 1) == number


def masked_mix(logits, mask):
    kept = jnp.where(mask > 0.0, logits, -1e30)
    expo = jnp.exp(kept - jnp.max(kept, axis=1, keepdims=True)) * mask
    return expo / jnp.sum(expo, axis=1, keepdims=True)


def one_hot(slots_ref, block, step, capacity):
    rows = slots_ref.shape[2]
    place = lax.broadcasted_iota(jnp.int32, (capacity, rows), 0)
    return place == slots_ref[block, step : step + 1, :]


def route_mask(tile, at, top):
    lane = lax.broadcasted_iota(jnp.int32, tile.shape, 1).astype(F32)
    named = tile.astype(F32)
    hit = lane == named[:, at : at + 1]
    for k in range(1, top):
        hit = hit | (lane == named[:, at + k : at + k + 1])
    return jnp.where(hit, 1.0, 0.0)


def weight_copies(scalars, own, pieces, buffers, sems):
    own_g, own_u, own_d = own
    parts = len(pieces[0][0])
    ff = own_g.shape[2] // parts
    is_own, flip = scalars[0], scalars[1]
    waits = {}
    for step in range(len(pieces[0])):
        for part in range(parts):
            expert = step ^ flip
            cols = pl.ds(part * ff, ff)
            sources = (own_g.at[expert, :, cols], own_u.at[expert, :, cols], own_d.at[expert, cols, :])
            for kind in range(3):
                target = buffers[kind].at[step, part]
                sem = sems.at[kind, step, part]

                @pl.when(is_own == 1)
                def _(source=sources[kind], target=target, sem=sem):
                    pltpu.make_async_copy(source, target, sem).start()

                @pl.when(is_own == 0)
                def _(source=pieces[kind][step][part], target=target, sem=sem):
                    pltpu.make_async_copy(source, target, sem).start()

                waits[kind, step, part] = pltpu.make_async_copy(
                    pieces[kind][step][part], target, sem
                )
    return waits


def split_refs(refs, counts):
    out, at = [], 0
    for count in counts:
        out.append(refs[at : at + count])
        at += count
    return out


def moe_fwd_kernel(folds, local, parts, capacity, routes_at, top, *refs):
    (scalars, router), tiles, blocks, own, flat, outs, partials, scratch = split_refs(
        refs, (2, folds, folds, 3, 3 * local * parts, 7, folds, 4)
    )
    scalars_ref = scalars
    picked_ref, gate_ref, up_ref, made_ref, grows_ref, slots, mix_ref = outs
    buf_g, buf_u, buf_d, sems = scratch
    pieces = [
        [[flat[(kind * local + step) * parts + part] for part in range(parts)] for step in range(local)]
        for kind in range(3)
    ]
    waits = weight_copies(scalars_ref, own, pieces, (buf_g, buf_u, buf_d), sems)
    rows = blocks[0].shape[0]
    width = blocks[0].shape[1]
    ff = buf_g.shape[3]
    square = (rows, rows)
    earlier = jnp.where(
        lax.broadcasted_iota(jnp.int32, square, 0) < lax.broadcasted_iota(jnp.int32, square, 1), 1.0, 0.0
    ).astype(BF16)
    same = jnp.where(
        lax.broadcasted_iota(jnp.int32, square, 0) == lax.broadcasted_iota(jnp.int32, square, 1), 1.0, 0.0
    ).astype(BF16)
    for k in range(folds):
        mask = route_mask(tiles[k][...], routes_at, top)
        mix = masked_mix(dot(blocks[k][...], router[...]), mask)
        if k == 0:
            mix_ref[...] = mix
        low = mask.astype(BF16)
        rank = dot_tn(low, earlier)
        named = dot_tn(low, same)
        place = jnp.where(named > 0.5, rank, -1.0)
        number = lax.broadcasted_iota(jnp.int32, place.shape, 0)
        for step in range(local):
            row = jnp.sum(jnp.where(number == scalars_ref[2 + step], place, 0.0), axis=0, keepdims=True)
            slots[k, step : step + 1, :] = row.astype(jnp.int32)
        for step in range(local):
            pick = one_hot(slots, k, step, capacity)
            at = pl.ds(k * capacity, capacity)
            picked_ref[step, at, :] = dot(
                jnp.where(pick, 1.0, 0.0).astype(BF16), blocks[k][...]
            ).astype(BF16)
            grows_ref[step, at, :] = lax.dot_general(
                jnp.where(pick, 1.0, 0.0), mix, (((1,), (0,)), ((), ())),
                precision=HIGHEST, preferred_element_type=F32,
            )
    for step in range(local):
        for part in range(parts):
            for kind in range(3):
                waits[kind, step, part].wait()
            cols = pl.ds(part * ff, ff)
            x = picked_ref[step]
            gate = dot(x, buf_g[step, part])
            up = dot(x, buf_u[step, part])
            gate_ref[step, :, cols] = gate
            up_ref[step, :, cols] = up
            inner = (gelu_parts(gate)[0] * up).astype(BF16)
            term = dot(inner, buf_d[step, part])
            made = term if part == 0 else made + term
        made_ref[step] = made.astype(BF16)
    for k in range(folds):
        at = pl.ds(k * capacity, capacity)
        picks, weighted = [], []
        for step in range(local):
            gates = grows_ref[step, at, :]
            own_lane = lane_is(gates.shape, scalars_ref[2 + step])
            factor = jnp.sum(jnp.where(own_lane, gates, 0.0), axis=1, keepdims=True)
            picks.append(jnp.where(one_hot(slots, k, step, capacity), 1.0, 0.0).astype(BF16))
            weighted.append((made_ref[step, at, :].astype(F32) * factor).astype(BF16))
        partials[k][...] = dot_tn(
            jnp.concatenate(picks, axis=0), jnp.concatenate(weighted, axis=0)
        ).astype(BF16)


def moe_bwd_kernel(folds, local, parts, capacity, *refs):
    (scalars, slots, gate_ref, up_ref, made_ref, grows_ref), blocks, own, flat, (ge_ref,), partials, scratch = split_refs(
        refs, (6, folds, 3, 3 * local * parts, 1, folds, 6)
    )
    buf_g, buf_u, buf_d, sems, dx_ref, dots_ref = scratch
    pieces = [
        [[flat[(kind * local + step) * parts + part] for part in range(parts)] for step in range(local)]
        for kind in range(3)
    ]
    waits = weight_copies(scalars, own, pieces, (buf_g, buf_u, buf_d), sems)
    ff = buf_g.shape[3]
    for step in range(local):
        for k in range(folds):
            at = pl.ds(k * capacity, capacity)
            pick = jnp.where(one_hot(slots, k, step, capacity), 1.0, 0.0).astype(BF16)
            dout = dot(pick, blocks[k][...])
            gates = grows_ref[step, at, :]
            own_lane = lane_is(gates.shape, scalars[2 + step])
            factor = jnp.sum(jnp.where(own_lane, gates, 0.0), axis=1, keepdims=True)
            value = jnp.sum(dout * made_ref[step, at, :].astype(F32), axis=1, keepdims=True)
            lane = lax.broadcasted_iota(jnp.int32, gates.shape, 1)
            number = scalars[2 + step]
            dots_ref[step, at, :] = jnp.where(
                (lane == number) | (lane == number + LANES // 2), value, 0.0
            )
            ge_ref[step, at, :] = (dout * factor).astype(BF16)
    for step in range(local):
        ge = ge_ref[step]
        for part in range(parts):
            for kind in range(3):
                waits[kind, step, part].wait()
            cols = pl.ds(part * ff, ff)
            grad_inner = dot_nt(ge, buf_d[step, part])
            gate = gate_ref[step, :, cols]
            up = up_ref[step, :, cols]
            value, slope = gelu_parts(gate)
            grad_gate = (grad_inner * up * slope).astype(BF16)
            grad_up = (grad_inner * value).astype(BF16)
            term = dot_nt(grad_gate, buf_g[step, part]) + dot_nt(grad_up, buf_u[step, part])
            total = term if part == 0 else total + term
        dx_ref[step] = total.astype(BF16)
    for k in range(folds):
        at = pl.ds(k * capacity, capacity)
        hot = [one_hot(slots, k, step, capacity) for step in range(local)]
        picks = jnp.concatenate([jnp.where(one, 1.0, 0.0) for one in hot], axis=0)
        width = ge_ref.shape[2]
        partials[k][:, :width] = dot_tn(
            picks.astype(BF16), jnp.concatenate([dx_ref[step, at, :] for step in range(local)], axis=0)
        ).astype(BF16)
        dots = lax.dot_general(
            picks, jnp.concatenate([dots_ref[step, at, :] for step in range(local)], axis=0),
            (((0,), (0,)), ((), ())), precision=HIGHEST, preferred_element_type=F32,
        )
        high = dots.astype(BF16).astype(F32)
        lane = lax.broadcasted_iota(jnp.int32, dots.shape, 1)
        partials[k][:, width:] = jnp.where(lane < LANES // 2, high, dots - high).astype(BF16)


def vmem(count):
    return [pl.BlockSpec(memory_space=pltpu.VMEM)] * count


def anywhere(count):
    return [pl.BlockSpec(memory_space=pl.ANY)] * count


def weight_scratch(own, local, parts):
    width, ff = own[0].shape[1], own[0].shape[2] // parts
    return [
        pltpu.VMEM((local, parts, width, ff), BF16),
        pltpu.VMEM((local, parts, width, ff), BF16),
        pltpu.VMEM((local, parts, ff, width), BF16),
        pltpu.SemaphoreType.DMA((3, local, parts)),
    ]


def cost(rows, width, ff, products):
    return pl.CostEstimate(
        flops=2 * rows * width * ff * products, bytes_accessed=2 * 3 * width * ff * 2 + 8 * rows * width,
        transcendentals=rows * ff,
    )


def moe_fwd_call(
    scalars, tiles, routes_at, router, blocks, own, flat, folds, local, rows, parts, width, ff, capacity, top, tile_at
):
    router, router_at = router
    picked_rows = folds * capacity
    shapes = [
        jax.ShapeDtypeStruct((local, picked_rows, width), BF16),
        jax.ShapeDtypeStruct((local, picked_rows, ff), F32),
        jax.ShapeDtypeStruct((local, picked_rows, ff), F32),
        jax.ShapeDtypeStruct((local, picked_rows, width), BF16),
        jax.ShapeDtypeStruct((local, picked_rows, LANES), F32),
        jax.ShapeDtypeStruct((folds, local, rows), jnp.int32),
        jax.ShapeDtypeStruct((rows, LANES), F32),
    ] + [jax.ShapeDtypeStruct((rows, width), BF16)] * folds
    out = pl.pallas_call(
        functools.partial(moe_fwd_kernel, folds, local, parts, capacity, routes_at, top),
        out_shape=shapes,
        in_specs=[
            pl.BlockSpec(memory_space=pltpu.SMEM),
            pl.BlockSpec((router.shape[0], LANES), lambda i: (0, router_at)),
        ]
        + [pl.BlockSpec((rows, LANES), lambda i: (0, tile_at))] * folds
        + vmem(folds) + anywhere(3 + len(flat)),
        grid=(1,),
        out_specs=vmem(len(shapes)),
        scratch_shapes=weight_scratch(own, local, parts),
        cost_estimate=cost(local * picked_rows, width, ff, 3),
        compiler_params=pltpu.CompilerParams(vmem_limit_bytes=56 << 20),
    )(scalars, router, *tiles, *blocks, *own, *flat)
    return out[:7], out[7:]


def moe_bwd_call(scalars, kept, blocks, own, flat, folds, local, rows, parts, width, ff, capacity, top, tile_at):
    _, gate_pre, up_pre, made, gate_rows, slots, _ = kept
    picked_rows = folds * capacity
    shapes = [jax.ShapeDtypeStruct((local, picked_rows, width), BF16)] + [
        jax.ShapeDtypeStruct((rows, width + LANES), BF16)
    ] * folds
    out = pl.pallas_call(
        functools.partial(moe_bwd_kernel, folds, local, parts, capacity),
        out_shape=shapes,
        in_specs=[pl.BlockSpec(memory_space=pltpu.SMEM)]
        + vmem(5 + folds) + anywhere(3 + len(flat)),
        out_specs=vmem(len(shapes)),
        scratch_shapes=weight_scratch(own, local, parts)
        + [pltpu.VMEM((local, picked_rows, width), BF16), pltpu.VMEM((local, picked_rows, LANES), F32)],
        cost_estimate=cost(local * picked_rows, width, ff, 3),
        compiler_params=pltpu.CompilerParams(vmem_limit_bytes=56 << 20),
    )(scalars, slots, gate_pre, up_pre, made, gate_rows, *blocks, *own, *flat)
    return out[0], out[1:]


def mm(a, b):
    return jnp.dot(a, b, preferred_element_type=F32)


def mm_nt(a, b):
    return lax.dot_general(a, b, (((1,), (1,)), ((), ())), preferred_element_type=F32)


def mm_shares(a, shares):
    if shares.ndim == 2:
        return mm_nt(a, shares)
    width = shares.shape[2]
    return sum(mm_nt(a[:, j * width : (j + 1) * width], shares[j]) for j in range(shares.shape[0]))


def mm_tn(a, b):
    return lax.dot_general(a, b, (((0,), (0,)), ((), ())), preferred_element_type=F32)


def ein(spec, a, b):
    return jnp.einsum(spec, a, b, preferred_element_type=F32)


def rel_gather(value):
    folds = lax.axis_size(F_AX)
    parts = [value]
    for k in range(1, folds):
        parts.append(lax.ppermute(value, F_AX, [(i, (i + k) % folds) for i in range(folds)]))
    return parts


def rel_scatter(parts):
    folds = lax.axis_size(F_AX)
    total = parts[0].astype(F32)
    for k in range(1, folds):
        got = lax.ppermute(parts[k], F_AX, [(i, (i - k) % folds) for i in range(folds)])
        total = total + got.astype(F32)
    return total


def send_back(parts):
    folds = lax.axis_size(F_AX)
    return [parts[0]] + [
        lax.ppermute(parts[k], F_AX, [(i, (i - k) % folds) for i in range(folds)]) for k in range(1, folds)
    ]


def add_up(parts):
    total = parts[0].astype(F32)
    for part in parts[1:]:
        total = total + part.astype(F32)
    return total


def swap_section(value):
    return lax.ppermute(value, S_AX, [(0, 1), (1, 0)])


def swap_core(value):
    count = lax.axis_size(R_AX)
    return lax.ppermute(value, R_AX, [(i, i ^ 1) for i in range(count)])


def rope_turn(values, cos, sin):
    half = HEAD // 2
    turned = jnp.concatenate([-values[..., half:], values[..., :half]], axis=-1)
    return values * cos + turned * sin


def rope_back(grads, cos, sin):
    half = HEAD // 2
    scaled = grads * sin
    turned = jnp.concatenate([scaled[..., half:], -scaled[..., :half]], axis=-1)
    return grads * cos + turned


def layout(lengths, position):
    bounds = jnp.cumsum(lengths)
    passed = (position[:, None] >= bounds[None, :]).astype(jnp.int32)
    segment = jnp.sum(passed, axis=1)
    start = jnp.sum(passed * lengths[None, :], axis=1)
    return segment, (position - start).astype(F32)


def gated(gate, up):
    return jax.nn.gelu(gate) * up


def attention_in(hidden, gain):
    scale = lax.rsqrt(jnp.mean(hidden * hidden, axis=1, keepdims=True) + EPS)
    normed = hidden * scale
    return scale, normed, (normed * gain.astype(F32)).astype(BF16)


def turn_heads(lin, common, kv_width):
    rows = lin.shape[0]
    q_width = lin.shape[1] - 2 * kv_width
    turned = rope_turn(
        lin[:, : q_width + kv_width].astype(F32).reshape(rows, -1, HEAD), common["cos"], common["sin"]
    ).astype(BF16).reshape(rows, -1)
    kv = jnp.concatenate([turned[:, q_width:], lin[:, q_width + kv_width :].astype(BF16)], axis=1)
    return turned[:, :q_width], kv


def grouped_heads(value, groups):
    rows = value.shape[0]
    return value.reshape(rows, groups, -1, HEAD)


def attend(query, kv_all, allowed, groups):
    keys = kv_all[:, : groups * HEAD].reshape(-1, groups, HEAD)
    values = kv_all[:, groups * HEAD :].reshape(-1, groups, HEAD)
    raw = ein("tgha,sga->ghts", grouped_heads(query, groups), keys) * HEAD ** (-0.5)
    scores = jnp.where(allowed[None, None], raw, MASKED)
    top = jnp.max(scores, axis=3, keepdims=True)
    expo = jnp.exp(scores - top)
    probs = expo / jnp.sum(expo, axis=3, keepdims=True)
    mixed = ein("ghts,sga->tgha", probs.astype(BF16), values)
    return mixed.reshape(query.shape), probs


def attend_back(grad_mixed, mixed, probs, query, kv_all, groups):
    rows = query.shape[0]
    keys = kv_all[:, : groups * HEAD].reshape(-1, groups, HEAD)
    values = kv_all[:, groups * HEAD :].reshape(-1, groups, HEAD)
    grad_grouped = grouped_heads(grad_mixed, groups)
    delta = jnp.sum(
        grad_grouped.astype(F32) * grouped_heads(mixed, groups), axis=3
    )
    delta = jnp.transpose(delta, (1, 2, 0))[..., None]
    grad_probs = ein("tgha,sga->ghts", grad_grouped, values)
    grad_scores = (probs * (grad_probs - delta)).astype(BF16)
    score_scale = HEAD ** (-0.5)
    grad_query = (ein("ghts,sga->tgha", grad_scores, keys) * score_scale).reshape(rows, -1, HEAD)
    grad_key = ein("ghts,tgha->sga", grad_scores, grouped_heads(query, groups)) * score_scale
    grad_value = ein("ghts,tgha->sga", probs.astype(BF16), grad_grouped)
    count = kv_all.shape[0]
    grad_kv = jnp.concatenate(
        [grad_key.reshape(count, -1), grad_value.reshape(count, -1)], axis=1
    ).astype(BF16)
    return grad_query, grad_kv


def moe_forward(router, tiles, routes_at, scalars, experts_w, size, blocks):
    outs, partials = moe_fwd_call(
        scalars, tiles, routes_at, router, blocks, *experts_w, **size
    )
    return partials, outs


def moe_backward(blocks, kept, scalars, experts_w, size, tie, hooks):
    blocks, tied = lax.optimization_barrier((blocks, tie))
    grad_expert, partials = moe_bwd_call(scalars, kept, blocks, *experts_w, **size)
    sent = hooks["rows"](grad_expert)
    summed, sent = lax.optimization_barrier((rel_scatter(partials), sent))
    width = blocks[0].shape[1]
    tail = summed[:, width:]
    half = LANES // 2
    dots = tail[:, :half] + tail[:, half:]
    return summed[:, :width], jnp.pad(dots, ((0, 0), (0, half))), sent, tied


def layer_forward(layer_in, weights, experts_w, common, tiles, routes_at, scalars, tie, projected=None, out_product=None):
    gains, w_qkv, w_out, router = weights
    groups = common["groups"]
    hidden = layer_in.astype(F32)
    scale, normed, attn_in = attention_in(hidden, gains[0])
    lin = mm(attn_in, w_qkv) if projected is None else projected
    lin, tied_lin = lax.optimization_barrier((lin, tie.get("lin", ())))
    query, kv = turn_heads(lin, common, groups * HEAD)
    kv_all, tied_kv = lax.optimization_barrier(
        (jnp.concatenate(rel_gather(kv), axis=0), tie.get("kv", ()))
    )
    mixed, probs = attend(query, kv_all, common["allowed"], groups)
    mixed_low = mixed.astype(BF16)
    more = tie["mixed"](tied_lin, tied_kv, attn_in, mixed_low) if "mixed" in tie else ()
    mixed_low, more = lax.optimization_barrier((mixed_low, more))
    if out_product is None:
        residual = hidden + mm(mixed_low, w_out)
    else:
        residual = hidden + out_product(mixed_low).astype(F32)
    scale_two = lax.rsqrt(jnp.mean(residual * residual, axis=1, keepdims=True) + EPS)
    normed_two = residual * scale_two
    moe_in = (normed_two * gains[1].astype(F32)).astype(BF16)
    if "moe" in tie:
        moe_in, experts_w, more = tie["moe"](moe_in, experts_w, more)
    blocks, tied = lax.optimization_barrier((rel_gather(moe_in), more))
    parts, moe_kept = moe_forward(tie["router"], tiles, routes_at, scalars, experts_w, common["size"], blocks)
    finish = lambda got: (residual + add_up(got)).astype(BF16)
    out = finish(send_back(parts)) if "last" not in tie else (parts, finish)
    kept = dict(
        scale=scale, normed=normed, attn_in=attn_in, query=query, kv=kv,
        kv_all=kv_all, mixed=mixed, probs=probs, mixed_low=mixed_low, scale_two=scale_two,
        normed_two=normed_two, moe_in=moe_in, mix=moe_kept[6], moe=moe_kept,
    )
    return out, kept, experts_w, tied


def layer_backward(grad_low, kept, weights, experts_w, common, scalars, tie, hooks):
    gains, w_qkv, w_out, router = weights
    groups = common["groups"]
    grad_out = grad_low.astype(F32)
    rows = grad_out.shape[0]
    blocks = hooks["blocks"] if "blocks" in hooks else rel_gather(grad_low)
    grad_moe_in, dots, sent, tied = moe_backward(
        blocks, kept["moe"], scalars, experts_w, common["size"], tie, hooks
    )
    mix = kept["mix"]
    grad_logits = mix * (dots - jnp.sum(mix * dots, axis=1, keepdims=True))
    moe_in = kept["moe_in"]
    count = common["experts"]
    high = grad_logits.astype(BF16)
    rest = (grad_logits - high.astype(F32)).astype(BF16)
    both = mm_tn(jnp.concatenate([high[:, :count], rest[:, :count]], axis=1), moe_in)
    grad_router = both[:count] + both[count:]
    grad_moe_in = grad_moe_in + mm_nt(high, router) + mm_nt(rest, router)
    normed_two = kept["normed_two"]
    grad_norm = grad_moe_in * gains[1].astype(F32)
    grad_gain_two = jnp.sum(grad_moe_in * normed_two, axis=0)
    grad_mid = grad_out + kept["scale_two"] * (
        grad_norm - normed_two * jnp.mean(grad_norm * normed_two, axis=1, keepdims=True)
    )
    grad_attn = grad_mid.astype(BF16)
    small = jnp.concatenate([grad_router, grad_gain_two[None]], axis=0).astype(BF16)
    crossed = hooks["attn"](grad_attn, small, sent)
    grad_mixed = mm_shares(grad_attn, w_out).astype(BF16)
    grad_query, grad_kv = attend_back(
        grad_mixed, kept["mixed"], kept["probs"], kept["query"], kept["kv_all"], groups
    )
    grad_kv, crossed = lax.optimization_barrier((grad_kv, crossed))
    later = hooks["later"](sent, crossed)
    own = rel_scatter([grad_kv[k * rows : (k + 1) * rows] for k in range(lax.axis_size(F_AX))])
    own, later = lax.optimization_barrier((own, later))
    cos, sin = common["cos"], common["sin"]
    kv_width = groups * HEAD
    grad_lin = jnp.concatenate(
        [
            rope_back(grad_query, cos, sin).reshape(rows, -1),
            rope_back(own[:, :kv_width].reshape(rows, -1, HEAD), cos, sin).reshape(rows, -1),
            own[:, kv_width:],
        ],
        axis=1,
    ).astype(BF16)
    grad_attn_in = mm_shares(grad_lin, w_qkv)
    normed = kept["normed"]
    grad_norm = grad_attn_in * gains[0].astype(F32)
    grad_in = grad_mid + kept["scale"] * (
        grad_norm - normed * jnp.mean(grad_norm * normed, axis=1, keepdims=True)
    )
    return grad_in.astype(BF16), grad_lin, later, tied


def expert_middle(rows_in, grad_rows, gate_w, up_w, down_w):
    value, slope = gelu_parts(mm(rows_in, gate_w))
    up_pre = mm(rows_in, up_w)
    grad_inner = mm_nt(grad_rows, down_w)
    return (
        (value * up_pre).astype(BF16),
        (grad_inner * up_pre * slope).astype(BF16),
        (grad_inner * value).astype(BF16),
    )


def body(
    tokens, cotangent, seq_lengths, routes, gains, w_query, w_key, w_value, w_out, w_router, w_gate, w_up, w_down
):
    section = lax.axis_index(S_AX)
    is_first = section == 0
    fold_id = lax.axis_index(F_AX)
    replica = lax.axis_index(R_AX)
    core = replica % 2
    flip = (replica // 2) % 2
    folds, replicas = lax.axis_size(F_AX), lax.axis_size(R_AX)
    rows = tokens.shape[2]
    top = routes.shape[4]
    local = w_gate.shape[1]
    expert_count = w_router.shape[2]
    kv_width = w_key.shape[2]
    q_width = w_query.shape[2]
    capacity = rows * top // expert_count

    def own_batch(value):
        return lax.dynamic_index_in_dim(value, section, 0, keepdims=False)

    def swap_xor(value, bit):
        return lax.ppermute(value, R_AX, [(i, i ^ bit) for i in range(replicas)])

    def own_layer(pair):
        return jnp.where(is_first, pair[0], pair[1])

    def other_layer(pair):
        return jnp.where(is_first, pair[1], pair[0])

    def by_section(keep, got):
        return jnp.stack([jnp.where(is_first, keep, got), jnp.where(is_first, got, keep)])

    def both_batches(pair):
        return by_section(own_layer(pair), swap_section(other_layer(pair)))

    split = q_width + 2 * kv_width
    routes_at = HEAD // 4

    def widened(pieces):
        weights_part, routes_part = pieces
        routes_part = jnp.pad(routes_part.astype(BF16), ((0, weights_part.shape[0] - rows), (0, 0)))
        gap = jnp.zeros((weights_part.shape[0], routes_at - weights_part.shape[1]), BF16)
        whole = jnp.concatenate([weights_part, gap, routes_part], axis=1)
        return jnp.pad(whole, ((0, 0), (0, HEAD - whole.shape[1])))

    small = jnp.concatenate([w_router[0], gains[0].T], axis=1)
    my_routes = own_batch(routes[0, :, 0])
    give_routes = lax.dynamic_index_in_dim(routes[0, :, 0], 1 - section, 0, keepdims=False)
    joined = jnp.concatenate([w_query[0], w_key[0], w_value[0]], axis=1)
    depth = joined.shape[0]

    def column_share(value):
        width = value.shape[1] // replicas
        return lax.dynamic_slice_in_dim(value, replica * width, width, 1)

    def stacked_parts(parts):
        whole = jnp.zeros((folds,) + parts[0].shape, parts[0].dtype)
        for k, part in enumerate(parts):
            whole = lax.dynamic_update_index_in_dim(whole, part, (fold_id - k) % folds, 0)
        return whole.reshape((-1,) + parts[0].shape[1:])

    def stacked_rows(value):
        return stacked_parts(rel_gather(value))

    def of_first(value):
        return jnp.where(is_first, value, swap_section(value))

    def share_back(value):
        whole = jnp.zeros(value.shape, value.dtype)
        for bit in range(replicas):
            got = value[bit] if bit == 0 else swap_xor(value[bit], bit)
            whole = lax.dynamic_update_index_in_dim(whole, got, replica ^ bit, 0)
        return jnp.concatenate([whole[j] for j in range(replicas)], axis=1)

    def group_rows(value):
        parts = []
        for bit in range(0, replicas, 2):
            same = value if bit == 0 else swap_xor(value, bit)
            parts += [same, swap_core(same)]
        return parts

    my_tokens = own_batch(tokens[:, 0])
    token_group = jnp.concatenate(group_rows(my_tokens), axis=0)
    head_own = column_share(joined)
    lin_width = head_own.shape[1]
    head_swap = swap_section(jnp.concatenate([head_own, widened((small, give_routes))], axis=1))
    got_routes = head_swap[:rows, lin_width + routes_at : lin_width + routes_at + top].astype(jnp.int32)
    both_routes = jnp.where(
        is_first,
        jnp.concatenate([my_routes, got_routes], axis=1),
        jnp.concatenate([got_routes, my_routes], axis=1),
    )
    tail_cols = jnp.where(is_first, small, head_swap[:, lin_width : lin_width + small.shape[1]])
    head_got = jnp.concatenate(
        [jnp.where(is_first, head_own, head_swap[:, :lin_width]), widened((tail_cols, both_routes))], axis=1
    )
    part_ff = w_gate.shape[3] // 2
    pieces = []
    for part, axis in ((w_gate, 1), (w_up, 1), (w_down, 0)):
        chosen = lax.dynamic_index_in_dim(part[0], flip, 0, keepdims=False)
        pieces.append(lax.dynamic_slice_in_dim(chosen, core * part_ff, part_ff, axis))
    pieces, head_got = lax.optimization_barrier((pieces, head_got))
    crossed_y = [swap_section(pieces[0]), None, None]
    last_grad = own_batch(cotangent[:, 0])
    head_got, last_blocks = lax.optimization_barrier((head_got, rel_gather(last_grad)))
    head_parts, crossed_y[0] = lax.optimization_barrier((rel_gather(head_got), crossed_y[0]))
    head_block = stacked_parts(head_parts)
    tiles = head_parts
    crossed_y[1:] = [swap_section(value) for value in pieces[1:]]
    first = fold_id * local
    numbers = first + (jnp.arange(local, dtype=jnp.int32) ^ flip)
    scalars = [
        jnp.concatenate([jnp.stack([(section == layer).astype(jnp.int32), flip]), numbers]).astype(jnp.int32)
        for layer in range(2)
    ]
    first_tail = head_block[:, lin_width:]
    out_block = of_first(column_share(w_out[0]))
    head_block, out_block = lax.optimization_barrier((head_block, out_block))
    out_block = stacked_rows(out_block)
    group_in = attention_in(token_group.astype(F32), first_tail[:, expert_count])[2]
    first_lin = share_back(
        mm(group_in, head_block[:, :lin_width]).astype(BF16).reshape(replicas, rows, lin_width)
    )

    def first_out(mixed_low):
        group = jnp.concatenate(group_rows(mixed_low), axis=0)
        made = mm(group, out_block).astype(BF16)
        return share_back(made.reshape(replicas, rows, -1))

    shard = jnp.concatenate([joined, jnp.pad(small, ((0, 0), (0, HEAD - small.shape[1]))), w_out[0]], axis=1)
    share = depth // (2 * replicas)
    keep = lax.dynamic_slice_in_dim(shard, (section * replicas + replica) * share, share, 0)
    give = lax.dynamic_slice_in_dim(shard, ((1 - section) * replicas + replica) * share, share, 0)
    give, _ = lax.optimization_barrier((give, head_got))
    got = swap_section(give)

    def whole_weights(layer, keep, got):
        piece = jnp.where(section == layer, keep, got)
        full = lax.all_gather(piece, (F_AX, S_AX, R_AX), axis=0, tiled=True)
        tail = full[:, split : split + LANES]
        held["full"] = full
        return tail[:, expert_count : expert_count + 2].T, full[:, :split], full[:, split + LANES :], tail

    first_w = (
        first_tail[:, expert_count : expert_count + 2].T, None, None, first_tail
    )
    size = dict(
        folds=folds, local=local, rows=rows, parts=2, width=tokens.shape[3], ff=w_gate.shape[3],
        capacity=capacity, top=top, tile_at=lin_width // LANES,
    )

    lengths = own_batch(seq_lengths[:, 0])
    position = fold_id * rows + jnp.arange(rows, dtype=jnp.int32)
    order = (fold_id - jnp.arange(folds)) % folds
    key_pos = (order[:, None] * rows + jnp.arange(rows)[None, :]).reshape(-1).astype(jnp.int32)
    segment, offset = layout(lengths, position)
    key_seg, _ = layout(lengths, key_pos)
    freq = ROPE_BASE ** (-2.0 * jnp.arange(HEAD // 2, dtype=F32) / HEAD)
    angles = offset[:, None] * freq
    angles = jnp.concatenate([angles, angles], axis=1)[:, None, :]
    common = dict(
        cos=jnp.cos(angles), sin=jnp.sin(angles), groups=kv_width // HEAD, size=size,
        experts=expert_count,
        allowed=(segment[:, None] == key_seg[None, :]) & (key_pos[None, :] <= position[:, None]),
    )

    def first_mixed(tied_lin, tied, attn_in, mixed_low):
        gate_x, up_y = tied
        held["second"] = whole_weights(1, *tied_lin)
        return (crossed_y[0], up_y), (gate_x,)

    def first_moe(moe_in, own, more):
        same, cross = more
        same, cross, moe_in = lax.optimization_barrier(((*same, crossed_y[2]), cross, moe_in))
        cross = [*cross, swap_xor(same[1], 2), swap_xor(same[2], 2)]
        flat = []
        for one, two in zip(same, cross):
            flat += [one, swap_core(one), two, swap_core(two)]
        return moe_in, (own, flat), ()

    held = {}
    first_value, first_kept, experts_w, _ = layer_forward(
        my_tokens, first_w, (w_gate[0], w_up[0], w_down[0]), common, tiles, routes_at, scalars[0],
        dict(router=(head_block, lin_width // LANES), lin=(keep, got), kv=(swap_xor(crossed_y[0], 2), crossed_y[1]), mixed=first_mixed, moe=first_moe),
        first_lin, first_out,
    )
    head_share, out_share, _ = lax.optimization_barrier(
        (head_block[:, :lin_width], out_block, first_kept["moe"][1])
    )
    weights_first = (
        first_w[0], lax.all_gather(head_share, R_AX, axis=0), lax.all_gather(out_share, R_AX, axis=0), first_tail
    )

    second_w = held["second"]

    def left_pair(attn_in, mixed_low):
        pair = (
            jnp.concatenate([first_kept["attn_in"], first_kept["mixed_low"]], axis=1),
            jnp.concatenate([attn_in, mixed_low], axis=1),
        )
        return own_layer(pair), swap_section(other_layer(pair))

    second_value, second_kept, _, tied = layer_forward(
        first_value, second_w, experts_w, common, tiles, routes_at + top, scalars[1],
        dict(
            mixed=lambda one, two, attn_in, mixed_low: (attn_in, mixed_low),
            moe=lambda moe_in, own, more: (moe_in, own, (left_pair(*more), weights_first)),
            last=True, router=(held["full"], split // LANES),
        ),
    )
    left_rows, weights_first = tied
    second_parts, second_finish = second_value
    left_rows = jnp.concatenate(left_rows, axis=0)
    kept, weights = [first_kept, second_kept], [weights_first, second_w]

    half = local // 2

    def chip_rows(pair):
        chip = []
        for value in pair:
            keep = lax.dynamic_slice_in_dim(value, (core ^ flip) * half, half, 0)
            give = lax.dynamic_slice_in_dim(value, (1 - (core ^ flip)) * half, half, 0)
            got = swap_core(give)
            chip.append(jnp.concatenate([keep, got], axis=1))
        return chip

    chips = replicas // 2

    def all_x(value):
        return [swap_xor(value, bit) for bit in range(2, replicas, 2)]

    def by_order(value, others):
        whole = jnp.zeros((chips,) + value.shape, value.dtype)
        for at, part in enumerate([value] + others):
            whole = lax.dynamic_update_index_in_dim(whole, part, (replica // 2) ^ at, 0)
        return whole

    def flat_rows(whole):
        return jnp.moveaxis(whole, 1, 0).reshape(half, -1, whole.shape[-1])

    x_chip = chip_rows([state["moe"][0] for state in kept])
    x_mine, x_give = own_layer(x_chip), other_layer(x_chip)
    def both_rows(pair):
        return jnp.concatenate([own_layer(pair), swap_section(other_layer(pair))], axis=0)

    def own_columns(value):
        width = value.shape[1] // replicas
        parts = []
        for bit in range(replicas):
            piece = lax.dynamic_slice_in_dim(value, (replica ^ bit) * width, width, 1)
            parts.append(piece if bit == 0 else swap_xor(piece, bit))
        return jnp.stack(parts)

    def fold_sum(left, right, extra):
        total = mm_tn(left, right).astype(BF16)
        if extra is not None:
            total = total.reshape(folds, -1, total.shape[1])
            total = jnp.concatenate([total, extra], axis=1).reshape(-1, total.shape[2])
        return total

    def late_part(total, tie):
        if tie == ():
            return lax.psum_scatter(total, F_AX, scatter_dimension=0, tiled=True)
        else:
            step = total.shape[0] // folds
            mine = rel_scatter(
                [
                    lax.dynamic_slice_in_dim(total, ((fold_id - k) % folds) * step, step, 0)
                    for k in range(folds)
                ]
            ).astype(BF16)
        return lax.optimization_barrier((mine, tie))

    def spread_rows(mine):
        whole = jnp.zeros((replicas,) + mine.shape, BF16)
        for bit, part in enumerate(group_rows(mine)):
            whole = lax.dynamic_update_index_in_dim(whole, part, replica ^ bit, 0)
        return whole

    def side_by_side(value):
        return jnp.concatenate([value[j].astype(F32) for j in range(replicas)], axis=1)

    left_whole = group_rows(left_rows)
    model = tokens.shape[3]
    piece = model // (folds * replicas)
    count = expert_count + 1
    tall = -(-count // 16) * 16

    def with_small(grad_attn, small):
        value = small.reshape(count, folds, replicas, piece)
        value = jnp.transpose(value, (0, 2, 1, 3)).reshape(count, model)
        return jnp.concatenate([grad_attn, jnp.pad(value, ((0, tall - count), (0, 0)))], axis=0)

    def last_rows(grad_expert):
        held["rows"] = chip_rows([grad_expert])[0]
        return left_whole, stacked_parts(second_parts)

    def two(value):
        middle_row = value.shape[1] // 2
        return value[:, :middle_row], value[:, middle_row:]

    def joined_rows(one, other):
        return [jnp.concatenate(pair, axis=1) for pair in zip(one, other)]

    def last_attn(grad_attn, small, sent):
        held["attn"] = with_small(grad_attn, small)
        give_one, give_two = two(x_give)
        return swap_section(give_one), give_two, sent[1]

    def last_later(sent, crossed):
        got_one, give_two, stack = crossed
        return sent[0], stack, got_one, swap_section(give_two), all_x(got_one), all_x(x_mine)

    def first_rows(grad_expert):
        chip = (chip_rows([grad_expert])[0], held["rows"])
        mine = own_layer(chip)
        return mine, all_x(mine), swap_section(other_layer(chip)), x_own, second_stack

    def first_attn(grad_attn, small, sent):
        *sent, stack = sent
        held["second_sum"] = lax.psum_scatter(stack, F_AX, scatter_dimension=0, tiled=True)
        return both_rows((with_small(grad_attn, small), held["attn"])), sent

    def first_later(sent, crossed):
        right_out, (mine, mine_x, got, x_own) = crossed
        g_own = by_order(mine, mine_x)
        return x_own, g_own, [expert_middle(x_own[i], flat_rows(g_own)[i], *[w[i] for w in mine_w]) for i in range(half)], got, own_columns(right_out)

    grads, grad_lin = [None, None], [None, None]
    grads[1], grad_lin[1], (left_whole, second_stack, x_got, x_got_two, x_got_x, x_mine_x), _ = layer_backward(
        last_grad, kept[1], weights[1], experts_w, common, scalars[1], (),
        dict(rows=last_rows, attn=last_attn, later=last_later, blocks=last_blocks),
    )
    x_own = flat_rows(by_order(x_mine, x_mine_x))
    x_own = [x_own[i] for i in range(half)]
    mine_w = [lax.dynamic_slice_in_dim(part[0], core * half, half, 0) for part in (w_gate, w_up, w_down)]
    grads[0], grad_lin[0], later, x_got_two_x = layer_backward(
        grads[1], kept[0], weights[0], experts_w, common, scalars[0], all_x(x_got_two),
        dict(rows=first_rows, attn=first_attn, later=first_later),
    )
    x_own, g_own, middle_own, got, right_out = later
    (x_got,) = joined_rows([x_got], [x_got_two])
    x_got_x = joined_rows(x_got_x, x_got_two_x)
    left_whole = jnp.concatenate(left_whole, axis=0)
    right_out = right_out.reshape(replicas, 2, rows + tall, -1)
    extra = jnp.sum(right_out[:, :, rows:].astype(F32), axis=(0, 1)).reshape(tall, folds, piece)
    extra = jnp.pad(
        jnp.transpose(extra, (1, 0, 2)), ((0, 0), (0, 0), (0, right_out.shape[3] - piece))
    ).astype(BF16)
    right_out = right_out[:, :, :rows].reshape(-1, right_out.shape[3])
    out_shard = late_part(fold_sum(left_whole[:, model:], right_out, extra), ())
    lin_rows, second_sum = lax.optimization_barrier((both_rows(grad_lin), held["second_sum"]))
    right, got = lax.optimization_barrier((own_columns(lin_rows), got))
    got_x = all_x(got)
    g_got, x_got = by_order(got, got_x), by_order(x_got, x_got_x)
    shard = fold_sum(left_whole[:, :model], right.reshape(-1, right.shape[2]), None)
    shard, (middle_own, x_own, first_value, grads) = lax.optimization_barrier(
        (shard, (middle_own, x_own, first_value, grads))
    )
    x_got = [flat_rows(x_got)[i] for i in range(half)]
    g_own, g_got = [[flat_rows(value)[i] for i in range(half)] for value in (g_own, g_got)]
    middle_got = [expert_middle(x_got[i], g_got[i], *[w[i] for w in mine_w]) for i in range(half)]

    shard, (middle_got, out_shard) = late_part(shard, (middle_got, out_shard))
    shard, out_shard = spread_rows(shard), spread_rows(out_shard)
    made = []
    for i in range(half):
        inner, gate, up = zip(middle_own[i], middle_got[i])
        made.append(
            (
                (mm_tn(x_own[i], gate[0]) + mm_tn(x_got[i], gate[1])).astype(BF16),
                (mm_tn(x_own[i], up[0]) + mm_tn(x_got[i], up[1])).astype(BF16),
                (mm_tn(inner[0], g_own[i]) + mm_tn(inner[1], g_got[i])).astype(BF16),
            )
        )
    made, second_sum = lax.optimization_barrier((made, second_sum))
    outs = [first_value, second_finish([second_sum])]
    small = side_by_side(out_shard[:, depth:, :piece])
    out_shard = side_by_side(out_shard[:, :depth])
    shard = side_by_side(shard)
    gain_one = jnp.sum(shard * joined.astype(F32), axis=1) / gains[0, 0].astype(F32)
    expert_out = []
    for slot in range(3):
        keep = jnp.stack([one[slot] for one in made])
        got = swap_core(keep)
        both = jnp.concatenate(
            [jnp.where(core == 0, keep, got), jnp.where(core == 0, got, keep)], axis=0
        )
        expert_out.append(both.astype(F32)[None])
    layer_outputs = both_batches(outs)
    input_grads = both_batches(grads)
    return (
        layer_outputs[None, :, None],
        input_grads[None, :, None],
        jnp.stack([gain_one, small[expert_count]])[None],
        shard[None, :, :q_width],
        shard[None, :, q_width : q_width + kv_width],
        shard[None, :, q_width + kv_width : split],
        out_shard[None],
        small[:expert_count].T[None],
        expert_out[0],
        expert_out[1],
        expert_out[2],
    )


def solution(mesh):
    acts = P(None, R_AX, F_AX, None)
    rows = P(S_AX, F_AX, None)
    expert = P(S_AX, F_AX, None, None)
    stacked = P(S_AX, None, R_AX, F_AX, None)
    gain = P(S_AX, None, F_AX)
    return jax.shard_map(
        body,
        mesh=mesh,
        in_specs=(acts, acts, P(None, R_AX, None), stacked, gain)
        + (rows,) * 5
        + (expert,) * 3,
        out_specs=(stacked, stacked, gain) + (rows,) * 5 + (expert,) * 3,
        check_vma=False,
    )
```

```python
import functools

import jax
import jax.numpy as jnp
from jax import lax
from jax.experimental import pallas as pl
from jax.experimental.pallas import tpu as pltpu
from jax.sharding import PartitionSpec as P

HEAD = 128
ROPE_BASE = 1000000.0
EPS = 1e-06
MASKED = -1e30
F32 = jnp.float32
BF16 = jnp.bfloat16
S_AX, F_AX, R_AX = "section", "fsdp", "replica"
HIGHEST = lax.Precision.HIGHEST
LANES = 128
GELU_C = 0.7978845608028654
GELU_A = 0.044715


def dot(a, b):
    return lax.dot_general(a, b, (((1,), (0,)), ((), ())), preferred_element_type=F32)


def dot_nt(a, b):
    return lax.dot_general(a, b, (((1,), (1,)), ((), ())), preferred_element_type=F32)


def dot_tn(a, b):
    return lax.dot_general(a, b, (((0,), (0,)), ((), ())), preferred_element_type=F32)


def gelu_parts(x):
    t = jnp.tanh(GELU_C * (x + GELU_A * x * x * x))
    value = 0.5 * x * (1.0 + t)
    slope = 0.5 * (1.0 + t) + 0.5 * x * (1.0 - t * t) * GELU_C * (1.0 + 3.0 * GELU_A * x * x)
    return value, slope


def lane_is(shape, number):
    return lax.broadcasted_iota(jnp.int32, shape, 1) == number


def masked_mix(logits, mask):
    kept = jnp.where(mask > 0.0, logits, -1e30)
    expo = jnp.exp(kept - jnp.max(kept, axis=1, keepdims=True)) * mask
    return expo / jnp.sum(expo, axis=1, keepdims=True)


def one_hot(slots_ref, block, step, capacity):
    rows = slots_ref.shape[2]
    place = lax.broadcasted_iota(jnp.int32, (capacity, rows), 0)
    return place == slots_ref[block, step : step + 1, :]


def route_mask(tile, at, top):
    lane = lax.broadcasted_iota(jnp.int32, tile.shape, 1).astype(F32)
    named = tile.astype(F32)
    hit = lane == named[:, at : at + 1]
    for k in range(1, top):
        hit = hit | (lane == named[:, at + k : at + k + 1])
    return jnp.where(hit, 1.0, 0.0)


def weight_copies(scalars, own, pieces, buffers, sems):
    own_g, own_u, own_d = own
    parts = len(pieces[0][0])
    ff = own_g.shape[2] // parts
    is_own, flip = scalars[0], scalars[1]
    waits = {}
    for step in range(len(pieces[0])):
        for part in range(parts):
            expert = step ^ flip
            cols = pl.ds(part * ff, ff)
            sources = (own_g.at[expert, :, cols], own_u.at[expert, :, cols], own_d.at[expert, cols, :])
            for kind in range(3):
                target = buffers[kind].at[step, part]
                sem = sems.at[kind, step, part]

                @pl.when(is_own == 1)
                def _(source=sources[kind], target=target, sem=sem):
                    pltpu.make_async_copy(source, target, sem).start()

                @pl.when(is_own == 0)
                def _(source=pieces[kind][step][part], target=target, sem=sem):
                    pltpu.make_async_copy(source, target, sem).start()

                waits[kind, step, part] = pltpu.make_async_copy(
                    pieces[kind][step][part], target, sem
                )
    return waits


def split_refs(refs, counts):
    out, at = [], 0
    for count in counts:
        out.append(refs[at : at + count])
        at += count
    return out


def moe_fwd_kernel(folds, local, parts, capacity, routes_at, top, *refs):
    (scalars, router), tiles, blocks, own, flat, outs, partials, scratch = split_refs(
        refs, (2, folds, folds, 3, 3 * local * parts, 7, folds, 4)
    )
    scalars_ref = scalars
    picked_ref, gate_ref, up_ref, made_ref, grows_ref, slots, mix_ref = outs
    buf_g, buf_u, buf_d, sems = scratch
    pieces = [
        [[flat[(kind * local + step) * parts + part] for part in range(parts)] for step in range(local)]
        for kind in range(3)
    ]
    waits = weight_copies(scalars_ref, own, pieces, (buf_g, buf_u, buf_d), sems)
    rows = blocks[0].shape[0]
    width = blocks[0].shape[1]
    ff = buf_g.shape[3]
    square = (rows, rows)
    earlier = jnp.where(
        lax.broadcasted_iota(jnp.int32, square, 0) < lax.broadcasted_iota(jnp.int32, square, 1), 1.0, 0.0
    ).astype(BF16)
    same = jnp.where(
        lax.broadcasted_iota(jnp.int32, square, 0) == lax.broadcasted_iota(jnp.int32, square, 1), 1.0, 0.0
    ).astype(BF16)
    for k in range(folds):
        mask = route_mask(tiles[k][...], routes_at, top)
        mix = masked_mix(dot(blocks[k][...], router[...]), mask)
        if k == 0:
            mix_ref[...] = mix
        low = mask.astype(BF16)
        rank = dot_tn(low, earlier)
        named = dot_tn(low, same)
        place = jnp.where(named > 0.5, rank, -1.0)
        number = lax.broadcasted_iota(jnp.int32, place.shape, 0)
        for step in range(local):
            row = jnp.sum(jnp.where(number == scalars_ref[2 + step], place, 0.0), axis=0, keepdims=True)
            slots[k, step : step + 1, :] = row.astype(jnp.int32)
        for step in range(local):
            pick = one_hot(slots, k, step, capacity)
            at = pl.ds(k * capacity, capacity)
            picked_ref[step, at, :] = dot(
                jnp.where(pick, 1.0, 0.0).astype(BF16), blocks[k][...]
            ).astype(BF16)
            grows_ref[step, at, :] = lax.dot_general(
                jnp.where(pick, 1.0, 0.0), mix, (((1,), (0,)), ((), ())),
                precision=HIGHEST, preferred_element_type=F32,
            )
    for step in range(local):
        for part in range(parts):
            for kind in range(3):
                waits[kind, step, part].wait()
            cols = pl.ds(part * ff, ff)
            x = picked_ref[step]
            gate = dot(x, buf_g[step, part])
            up = dot(x, buf_u[step, part])
            gate_ref[step, :, cols] = gate
            up_ref[step, :, cols] = up
            inner = (gelu_parts(gate)[0] * up).astype(BF16)
            term = dot(inner, buf_d[step, part])
            made = term if part == 0 else made + term
        made_ref[step] = made.astype(BF16)
    for k in range(folds):
        at = pl.ds(k * capacity, capacity)
        picks, weighted = [], []
        for step in range(local):
            gates = grows_ref[step, at, :]
            own_lane = lane_is(gates.shape, scalars_ref[2 + step])
            factor = jnp.sum(jnp.where(own_lane, gates, 0.0), axis=1, keepdims=True)
            picks.append(jnp.where(one_hot(slots, k, step, capacity), 1.0, 0.0).astype(BF16))
            weighted.append((made_ref[step, at, :].astype(F32) * factor).astype(BF16))
        partials[k][...] = dot_tn(
            jnp.concatenate(picks, axis=0), jnp.concatenate(weighted, axis=0)
        ).astype(BF16)


def moe_bwd_kernel(folds, local, parts, capacity, *refs):
    (scalars, slots, gate_ref, up_ref, made_ref, grows_ref), blocks, own, flat, (ge_ref,), partials, scratch = split_refs(
        refs, (6, folds, 3, 3 * local * parts, 1, folds, 6)
    )
    buf_g, buf_u, buf_d, sems, dx_ref, dots_ref = scratch
    pieces = [
        [[flat[(kind * local + step) * parts + part] for part in range(parts)] for step in range(local)]
        for kind in range(3)
    ]
    waits = weight_copies(scalars, own, pieces, (buf_g, buf_u, buf_d), sems)
    ff = buf_g.shape[3]
    for step in range(local):
        for k in range(folds):
            at = pl.ds(k * capacity, capacity)
            pick = jnp.where(one_hot(slots, k, step, capacity), 1.0, 0.0).astype(BF16)
            dout = dot(pick, blocks[k][...])
            gates = grows_ref[step, at, :]
            own_lane = lane_is(gates.shape, scalars[2 + step])
            factor = jnp.sum(jnp.where(own_lane, gates, 0.0), axis=1, keepdims=True)
            value = jnp.sum(dout * made_ref[step, at, :].astype(F32), axis=1, keepdims=True)
            lane = lax.broadcasted_iota(jnp.int32, gates.shape, 1)
            number = scalars[2 + step]
            dots_ref[step, at, :] = jnp.where(
                (lane == number) | (lane == number + LANES // 2), value, 0.0
            )
            ge_ref[step, at, :] = (dout * factor).astype(BF16)
    for step in range(local):
        ge = ge_ref[step]
        for part in range(parts):
            for kind in range(3):
                waits[kind, step, part].wait()
            cols = pl.ds(part * ff, ff)
            grad_inner = dot_nt(ge, buf_d[step, part])
            gate = gate_ref[step, :, cols]
            up = up_ref[step, :, cols]
            value, slope = gelu_parts(gate)
            grad_gate = (grad_inner * up * slope).astype(BF16)
            grad_up = (grad_inner * value).astype(BF16)
            term = dot_nt(grad_gate, buf_g[step, part]) + dot_nt(grad_up, buf_u[step, part])
            total = term if part == 0 else total + term
        dx_ref[step] = total.astype(BF16)
    for k in range(folds):
        at = pl.ds(k * capacity, capacity)
        hot = [one_hot(slots, k, step, capacity) for step in range(local)]
        picks = jnp.concatenate([jnp.where(one, 1.0, 0.0) for one in hot], axis=0)
        width = ge_ref.shape[2]
        partials[k][:, :width] = dot_tn(
            picks.astype(BF16), jnp.concatenate([dx_ref[step, at, :] for step in range(local)], axis=0)
        ).astype(BF16)
        dots = lax.dot_general(
            picks, jnp.concatenate([dots_ref[step, at, :] for step in range(local)], axis=0),
            (((0,), (0,)), ((), ())), precision=HIGHEST, preferred_element_type=F32,
        )
        high = dots.astype(BF16).astype(F32)
        lane = lax.broadcasted_iota(jnp.int32, dots.shape, 1)
        partials[k][:, width:] = jnp.where(lane < LANES // 2, high, dots - high).astype(BF16)


def vmem(count):
    return [pl.BlockSpec(memory_space=pltpu.VMEM)] * count


def anywhere(count):
    return [pl.BlockSpec(memory_space=pl.ANY)] * count


def weight_scratch(own, local, parts):
    width, ff = own[0].shape[1], own[0].shape[2] // parts
    return [
        pltpu.VMEM((local, parts, width, ff), BF16),
        pltpu.VMEM((local, parts, width, ff), BF16),
        pltpu.VMEM((local, parts, ff, width), BF16),
        pltpu.SemaphoreType.DMA((3, local, parts)),
    ]


def cost(rows, width, ff, products):
    return pl.CostEstimate(
        flops=2 * rows * width * ff * products, bytes_accessed=2 * 3 * width * ff * 2 + 8 * rows * width,
        transcendentals=rows * ff,
    )


def moe_fwd_call(
    scalars, tiles, routes_at, router, blocks, own, flat, folds, local, rows, parts, width, ff, capacity, top, tile_at
):
    router, router_at = router
    picked_rows = folds * capacity
    shapes = [
        jax.ShapeDtypeStruct((local, picked_rows, width), BF16),
        jax.ShapeDtypeStruct((local, picked_rows, ff), F32),
        jax.ShapeDtypeStruct((local, picked_rows, ff), F32),
        jax.ShapeDtypeStruct((local, picked_rows, width), BF16),
        jax.ShapeDtypeStruct((local, picked_rows, LANES), F32),
        jax.ShapeDtypeStruct((folds, local, rows), jnp.int32),
        jax.ShapeDtypeStruct((rows, LANES), F32),
    ] + [jax.ShapeDtypeStruct((rows, width), BF16)] * folds
    out = pl.pallas_call(
        functools.partial(moe_fwd_kernel, folds, local, parts, capacity, routes_at, top),
        out_shape=shapes,
        in_specs=[
            pl.BlockSpec(memory_space=pltpu.SMEM),
            pl.BlockSpec((router.shape[0], LANES), lambda i: (0, router_at)),
        ]
        + [pl.BlockSpec((rows, LANES), lambda i: (0, tile_at))] * folds
        + vmem(folds) + anywhere(3 + len(flat)),
        grid=(1,),
        out_specs=vmem(len(shapes)),
        scratch_shapes=weight_scratch(own, local, parts),
        cost_estimate=cost(local * picked_rows, width, ff, 3),
        compiler_params=pltpu.CompilerParams(vmem_limit_bytes=56 << 20),
    )(scalars, router, *tiles, *blocks, *own, *flat)
    return out[:7], out[7:]


def moe_bwd_call(scalars, kept, blocks, own, flat, folds, local, rows, parts, width, ff, capacity, top, tile_at):
    _, gate_pre, up_pre, made, gate_rows, slots, _ = kept
    picked_rows = folds * capacity
    shapes = [jax.ShapeDtypeStruct((local, picked_rows, width), BF16)] + [
        jax.ShapeDtypeStruct((rows, width + LANES), BF16)
    ] * folds
    out = pl.pallas_call(
        functools.partial(moe_bwd_kernel, folds, local, parts, capacity),
        out_shape=shapes,
        in_specs=[pl.BlockSpec(memory_space=pltpu.SMEM)]
        + vmem(5 + folds) + anywhere(3 + len(flat)),
        out_specs=vmem(len(shapes)),
        scratch_shapes=weight_scratch(own, local, parts)
        + [pltpu.VMEM((local, picked_rows, width), BF16), pltpu.VMEM((local, picked_rows, LANES), F32)],
        cost_estimate=cost(local * picked_rows, width, ff, 3),
        compiler_params=pltpu.CompilerParams(vmem_limit_bytes=56 << 20),
    )(scalars, slots, gate_pre, up_pre, made, gate_rows, *blocks, *own, *flat)
    return out[0], out[1:]


def mm(a, b):
    return jnp.dot(a, b, preferred_element_type=F32)


def mm_nt(a, b):
    return lax.dot_general(a, b, (((1,), (1,)), ((), ())), preferred_element_type=F32)


def mm_shares(a, shares):
    if shares.ndim == 2:
        return mm_nt(a, shares)
    width = shares.shape[2]
    return sum(mm_nt(a[:, j * width : (j + 1) * width], shares[j]) for j in range(shares.shape[0]))


def mm_tn(a, b):
    return lax.dot_general(a, b, (((0,), (0,)), ((), ())), preferred_element_type=F32)


def ein(spec, a, b):
    return jnp.einsum(spec, a, b, preferred_element_type=F32)


def rel_gather(value):
    folds = lax.axis_size(F_AX)
    parts = [value]
    for k in range(1, folds):
        parts.append(lax.ppermute(value, F_AX, [(i, (i + k) % folds) for i in range(folds)]))
    return parts


def rel_scatter(parts):
    folds = lax.axis_size(F_AX)
    total = parts[0].astype(F32)
    for k in range(1, folds):
        got = lax.ppermute(parts[k], F_AX, [(i, (i - k) % folds) for i in range(folds)])
        total = total + got.astype(F32)
    return total


def send_back(parts):
    folds = lax.axis_size(F_AX)
    return [parts[0]] + [
        lax.ppermute(parts[k], F_AX, [(i, (i - k) % folds) for i in range(folds)]) for k in range(1, folds)
    ]


def add_up(parts):
    total = parts[0].astype(F32)
    for part in parts[1:]:
        total = total + part.astype(F32)
    return total


def swap_section(value):
    return lax.ppermute(value, S_AX, [(0, 1), (1, 0)])


def swap_core(value):
    count = lax.axis_size(R_AX)
    return lax.ppermute(value, R_AX, [(i, i ^ 1) for i in range(count)])


def rope_turn(values, cos, sin):
    half = HEAD // 2
    turned = jnp.concatenate([-values[..., half:], values[..., :half]], axis=-1)
    return values * cos + turned * sin


def rope_back(grads, cos, sin):
    half = HEAD // 2
    scaled = grads * sin
    turned = jnp.concatenate([scaled[..., half:], -scaled[..., :half]], axis=-1)
    return grads * cos + turned


def layout(lengths, position):
    bounds = jnp.cumsum(lengths)
    passed = (position[:, None] >= bounds[None, :]).astype(jnp.int32)
    segment = jnp.sum(passed, axis=1)
    start = jnp.sum(passed * lengths[None, :], axis=1)
    return segment, (position - start).astype(F32)


def gated(gate, up):
    return jax.nn.gelu(gate) * up


def attention_in(hidden, gain):
    scale = lax.rsqrt(jnp.mean(hidden * hidden, axis=1, keepdims=True) + EPS)
    normed = hidden * scale
    return scale, normed, (normed * gain.astype(F32)).astype(BF16)


def turn_heads(lin, common, kv_width):
    rows = lin.shape[0]
    q_width = lin.shape[1] - 2 * kv_width
    turned = rope_turn(
        lin[:, : q_width + kv_width].astype(F32).reshape(rows, -1, HEAD), common["cos"], common["sin"]
    ).astype(BF16).reshape(rows, -1)
    kv = jnp.concatenate([turned[:, q_width:], lin[:, q_width + kv_width :].astype(BF16)], axis=1)
    return turned[:, :q_width], kv


def grouped_heads(value, groups):
    rows = value.shape[0]
    return value.reshape(rows, groups, -1, HEAD)


def attend(query, kv_all, allowed, groups):
    keys = kv_all[:, : groups * HEAD].reshape(-1, groups, HEAD)
    values = kv_all[:, groups * HEAD :].reshape(-1, groups, HEAD)
    raw = ein("tgha,sga->ghts", grouped_heads(query, groups), keys) * HEAD ** (-0.5)
    scores = jnp.where(allowed[None, None], raw, MASKED)
    top = jnp.max(scores, axis=3, keepdims=True)
    expo = jnp.exp(scores - top)
    probs = expo / jnp.sum(expo, axis=3, keepdims=True)
    mixed = ein("ghts,sga->tgha", probs.astype(BF16), values)
    return mixed.reshape(query.shape), probs


def attend_back(grad_mixed, mixed, probs, query, kv_all, groups):
    rows = query.shape[0]
    keys = kv_all[:, : groups * HEAD].reshape(-1, groups, HEAD)
    values = kv_all[:, groups * HEAD :].reshape(-1, groups, HEAD)
    grad_grouped = grouped_heads(grad_mixed, groups)
    delta = jnp.sum(
        grad_grouped.astype(F32) * grouped_heads(mixed, groups), axis=3
    )
    delta = jnp.transpose(delta, (1, 2, 0))[..., None]
    grad_probs = ein("tgha,sga->ghts", grad_grouped, values)
    grad_scores = (probs * (grad_probs - delta)).astype(BF16)
    score_scale = HEAD ** (-0.5)
    grad_query = (ein("ghts,sga->tgha", grad_scores, keys) * score_scale).reshape(rows, -1, HEAD)
    grad_key = ein("ghts,tgha->sga", grad_scores, grouped_heads(query, groups)) * score_scale
    grad_value = ein("ghts,tgha->sga", probs.astype(BF16), grad_grouped)
    count = kv_all.shape[0]
    grad_kv = jnp.concatenate(
        [grad_key.reshape(count, -1), grad_value.reshape(count, -1)], axis=1
    ).astype(BF16)
    return grad_query, grad_kv


def moe_forward(router, tiles, routes_at, scalars, experts_w, size, blocks):
    outs, partials = moe_fwd_call(
        scalars, tiles, routes_at, router, blocks, *experts_w, **size
    )
    return partials, outs


def moe_backward(blocks, kept, scalars, experts_w, size, tie, hooks):
    blocks, tied = lax.optimization_barrier((blocks, tie))
    grad_expert, partials = moe_bwd_call(scalars, kept, blocks, *experts_w, **size)
    sent = hooks["rows"](grad_expert)
    summed, sent = lax.optimization_barrier((rel_scatter(partials), sent))
    width = blocks[0].shape[1]
    tail = summed[:, width:]
    half = LANES // 2
    dots = tail[:, :half] + tail[:, half:]
    return summed[:, :width], jnp.pad(dots, ((0, 0), (0, half))), sent, tied


def layer_forward(layer_in, weights, experts_w, common, tiles, routes_at, scalars, tie, projected=None, out_product=None):
    gains, w_qkv, w_out, router = weights
    groups = common["groups"]
    hidden = layer_in.astype(F32)
    scale, normed, attn_in = attention_in(hidden, gains[0])
    lin = mm(attn_in, w_qkv) if projected is None else projected
    lin, tied_lin = lax.optimization_barrier((lin, tie.get("lin", ())))
    query, kv = turn_heads(lin, common, groups * HEAD)
    kv_all, tied_kv = lax.optimization_barrier(
        (jnp.concatenate(rel_gather(kv), axis=0), tie.get("kv", ()))
    )
    mixed, probs = attend(query, kv_all, common["allowed"], groups)
    mixed_low = mixed.astype(BF16)
    more = tie["mixed"](tied_lin, tied_kv, attn_in, mixed_low) if "mixed" in tie else ()
    mixed_low, more = lax.optimization_barrier((mixed_low, more))
    if out_product is None:
        residual = hidden + mm(mixed_low, w_out)
    else:
        residual = hidden + out_product(mixed_low).astype(F32)
    scale_two = lax.rsqrt(jnp.mean(residual * residual, axis=1, keepdims=True) + EPS)
    normed_two = residual * scale_two
    moe_in = (normed_two * gains[1].astype(F32)).astype(BF16)
    if "moe" in tie:
        moe_in, experts_w, more = tie["moe"](moe_in, experts_w, more)
    blocks, tied = lax.optimization_barrier((rel_gather(moe_in), more))
    parts, moe_kept = moe_forward(tie["router"], tiles, routes_at, scalars, experts_w, common["size"], blocks)
    finish = lambda got: (residual + add_up(got)).astype(BF16)
    out = finish(send_back(parts)) if "last" not in tie else (parts, finish)
    kept = dict(
        scale=scale, normed=normed, attn_in=attn_in, query=query, kv=kv,
        kv_all=kv_all, mixed=mixed, probs=probs, mixed_low=mixed_low, scale_two=scale_two,
        normed_two=normed_two, moe_in=moe_in, mix=moe_kept[6], moe=moe_kept,
    )
    return out, kept, experts_w, tied


def layer_backward(grad_low, kept, weights, experts_w, common, scalars, tie, hooks):
    gains, w_qkv, w_out, router = weights
    groups = common["groups"]
    grad_out = grad_low.astype(F32)
    rows = grad_out.shape[0]
    blocks = hooks["blocks"] if "blocks" in hooks else rel_gather(grad_low)
    grad_moe_in, dots, sent, tied = moe_backward(
        blocks, kept["moe"], scalars, experts_w, common["size"], tie, hooks
    )
    mix = kept["mix"]
    grad_logits = mix * (dots - jnp.sum(mix * dots, axis=1, keepdims=True))
    moe_in = kept["moe_in"]
    count = common["experts"]
    high = grad_logits.astype(BF16)
    rest = (grad_logits - high.astype(F32)).astype(BF16)
    both = mm_tn(jnp.concatenate([high[:, :count], rest[:, :count]], axis=1), moe_in)
    grad_router = both[:count] + both[count:]
    grad_moe_in = grad_moe_in + mm_nt(high, router) + mm_nt(rest, router)
    normed_two = kept["normed_two"]
    grad_norm = grad_moe_in * gains[1].astype(F32)
    grad_gain_two = jnp.sum(grad_moe_in * normed_two, axis=0)
    grad_mid = grad_out + kept["scale_two"] * (
        grad_norm - normed_two * jnp.mean(grad_norm * normed_two, axis=1, keepdims=True)
    )
    grad_attn = grad_mid.astype(BF16)
    small = jnp.concatenate([grad_router, grad_gain_two[None]], axis=0).astype(BF16)
    crossed = hooks["attn"](grad_attn, small, sent)
    grad_mixed = mm_shares(grad_attn, w_out).astype(BF16)
    grad_query, grad_kv = attend_back(
        grad_mixed, kept["mixed"], kept["probs"], kept["query"], kept["kv_all"], groups
    )
    grad_kv, crossed = lax.optimization_barrier((grad_kv, crossed))
    later = hooks["later"](sent, crossed)
    own = rel_scatter([grad_kv[k * rows : (k + 1) * rows] for k in range(lax.axis_size(F_AX))])
    own, later = lax.optimization_barrier((own, later))
    cos, sin = common["cos"], common["sin"]
    kv_width = groups * HEAD
    grad_lin = jnp.concatenate(
        [
            rope_back(grad_query, cos, sin).reshape(rows, -1),
            rope_back(own[:, :kv_width].reshape(rows, -1, HEAD), cos, sin).reshape(rows, -1),
            own[:, kv_width:],
        ],
        axis=1,
    ).astype(BF16)
    grad_attn_in = mm_shares(grad_lin, w_qkv)
    normed = kept["normed"]
    grad_norm = grad_attn_in * gains[0].astype(F32)
    grad_in = grad_mid + kept["scale"] * (
        grad_norm - normed * jnp.mean(grad_norm * normed, axis=1, keepdims=True)
    )
    return grad_in.astype(BF16), grad_lin, later, tied


def expert_middle(rows_in, grad_rows, gate_w, up_w, down_w):
    value, slope = gelu_parts(mm(rows_in, gate_w))
    up_pre = mm(rows_in, up_w)
    grad_inner = mm_nt(grad_rows, down_w)
    return (
        (value * up_pre).astype(BF16),
        (grad_inner * up_pre * slope).astype(BF16),
        (grad_inner * value).astype(BF16),
    )


def body(
    tokens, cotangent, seq_lengths, routes, gains, w_query, w_key, w_value, w_out, w_router, w_gate, w_up, w_down
):
    section = lax.axis_index(S_AX)
    is_first = section == 0
    fold_id = lax.axis_index(F_AX)
    replica = lax.axis_index(R_AX)
    core = replica % 2
    flip = (replica // 2) % 2
    folds, replicas = lax.axis_size(F_AX), lax.axis_size(R_AX)
    rows = tokens.shape[2]
    top = routes.shape[4]
    local = w_gate.shape[1]
    expert_count = w_router.shape[2]
    kv_width = w_key.shape[2]
    q_width = w_query.shape[2]
    capacity = rows * top // expert_count

    def own_batch(value):
        return lax.dynamic_index_in_dim(value, section, 0, keepdims=False)

    def swap_xor(value, bit):
        return lax.ppermute(value, R_AX, [(i, i ^ bit) for i in range(replicas)])

    def own_layer(pair):
        return jnp.where(is_first, pair[0], pair[1])

    def other_layer(pair):
        return jnp.where(is_first, pair[1], pair[0])

    def by_section(keep, got):
        return jnp.stack([jnp.where(is_first, keep, got), jnp.where(is_first, got, keep)])

    def both_batches(pair):
        return by_section(own_layer(pair), swap_section(other_layer(pair)))

    split = q_width + 2 * kv_width
    routes_at = HEAD // 4

    def widened(pieces):
        weights_part, routes_part = pieces
        routes_part = jnp.pad(routes_part.astype(BF16), ((0, weights_part.shape[0] - rows), (0, 0)))
        gap = jnp.zeros((weights_part.shape[0], routes_at - weights_part.shape[1]), BF16)
        whole = jnp.concatenate([weights_part, gap, routes_part], axis=1)
        return jnp.pad(whole, ((0, 0), (0, HEAD - whole.shape[1])))

    small = jnp.concatenate([w_router[0], gains[0].T], axis=1)
    my_routes = own_batch(routes[0, :, 0])
    give_routes = lax.dynamic_index_in_dim(routes[0, :, 0], 1 - section, 0, keepdims=False)
    joined = jnp.concatenate([w_query[0], w_key[0], w_value[0]], axis=1)
    depth = joined.shape[0]

    def column_share(value):
        width = value.shape[1] // replicas
        return lax.dynamic_slice_in_dim(value, replica * width, width, 1)

    def stacked_parts(parts):
        whole = jnp.zeros((folds,) + parts[0].shape, parts[0].dtype)
        for k, part in enumerate(parts):
            whole = lax.dynamic_update_index_in_dim(whole, part, (fold_id - k) % folds, 0)
        return whole.reshape((-1,) + parts[0].shape[1:])

    def stacked_rows(value):
        return stacked_parts(rel_gather(value))

    def of_first(value):
        return jnp.where(is_first, value, swap_section(value))

    def share_back(value):
        whole = jnp.zeros(value.shape, value.dtype)
        for bit in range(replicas):
            got = value[bit] if bit == 0 else swap_xor(value[bit], bit)
            whole = lax.dynamic_update_index_in_dim(whole, got, replica ^ bit, 0)
        return jnp.concatenate([whole[j] for j in range(replicas)], axis=1)

    def group_rows(value):
        parts = []
        for bit in range(0, replicas, 2):
            same = value if bit == 0 else swap_xor(value, bit)
            parts += [same, swap_core(same)]
        return parts

    my_tokens = own_batch(tokens[:, 0])
    token_group = jnp.concatenate(group_rows(my_tokens), axis=0)
    head_own = column_share(joined)
    lin_width = head_own.shape[1]
    head_swap = swap_section(jnp.concatenate([head_own, widened((small, give_routes))], axis=1))
    got_routes = head_swap[:rows, lin_width + routes_at : lin_width + routes_at + top].astype(jnp.int32)
    both_routes = jnp.where(
        is_first,
        jnp.concatenate([my_routes, got_routes], axis=1),
        jnp.concatenate([got_routes, my_routes], axis=1),
    )
    tail_cols = jnp.where(is_first, small, head_swap[:, lin_width : lin_width + small.shape[1]])
    head_got = jnp.concatenate(
        [jnp.where(is_first, head_own, head_swap[:, :lin_width]), widened((tail_cols, both_routes))], axis=1
    )
    part_ff = w_gate.shape[3] // 2
    pieces = []
    for part, axis in ((w_gate, 1), (w_up, 1), (w_down, 0)):
        chosen = lax.dynamic_index_in_dim(part[0], flip, 0, keepdims=False)
        pieces.append(lax.dynamic_slice_in_dim(chosen, core * part_ff, part_ff, axis))
    pieces, head_got = lax.optimization_barrier((pieces, head_got))
    crossed_y = [swap_section(pieces[0]), None, None]
    last_grad = own_batch(cotangent[:, 0])
    head_got, last_blocks = lax.optimization_barrier((head_got, rel_gather(last_grad)))
    head_parts, crossed_y[0] = lax.optimization_barrier((rel_gather(head_got), crossed_y[0]))
    head_block = stacked_parts(head_parts)
    tiles = head_parts
    crossed_y[1:] = [swap_section(value) for value in pieces[1:]]
    first = fold_id * local
    numbers = first + (jnp.arange(local, dtype=jnp.int32) ^ flip)
    scalars = [
        jnp.concatenate([jnp.stack([(section == layer).astype(jnp.int32), flip]), numbers]).astype(jnp.int32)
        for layer in range(2)
    ]
    first_tail = head_block[:, lin_width:]
    out_block = of_first(column_share(w_out[0]))
    head_block, out_block = lax.optimization_barrier((head_block, out_block))
    out_block = stacked_rows(out_block)
    group_in = attention_in(token_group.astype(F32), first_tail[:, expert_count])[2]
    first_lin = share_back(
        mm(group_in, head_block[:, :lin_width]).astype(BF16).reshape(replicas, rows, lin_width)
    )

    def first_out(mixed_low):
        group = jnp.concatenate(group_rows(mixed_low), axis=0)
        made = mm(group, out_block).astype(BF16)
        return share_back(made.reshape(replicas, rows, -1))

    shard = jnp.concatenate([joined, jnp.pad(small, ((0, 0), (0, HEAD - small.shape[1]))), w_out[0]], axis=1)
    share = depth // (2 * replicas)
    keep = lax.dynamic_slice_in_dim(shard, (section * replicas + replica) * share, share, 0)
    give = lax.dynamic_slice_in_dim(shard, ((1 - section) * replicas + replica) * share, share, 0)
    give, _ = lax.optimization_barrier((give, head_got))
    got = swap_section(give)

    def whole_weights(layer, keep, got):
        piece = jnp.where(section == layer, keep, got)
        full = lax.all_gather(piece, (F_AX, S_AX, R_AX), axis=0, tiled=True)
        tail = full[:, split : split + LANES]
        held["full"] = full
        return tail[:, expert_count : expert_count + 2].T, full[:, :split], full[:, split + LANES :], tail

    first_w = (
        first_tail[:, expert_count : expert_count + 2].T, None, None, first_tail
    )
    size = dict(
        folds=folds, local=local, rows=rows, parts=2, width=tokens.shape[3], ff=w_gate.shape[3],
        capacity=capacity, top=top, tile_at=lin_width // LANES,
    )

    lengths = own_batch(seq_lengths[:, 0])
    position = fold_id * rows + jnp.arange(rows, dtype=jnp.int32)
    order = (fold_id - jnp.arange(folds)) % folds
    key_pos = (order[:, None] * rows + jnp.arange(rows)[None, :]).reshape(-1).astype(jnp.int32)
    segment, offset = layout(lengths, position)
    key_seg, _ = layout(lengths, key_pos)
    freq = ROPE_BASE ** (-2.0 * jnp.arange(HEAD // 2, dtype=F32) / HEAD)
    angles = offset[:, None] * freq
    angles = jnp.concatenate([angles, angles], axis=1)[:, None, :]
    common = dict(
        cos=jnp.cos(angles), sin=jnp.sin(angles), groups=kv_width // HEAD, size=size,
        experts=expert_count,
        allowed=(segment[:, None] == key_seg[None, :]) & (key_pos[None, :] <= position[:, None]),
    )

    def first_mixed(tied_lin, tied, attn_in, mixed_low):
        gate_x, up_y = tied
        held["second"] = whole_weights(1, *tied_lin)
        return (crossed_y[0], up_y), (gate_x,)

    def first_moe(moe_in, own, more):
        same, cross = more
        same, cross, moe_in = lax.optimization_barrier(((*same, crossed_y[2]), cross, moe_in))
        cross = [*cross, swap_xor(same[1], 2), swap_xor(same[2], 2)]
        flat = []
        for one, two in zip(same, cross):
            flat += [one, swap_core(one), two, swap_core(two)]
        return moe_in, (own, flat), ()

    held = {}
    first_value, first_kept, experts_w, _ = layer_forward(
        my_tokens, first_w, (w_gate[0], w_up[0], w_down[0]), common, tiles, routes_at, scalars[0],
        dict(router=(head_block, lin_width // LANES), lin=(keep, got), kv=(swap_xor(crossed_y[0], 2), crossed_y[1]), mixed=first_mixed, moe=first_moe),
        first_lin, first_out,
    )
    head_share, out_share, _ = lax.optimization_barrier(
        (head_block[:, :lin_width], out_block, first_kept["moe"][1])
    )
    weights_first = (
        first_w[0], lax.all_gather(head_share, R_AX, axis=0), lax.all_gather(out_share, R_AX, axis=0), first_tail
    )

    second_w = held["second"]

    def left_pair(attn_in, mixed_low):
        pair = (
            jnp.concatenate([first_kept["attn_in"], first_kept["mixed_low"]], axis=1),
            jnp.concatenate([attn_in, mixed_low], axis=1),
        )
        return own_layer(pair), swap_section(other_layer(pair))

    second_value, second_kept, _, tied = layer_forward(
        first_value, second_w, experts_w, common, tiles, routes_at + top, scalars[1],
        dict(
            mixed=lambda one, two, attn_in, mixed_low: (attn_in, mixed_low),
            moe=lambda moe_in, own, more: (moe_in, own, (left_pair(*more), weights_first)),
            last=True, router=(held["full"], split // LANES),
        ),
    )
    left_rows, weights_first = tied
    second_parts, second_finish = second_value
    left_rows = jnp.concatenate(left_rows, axis=0)
    kept, weights = [first_kept, second_kept], [weights_first, second_w]

    half = local // 2

    def chip_rows(pair):
        chip = []
        for value in pair:
            keep = lax.dynamic_slice_in_dim(value, (core ^ flip) * half, half, 0)
            give = lax.dynamic_slice_in_dim(value, (1 - (core ^ flip)) * half, half, 0)
            got = swap_core(give)
            chip.append(jnp.concatenate([keep, got], axis=1))
        return chip

    chips = replicas // 2

    def all_x(value):
        return [swap_xor(value, bit) for bit in range(2, replicas, 2)]

    def by_order(value, others):
        whole = jnp.zeros((chips,) + value.shape, value.dtype)
        for at, part in enumerate([value] + others):
            whole = lax.dynamic_update_index_in_dim(whole, part, (replica // 2) ^ at, 0)
        return whole

    def flat_rows(whole):
        return jnp.moveaxis(whole, 1, 0).reshape(half, -1, whole.shape[-1])

    x_chip = chip_rows([state["moe"][0] for state in kept])
    x_mine, x_give = own_layer(x_chip), other_layer(x_chip)
    def both_rows(pair):
        return jnp.concatenate([own_layer(pair), swap_section(other_layer(pair))], axis=0)

    def own_columns(value):
        width = value.shape[1] // replicas
        parts = []
        for bit in range(replicas):
            piece = lax.dynamic_slice_in_dim(value, (replica ^ bit) * width, width, 1)
            parts.append(piece if bit == 0 else swap_xor(piece, bit))
        return jnp.stack(parts)

    def fold_sum(left, right, extra):
        total = mm_tn(left, right).astype(BF16)
        if extra is not None:
            total = total.reshape(folds, -1, total.shape[1])
            total = jnp.concatenate([total, extra], axis=1).reshape(-1, total.shape[2])
        return total

    def late_part(total, tie):
        if tie == ():
            return lax.psum_scatter(total, F_AX, scatter_dimension=0, tiled=True)
        else:
            step = total.shape[0] // folds
            mine = rel_scatter(
                [
                    lax.dynamic_slice_in_dim(total, ((fold_id - k) % folds) * step, step, 0)
                    for k in range(folds)
                ]
            ).astype(BF16)
        return lax.optimization_barrier((mine, tie))

    def spread_rows(mine):
        whole = jnp.zeros((replicas,) + mine.shape, BF16)
        for bit, part in enumerate(group_rows(mine)):
            whole = lax.dynamic_update_index_in_dim(whole, part, replica ^ bit, 0)
        return whole

    def side_by_side(value):
        return jnp.concatenate([value[j].astype(F32) for j in range(replicas)], axis=1)

    left_whole = group_rows(left_rows)
    model = tokens.shape[3]
    piece = model // (folds * replicas)
    count = expert_count + 1
    tall = -(-count // 16) * 16

    def with_small(grad_attn, small):
        value = small.reshape(count, folds, replicas, piece)
        value = jnp.transpose(value, (0, 2, 1, 3)).reshape(count, model)
        return jnp.concatenate([grad_attn, jnp.pad(value, ((0, tall - count), (0, 0)))], axis=0)

    def last_rows(grad_expert):
        held["rows"] = chip_rows([grad_expert])[0]
        return left_whole, stacked_parts(second_parts)

    def two(value):
        middle_row = value.shape[1] // 2
        return value[:, :middle_row], value[:, middle_row:]

    def joined_rows(one, other):
        return [jnp.concatenate(pair, axis=1) for pair in zip(one, other)]

    def last_attn(grad_attn, small, sent):
        held["attn"] = with_small(grad_attn, small)
        give_one, give_two = two(x_give)
        return swap_section(give_one), give_two, sent[1]

    def last_later(sent, crossed):
        got_one, give_two, stack = crossed
        return sent[0], stack, got_one, swap_section(give_two), all_x(got_one), all_x(x_mine)

    def first_rows(grad_expert):
        chip = (chip_rows([grad_expert])[0], held["rows"])
        mine = own_layer(chip)
        return mine, all_x(mine), swap_section(other_layer(chip)), x_own, second_stack

    def first_attn(grad_attn, small, sent):
        *sent, stack = sent
        held["second_sum"] = lax.psum_scatter(stack, F_AX, scatter_dimension=0, tiled=True)
        return both_rows((with_small(grad_attn, small), held["attn"])), sent

    def first_later(sent, crossed):
        right_out, (mine, mine_x, got, x_own) = crossed
        g_own = by_order(mine, mine_x)
        return x_own, g_own, [expert_middle(x_own[i], flat_rows(g_own)[i], *[w[i] for w in mine_w]) for i in range(half)], got, own_columns(right_out)

    grads, grad_lin = [None, None], [None, None]
    grads[1], grad_lin[1], (left_whole, second_stack, x_got, x_got_two, x_got_x, x_mine_x), _ = layer_backward(
        last_grad, kept[1], weights[1], experts_w, common, scalars[1], (),
        dict(rows=last_rows, attn=last_attn, later=last_later, blocks=last_blocks),
    )
    x_own = flat_rows(by_order(x_mine, x_mine_x))
    x_own = [x_own[i] for i in range(half)]
    mine_w = [lax.dynamic_slice_in_dim(part[0], core * half, half, 0) for part in (w_gate, w_up, w_down)]
    grads[0], grad_lin[0], later, x_got_two_x = layer_backward(
        grads[1], kept[0], weights[0], experts_w, common, scalars[0], all_x(x_got_two),
        dict(rows=first_rows, attn=first_attn, later=first_later),
    )
    x_own, g_own, middle_own, got, right_out = later
    (x_got,) = joined_rows([x_got], [x_got_two])
    x_got_x = joined_rows(x_got_x, x_got_two_x)
    left_whole = jnp.concatenate(left_whole, axis=0)
    right_out = right_out.reshape(replicas, 2, rows + tall, -1)
    extra = jnp.sum(right_out[:, :, rows:].astype(F32), axis=(0, 1)).reshape(tall, folds, piece)
    extra = jnp.pad(
        jnp.transpose(extra, (1, 0, 2)), ((0, 0), (0, 0), (0, right_out.shape[3] - piece))
    ).astype(BF16)
    right_out = right_out[:, :, :rows].reshape(-1, right_out.shape[3])
    out_shard = late_part(fold_sum(left_whole[:, model:], right_out, extra), ())
    lin_rows, second_sum = lax.optimization_barrier((both_rows(grad_lin), held["second_sum"]))
    right, got = lax.optimization_barrier((own_columns(lin_rows), got))
    got_x = all_x(got)
    g_got, x_got = by_order(got, got_x), by_order(x_got, x_got_x)
    shard = fold_sum(left_whole[:, :model], right.reshape(-1, right.shape[2]), None)
    shard, (middle_own, x_own, first_value, grads, second_sum) = lax.optimization_barrier(
        (shard, (middle_own, x_own, first_value, grads, second_sum))
    )
    x_got = [flat_rows(x_got)[i] for i in range(half)]
    g_own, g_got = [[flat_rows(value)[i] for i in range(half)] for value in (g_own, g_got)]
    middle_got = [expert_middle(x_got[i], g_got[i], *[w[i] for w in mine_w]) for i in range(half)]

    shard, (middle_got, out_shard) = late_part(shard, (middle_got, out_shard))
    shard, out_shard = spread_rows(shard), spread_rows(out_shard)
    made = []
    for i in range(half):
        inner, gate, up = zip(middle_own[i], middle_got[i])
        made.append(
            (
                (mm_tn(x_own[i], gate[0]) + mm_tn(x_got[i], gate[1])).astype(BF16),
                (mm_tn(x_own[i], up[0]) + mm_tn(x_got[i], up[1])).astype(BF16),
                (mm_tn(inner[0], g_own[i]) + mm_tn(inner[1], g_got[i])).astype(BF16),
            )
        )
    outs = [first_value, second_finish([second_sum])]
    small = side_by_side(out_shard[:, depth:, :piece])
    out_shard = side_by_side(out_shard[:, :depth])
    shard = side_by_side(shard)
    gain_one = jnp.sum(shard * joined.astype(F32), axis=1) / gains[0, 0].astype(F32)
    expert_out = []
    for slot in range(3):
        keep = jnp.stack([one[slot] for one in made])
        got = swap_core(keep)
        both = jnp.concatenate(
            [jnp.where(core == 0, keep, got), jnp.where(core == 0, got, keep)], axis=0
        )
        expert_out.append(both.astype(F32)[None])
    layer_outputs = both_batches(outs)
    input_grads = both_batches(grads)
    return (
        layer_outputs[None, :, None],
        input_grads[None, :, None],
        jnp.stack([gain_one, small[expert_count]])[None],
        shard[None, :, :q_width],
        shard[None, :, q_width : q_width + kv_width],
        shard[None, :, q_width + kv_width : split],
        out_shard[None],
        small[:expert_count].T[None],
        expert_out[0],
        expert_out[1],
        expert_out[2],
    )


def solution(mesh):
    acts = P(None, R_AX, F_AX, None)
    rows = P(S_AX, F_AX, None)
    expert = P(S_AX, F_AX, None, None)
    stacked = P(S_AX, None, R_AX, F_AX, None)
    gain = P(S_AX, None, F_AX)
    return jax.shard_map(
        body,
        mesh=mesh,
        in_specs=(acts, acts, P(None, R_AX, None), stacked, gain)
        + (rows,) * 5
        + (expert,) * 3,
        out_specs=(stacked, stacked, gain) + (rows,) * 5 + (expert,) * 3,
        check_vma=False,
    )
```

```python
import functools

import jax
import jax.numpy as jnp
from jax import lax
from jax.experimental import pallas as pl
from jax.experimental.pallas import tpu as pltpu
from jax.sharding import PartitionSpec as P

HEAD = 128
ROPE_BASE = 1000000.0
EPS = 1e-06
MASKED = -1e30
F32 = jnp.float32
BF16 = jnp.bfloat16
S_AX, F_AX, R_AX = "section", "fsdp", "replica"
HIGHEST = lax.Precision.HIGHEST
LANES = 128
GELU_C = 0.7978845608028654
GELU_A = 0.044715


def dot(a, b):
    return lax.dot_general(a, b, (((1,), (0,)), ((), ())), preferred_element_type=F32)


def dot_nt(a, b):
    return lax.dot_general(a, b, (((1,), (1,)), ((), ())), preferred_element_type=F32)


def dot_tn(a, b):
    return lax.dot_general(a, b, (((0,), (0,)), ((), ())), preferred_element_type=F32)


def gelu_parts(x):
    t = jnp.tanh(GELU_C * (x + GELU_A * x * x * x))
    value = 0.5 * x * (1.0 + t)
    slope = 0.5 * (1.0 + t) + 0.5 * x * (1.0 - t * t) * GELU_C * (1.0 + 3.0 * GELU_A * x * x)
    return value, slope


def lane_is(shape, number):
    return lax.broadcasted_iota(jnp.int32, shape, 1) == number


def masked_mix(logits, mask):
    kept = jnp.where(mask > 0.0, logits, -1e30)
    expo = jnp.exp(kept - jnp.max(kept, axis=1, keepdims=True)) * mask
    return expo / jnp.sum(expo, axis=1, keepdims=True)


def one_hot(slots_ref, block, step, capacity):
    rows = slots_ref.shape[2]
    place = lax.broadcasted_iota(jnp.int32, (capacity, rows), 0)
    return place == slots_ref[block, step : step + 1, :]


def route_mask(tile, at, top):
    lane = lax.broadcasted_iota(jnp.int32, tile.shape, 1).astype(F32)
    named = tile.astype(F32)
    hit = lane == named[:, at : at + 1]
    for k in range(1, top):
        hit = hit | (lane == named[:, at + k : at + k + 1])
    return jnp.where(hit, 1.0, 0.0)


def weight_copies(scalars, own, pieces, buffers, sems):
    own_g, own_u, own_d = own
    parts = len(pieces[0][0])
    ff = own_g.shape[2] // parts
    is_own, flip = scalars[0], scalars[1]
    waits = {}
    for step in range(len(pieces[0])):
        for part in range(parts):
            expert = step ^ flip
            cols = pl.ds(part * ff, ff)
            sources = (own_g.at[expert, :, cols], own_u.at[expert, :, cols], own_d.at[expert, cols, :])
            for kind in range(3):
                target = buffers[kind].at[step, part]
                sem = sems.at[kind, step, part]

                @pl.when(is_own == 1)
                def _(source=sources[kind], target=target, sem=sem):
                    pltpu.make_async_copy(source, target, sem).start()

                @pl.when(is_own == 0)
                def _(source=pieces[kind][step][part], target=target, sem=sem):
                    pltpu.make_async_copy(source, target, sem).start()

                waits[kind, step, part] = pltpu.make_async_copy(
                    pieces[kind][step][part], target, sem
                )
    return waits


def split_refs(refs, counts):
    out, at = [], 0
    for count in counts:
        out.append(refs[at : at + count])
        at += count
    return out


def moe_fwd_kernel(folds, local, parts, capacity, routes_at, top, *refs):
    (scalars, router), tiles, blocks, own, flat, outs, partials, scratch = split_refs(
        refs, (2, folds, folds, 3, 3 * local * parts, 7, folds, 4)
    )
    scalars_ref = scalars
    picked_ref, gate_ref, up_ref, made_ref, grows_ref, slots, mix_ref = outs
    buf_g, buf_u, buf_d, sems = scratch
    pieces = [
        [[flat[(kind * local + step) * parts + part] for part in range(parts)] for step in range(local)]
        for kind in range(3)
    ]
    waits = weight_copies(scalars_ref, own, pieces, (buf_g, buf_u, buf_d), sems)
    rows = blocks[0].shape[0]
    width = blocks[0].shape[1]
    ff = buf_g.shape[3]
    square = (rows, rows)
    earlier = jnp.where(
        lax.broadcasted_iota(jnp.int32, square, 0) < lax.broadcasted_iota(jnp.int32, square, 1), 1.0, 0.0
    ).astype(BF16)
    same = jnp.where(
        lax.broadcasted_iota(jnp.int32, square, 0) == lax.broadcasted_iota(jnp.int32, square, 1), 1.0, 0.0
    ).astype(BF16)
    for k in range(folds):
        mask = route_mask(tiles[k][...], routes_at, top)
        mix = masked_mix(dot(blocks[k][...], router[...]), mask)
        if k == 0:
            mix_ref[...] = mix
        low = mask.astype(BF16)
        rank = dot_tn(low, earlier)
        named = dot_tn(low, same)
        place = jnp.where(named > 0.5, rank, -1.0)
        number = lax.broadcasted_iota(jnp.int32, place.shape, 0)
        for step in range(local):
            row = jnp.sum(jnp.where(number == scalars_ref[2 + step], place, 0.0), axis=0, keepdims=True)
            slots[k, step : step + 1, :] = row.astype(jnp.int32)
        for step in range(local):
            pick = one_hot(slots, k, step, capacity)
            at = pl.ds(k * capacity, capacity)
            picked_ref[step, at, :] = dot(
                jnp.where(pick, 1.0, 0.0).astype(BF16), blocks[k][...]
            ).astype(BF16)
            grows_ref[step, at, :] = lax.dot_general(
                jnp.where(pick, 1.0, 0.0), mix, (((1,), (0,)), ((), ())),
                precision=HIGHEST, preferred_element_type=F32,
            )
    for step in range(local):
        for part in range(parts):
            for kind in range(3):
                waits[kind, step, part].wait()
            cols = pl.ds(part * ff, ff)
            x = picked_ref[step]
            gate = dot(x, buf_g[step, part])
            up = dot(x, buf_u[step, part])
            gate_ref[step, :, cols] = gate
            up_ref[step, :, cols] = up
            inner = (gelu_parts(gate)[0] * up).astype(BF16)
            term = dot(inner, buf_d[step, part])
            made = term if part == 0 else made + term
        made_ref[step] = made.astype(BF16)
    for k in range(folds):
        at = pl.ds(k * capacity, capacity)
        picks, weighted = [], []
        for step in range(local):
            gates = grows_ref[step, at, :]
            own_lane = lane_is(gates.shape, scalars_ref[2 + step])
            factor = jnp.sum(jnp.where(own_lane, gates, 0.0), axis=1, keepdims=True)
            picks.append(jnp.where(one_hot(slots, k, step, capacity), 1.0, 0.0).astype(BF16))
            weighted.append((made_ref[step, at, :].astype(F32) * factor).astype(BF16))
        partials[k][...] = dot_tn(
            jnp.concatenate(picks, axis=0), jnp.concatenate(weighted, axis=0)
        ).astype(BF16)


def moe_bwd_kernel(folds, local, parts, capacity, *refs):
    (scalars, slots, gate_ref, up_ref, made_ref, grows_ref), blocks, own, flat, (ge_ref,), partials, scratch = split_refs(
        refs, (6, folds, 3, 3 * local * parts, 1, folds, 6)
    )
    buf_g, buf_u, buf_d, sems, dx_ref, dots_ref = scratch
    pieces = [
        [[flat[(kind * local + step) * parts + part] for part in range(parts)] for step in range(local)]
        for kind in range(3)
    ]
    waits = weight_copies(scalars, own, pieces, (buf_g, buf_u, buf_d), sems)
    ff = buf_g.shape[3]
    for step in range(local):
        for k in range(folds):
            at = pl.ds(k * capacity, capacity)
            pick = jnp.where(one_hot(slots, k, step, capacity), 1.0, 0.0).astype(BF16)
            dout = dot(pick, blocks[k][...])
            gates = grows_ref[step, at, :]
            own_lane = lane_is(gates.shape, scalars[2 + step])
            factor = jnp.sum(jnp.where(own_lane, gates, 0.0), axis=1, keepdims=True)
            value = jnp.sum(dout * made_ref[step, at, :].astype(F32), axis=1, keepdims=True)
            lane = lax.broadcasted_iota(jnp.int32, gates.shape, 1)
            number = scalars[2 + step]
            dots_ref[step, at, :] = jnp.where(
                (lane == number) | (lane == number + LANES // 2), value, 0.0
            )
            ge_ref[step, at, :] = (dout * factor).astype(BF16)
    for step in range(local):
        ge = ge_ref[step]
        for part in range(parts):
            for kind in range(3):
                waits[kind, step, part].wait()
            cols = pl.ds(part * ff, ff)
            grad_inner = dot_nt(ge, buf_d[step, part])
            gate = gate_ref[step, :, cols]
            up = up_ref[step, :, cols]
            value, slope = gelu_parts(gate)
            grad_gate = (grad_inner * up * slope).astype(BF16)
            grad_up = (grad_inner * value).astype(BF16)
            term = dot_nt(grad_gate, buf_g[step, part]) + dot_nt(grad_up, buf_u[step, part])
            total = term if part == 0 else total + term
        dx_ref[step] = total.astype(BF16)
    for k in range(folds):
        at = pl.ds(k * capacity, capacity)
        hot = [one_hot(slots, k, step, capacity) for step in range(local)]
        picks = jnp.concatenate([jnp.where(one, 1.0, 0.0) for one in hot], axis=0)
        width = ge_ref.shape[2]
        partials[k][:, :width] = dot_tn(
            picks.astype(BF16), jnp.concatenate([dx_ref[step, at, :] for step in range(local)], axis=0)
        ).astype(BF16)
        dots = lax.dot_general(
            picks, jnp.concatenate([dots_ref[step, at, :] for step in range(local)], axis=0),
            (((0,), (0,)), ((), ())), precision=HIGHEST, preferred_element_type=F32,
        )
        high = dots.astype(BF16).astype(F32)
        lane = lax.broadcasted_iota(jnp.int32, dots.shape, 1)
        partials[k][:, width:] = jnp.where(lane < LANES // 2, high, dots - high).astype(BF16)


def vmem(count):
    return [pl.BlockSpec(memory_space=pltpu.VMEM)] * count


def anywhere(count):
    return [pl.BlockSpec(memory_space=pl.ANY)] * count


def weight_scratch(own, local, parts):
    width, ff = own[0].shape[1], own[0].shape[2] // parts
    return [
        pltpu.VMEM((local, parts, width, ff), BF16),
        pltpu.VMEM((local, parts, width, ff), BF16),
        pltpu.VMEM((local, parts, ff, width), BF16),
        pltpu.SemaphoreType.DMA((3, local, parts)),
    ]


def cost(rows, width, ff, products):
    return pl.CostEstimate(
        flops=2 * rows * width * ff * products, bytes_accessed=2 * 3 * width * ff * 2 + 8 * rows * width,
        transcendentals=rows * ff,
    )


def moe_fwd_call(
    scalars, tiles, routes_at, router, blocks, own, flat, folds, local, rows, parts, width, ff, capacity, top, tile_at
):
    router, router_at = router
    picked_rows = folds * capacity
    shapes = [
        jax.ShapeDtypeStruct((local, picked_rows, width), BF16),
        jax.ShapeDtypeStruct((local, picked_rows, ff), F32),
        jax.ShapeDtypeStruct((local, picked_rows, ff), F32),
        jax.ShapeDtypeStruct((local, picked_rows, width), BF16),
        jax.ShapeDtypeStruct((local, picked_rows, LANES), F32),
        jax.ShapeDtypeStruct((folds, local, rows), jnp.int32),
        jax.ShapeDtypeStruct((rows, LANES), F32),
    ] + [jax.ShapeDtypeStruct((rows, width), BF16)] * folds
    out = pl.pallas_call(
        functools.partial(moe_fwd_kernel, folds, local, parts, capacity, routes_at, top),
        out_shape=shapes,
        in_specs=[
            pl.BlockSpec(memory_space=pltpu.SMEM),
            pl.BlockSpec((router.shape[0], LANES), lambda i: (0, router_at)),
        ]
        + [pl.BlockSpec((rows, LANES), lambda i: (0, tile_at))] * folds
        + vmem(folds) + anywhere(3 + len(flat)),
        grid=(1,),
        out_specs=vmem(len(shapes)),
        scratch_shapes=weight_scratch(own, local, parts),
        cost_estimate=cost(local * picked_rows, width, ff, 3),
        compiler_params=pltpu.CompilerParams(vmem_limit_bytes=56 << 20),
    )(scalars, router, *tiles, *blocks, *own, *flat)
    return out[:7], out[7:]


def moe_bwd_call(scalars, kept, blocks, own, flat, folds, local, rows, parts, width, ff, capacity, top, tile_at):
    _, gate_pre, up_pre, made, gate_rows, slots, _ = kept
    picked_rows = folds * capacity
    shapes = [jax.ShapeDtypeStruct((local, picked_rows, width), BF16)] + [
        jax.ShapeDtypeStruct((rows, width + LANES), BF16)
    ] * folds
    out = pl.pallas_call(
        functools.partial(moe_bwd_kernel, folds, local, parts, capacity),
        out_shape=shapes,
        in_specs=[pl.BlockSpec(memory_space=pltpu.SMEM)]
        + vmem(5 + folds) + anywhere(3 + len(flat)),
        out_specs=vmem(len(shapes)),
        scratch_shapes=weight_scratch(own, local, parts)
        + [pltpu.VMEM((local, picked_rows, width), BF16), pltpu.VMEM((local, picked_rows, LANES), F32)],
        cost_estimate=cost(local * picked_rows, width, ff, 3),
        compiler_params=pltpu.CompilerParams(vmem_limit_bytes=56 << 20),
    )(scalars, slots, gate_pre, up_pre, made, gate_rows, *blocks, *own, *flat)
    return out[0], out[1:]


def mm(a, b):
    return jnp.dot(a, b, preferred_element_type=F32)


def mm_nt(a, b):
    return lax.dot_general(a, b, (((1,), (1,)), ((), ())), preferred_element_type=F32)


def mm_shares(a, shares):
    if shares.ndim == 2:
        return mm_nt(a, shares)
    width = shares.shape[2]
    return sum(mm_nt(a[:, j * width : (j + 1) * width], shares[j]) for j in range(shares.shape[0]))


def mm_tn(a, b):
    return lax.dot_general(a, b, (((0,), (0,)), ((), ())), preferred_element_type=F32)


def ein(spec, a, b):
    return jnp.einsum(spec, a, b, preferred_element_type=F32)


def rel_gather(value):
    folds = lax.axis_size(F_AX)
    parts = [value]
    for k in range(1, folds):
        parts.append(lax.ppermute(value, F_AX, [(i, (i + k) % folds) for i in range(folds)]))
    return parts


def rel_scatter(parts):
    folds = lax.axis_size(F_AX)
    total = parts[0].astype(F32)
    for k in range(1, folds):
        got = lax.ppermute(parts[k], F_AX, [(i, (i - k) % folds) for i in range(folds)])
        total = total + got.astype(F32)
    return total


def send_back(parts):
    folds = lax.axis_size(F_AX)
    return [parts[0]] + [
        lax.ppermute(parts[k], F_AX, [(i, (i - k) % folds) for i in range(folds)]) for k in range(1, folds)
    ]


def add_up(parts):
    total = parts[0].astype(F32)
    for part in parts[1:]:
        total = total + part.astype(F32)
    return total


def swap_section(value):
    return lax.ppermute(value, S_AX, [(0, 1), (1, 0)])


def swap_core(value):
    count = lax.axis_size(R_AX)
    return lax.ppermute(value, R_AX, [(i, i ^ 1) for i in range(count)])


def rope_turn(values, cos, sin):
    half = HEAD // 2
    turned = jnp.concatenate([-values[..., half:], values[..., :half]], axis=-1)
    return values * cos + turned * sin


def rope_back(grads, cos, sin):
    half = HEAD // 2
    scaled = grads * sin
    turned = jnp.concatenate([scaled[..., half:], -scaled[..., :half]], axis=-1)
    return grads * cos + turned


def layout(lengths, position):
    bounds = jnp.cumsum(lengths)
    passed = (position[:, None] >= bounds[None, :]).astype(jnp.int32)
    segment = jnp.sum(passed, axis=1)
    start = jnp.sum(passed * lengths[None, :], axis=1)
    return segment, (position - start).astype(F32)


def gated(gate, up):
    return jax.nn.gelu(gate) * up


def attention_in(hidden, gain):
    scale = lax.rsqrt(jnp.mean(hidden * hidden, axis=1, keepdims=True) + EPS)
    normed = hidden * scale
    return scale, normed, (normed * gain.astype(F32)).astype(BF16)


def turn_heads(lin, common, kv_width):
    rows = lin.shape[0]
    q_width = lin.shape[1] - 2 * kv_width
    turned = rope_turn(
        lin[:, : q_width + kv_width].astype(F32).reshape(rows, -1, HEAD), common["cos"], common["sin"]
    ).astype(BF16).reshape(rows, -1)
    kv = jnp.concatenate([turned[:, q_width:], lin[:, q_width + kv_width :].astype(BF16)], axis=1)
    return turned[:, :q_width], kv


def grouped_heads(value, groups):
    rows = value.shape[0]
    return value.reshape(rows, groups, -1, HEAD)


def attend(query, kv_all, allowed, groups):
    keys = kv_all[:, : groups * HEAD].reshape(-1, groups, HEAD)
    values = kv_all[:, groups * HEAD :].reshape(-1, groups, HEAD)
    raw = ein("tgha,sga->ghts", grouped_heads(query, groups), keys) * HEAD ** (-0.5)
    scores = jnp.where(allowed[None, None], raw, MASKED)
    top = jnp.max(scores, axis=3, keepdims=True)
    expo = jnp.exp(scores - top)
    probs = expo / jnp.sum(expo, axis=3, keepdims=True)
    mixed = ein("ghts,sga->tgha", probs.astype(BF16), values)
    return mixed.reshape(query.shape), probs


def attend_back(grad_mixed, mixed, probs, query, kv_all, groups):
    rows = query.shape[0]
    keys = kv_all[:, : groups * HEAD].reshape(-1, groups, HEAD)
    values = kv_all[:, groups * HEAD :].reshape(-1, groups, HEAD)
    grad_grouped = grouped_heads(grad_mixed, groups)
    delta = jnp.sum(
        grad_grouped.astype(F32) * grouped_heads(mixed, groups), axis=3
    )
    delta = jnp.transpose(delta, (1, 2, 0))[..., None]
    grad_probs = ein("tgha,sga->ghts", grad_grouped, values)
    grad_scores = (probs * (grad_probs - delta)).astype(BF16)
    score_scale = HEAD ** (-0.5)
    grad_query = (ein("ghts,sga->tgha", grad_scores, keys) * score_scale).reshape(rows, -1, HEAD)
    grad_key = ein("ghts,tgha->sga", grad_scores, grouped_heads(query, groups)) * score_scale
    grad_value = ein("ghts,tgha->sga", probs.astype(BF16), grad_grouped)
    count = kv_all.shape[0]
    grad_kv = jnp.concatenate(
        [grad_key.reshape(count, -1), grad_value.reshape(count, -1)], axis=1
    ).astype(BF16)
    return grad_query, grad_kv


def moe_forward(router, tiles, routes_at, scalars, experts_w, size, blocks):
    outs, partials = moe_fwd_call(
        scalars, tiles, routes_at, router, blocks, *experts_w, **size
    )
    return partials, outs


def moe_backward(blocks, kept, scalars, experts_w, size, tie, hooks):
    blocks, tied = lax.optimization_barrier((blocks, tie))
    grad_expert, partials = moe_bwd_call(scalars, kept, blocks, *experts_w, **size)
    sent = hooks["rows"](grad_expert)
    summed, sent = lax.optimization_barrier((rel_scatter(partials), sent))
    width = blocks[0].shape[1]
    tail = summed[:, width:]
    half = LANES // 2
    dots = tail[:, :half] + tail[:, half:]
    return summed[:, :width], jnp.pad(dots, ((0, 0), (0, half))), sent, tied


def layer_forward(layer_in, weights, experts_w, common, tiles, routes_at, scalars, tie, projected=None, out_product=None):
    gains, w_qkv, w_out, router = weights
    groups = common["groups"]
    hidden = layer_in.astype(F32)
    scale, normed, attn_in = attention_in(hidden, gains[0])
    lin = mm(attn_in, w_qkv) if projected is None else projected
    lin, tied_lin = lax.optimization_barrier((lin, tie.get("lin", ())))
    query, kv = turn_heads(lin, common, groups * HEAD)
    kv_all, tied_kv = lax.optimization_barrier(
        (jnp.concatenate(rel_gather(kv), axis=0), tie.get("kv", ()))
    )
    mixed, probs = attend(query, kv_all, common["allowed"], groups)
    mixed_low = mixed.astype(BF16)
    more = tie["mixed"](tied_lin, tied_kv, attn_in, mixed_low) if "mixed" in tie else ()
    mixed_low, more = lax.optimization_barrier((mixed_low, more))
    if out_product is None:
        residual = hidden + mm(mixed_low, w_out)
    else:
        residual = hidden + out_product(mixed_low).astype(F32)
    scale_two = lax.rsqrt(jnp.mean(residual * residual, axis=1, keepdims=True) + EPS)
    normed_two = residual * scale_two
    moe_in = (normed_two * gains[1].astype(F32)).astype(BF16)
    if "moe" in tie:
        moe_in, experts_w, more = tie["moe"](moe_in, experts_w, more)
    blocks, tied = lax.optimization_barrier((rel_gather(moe_in), more))
    parts, moe_kept = moe_forward(tie["router"], tiles, routes_at, scalars, experts_w, common["size"], blocks)
    finish = lambda got: (residual + add_up(got)).astype(BF16)
    out = finish(send_back(parts)) if "last" not in tie else (parts, finish)
    kept = dict(
        scale=scale, normed=normed, attn_in=attn_in, query=query, kv=kv,
        kv_all=kv_all, mixed=mixed, probs=probs, mixed_low=mixed_low, scale_two=scale_two,
        normed_two=normed_two, moe_in=moe_in, mix=moe_kept[6], moe=moe_kept,
    )
    return out, kept, experts_w, tied


def layer_backward(grad_low, kept, weights, experts_w, common, scalars, tie, hooks):
    gains, w_qkv, w_out, router = weights
    groups = common["groups"]
    grad_out = grad_low.astype(F32)
    rows = grad_out.shape[0]
    blocks = hooks["blocks"] if "blocks" in hooks else rel_gather(grad_low)
    grad_moe_in, dots, sent, tied = moe_backward(
        blocks, kept["moe"], scalars, experts_w, common["size"], tie, hooks
    )
    mix = kept["mix"]
    grad_logits = mix * (dots - jnp.sum(mix * dots, axis=1, keepdims=True))
    moe_in = kept["moe_in"]
    count = common["experts"]
    high = grad_logits.astype(BF16)
    rest = (grad_logits - high.astype(F32)).astype(BF16)
    both = mm_tn(jnp.concatenate([high[:, :count], rest[:, :count]], axis=1), moe_in)
    grad_router = both[:count] + both[count:]
    grad_moe_in = grad_moe_in + mm_nt(high, router) + mm_nt(rest, router)
    normed_two = kept["normed_two"]
    grad_norm = grad_moe_in * gains[1].astype(F32)
    grad_gain_two = jnp.sum(grad_moe_in * normed_two, axis=0)
    grad_mid = grad_out + kept["scale_two"] * (
        grad_norm - normed_two * jnp.mean(grad_norm * normed_two, axis=1, keepdims=True)
    )
    grad_attn = grad_mid.astype(BF16)
    small = jnp.concatenate([grad_router, grad_gain_two[None]], axis=0).astype(BF16)
    crossed = hooks["attn"](grad_attn, small, sent)
    grad_mixed = mm_shares(grad_attn, w_out).astype(BF16)
    grad_query, grad_kv = attend_back(
        grad_mixed, kept["mixed"], kept["probs"], kept["query"], kept["kv_all"], groups
    )
    grad_kv, crossed = lax.optimization_barrier((grad_kv, crossed))
    later = hooks["later"](sent, crossed)
    own = rel_scatter([grad_kv[k * rows : (k + 1) * rows] for k in range(lax.axis_size(F_AX))])
    own, later = lax.optimization_barrier((own, later))
    cos, sin = common["cos"], common["sin"]
    kv_width = groups * HEAD
    grad_lin = jnp.concatenate(
        [
            rope_back(grad_query, cos, sin).reshape(rows, -1),
            rope_back(own[:, :kv_width].reshape(rows, -1, HEAD), cos, sin).reshape(rows, -1),
            own[:, kv_width:],
        ],
        axis=1,
    ).astype(BF16)
    grad_attn_in = mm_shares(grad_lin, w_qkv)
    normed = kept["normed"]
    grad_norm = grad_attn_in * gains[0].astype(F32)
    grad_in = grad_mid + kept["scale"] * (
        grad_norm - normed * jnp.mean(grad_norm * normed, axis=1, keepdims=True)
    )
    return grad_in.astype(BF16), grad_lin, later, tied


def expert_middle(rows_in, grad_rows, gate_w, up_w, down_w):
    value, slope = gelu_parts(mm(rows_in, gate_w))
    up_pre = mm(rows_in, up_w)
    grad_inner = mm_nt(grad_rows, down_w)
    return (
        (value * up_pre).astype(BF16),
        (grad_inner * up_pre * slope).astype(BF16),
        (grad_inner * value).astype(BF16),
    )


def body(
    tokens, cotangent, seq_lengths, routes, gains, w_query, w_key, w_value, w_out, w_router, w_gate, w_up, w_down
):
    section = lax.axis_index(S_AX)
    is_first = section == 0
    fold_id = lax.axis_index(F_AX)
    replica = lax.axis_index(R_AX)
    core = replica % 2
    flip = (replica // 2) % 2
    folds, replicas = lax.axis_size(F_AX), lax.axis_size(R_AX)
    rows = tokens.shape[2]
    top = routes.shape[4]
    local = w_gate.shape[1]
    expert_count = w_router.shape[2]
    kv_width = w_key.shape[2]
    q_width = w_query.shape[2]
    capacity = rows * top // expert_count

    def own_batch(value):
        return lax.dynamic_index_in_dim(value, section, 0, keepdims=False)

    def swap_xor(value, bit):
        return lax.ppermute(value, R_AX, [(i, i ^ bit) for i in range(replicas)])

    def own_layer(pair):
        return jnp.where(is_first, pair[0], pair[1])

    def other_layer(pair):
        return jnp.where(is_first, pair[1], pair[0])

    def by_section(keep, got):
        return jnp.stack([jnp.where(is_first, keep, got), jnp.where(is_first, got, keep)])

    def both_batches(pair):
        return by_section(own_layer(pair), swap_section(other_layer(pair)))

    split = q_width + 2 * kv_width
    routes_at = HEAD // 4

    def widened(pieces):
        weights_part, routes_part = pieces
        routes_part = jnp.pad(routes_part.astype(BF16), ((0, weights_part.shape[0] - rows), (0, 0)))
        gap = jnp.zeros((weights_part.shape[0], routes_at - weights_part.shape[1]), BF16)
        whole = jnp.concatenate([weights_part, gap, routes_part], axis=1)
        return jnp.pad(whole, ((0, 0), (0, HEAD - whole.shape[1])))

    small = jnp.concatenate([w_router[0], gains[0].T], axis=1)
    my_routes = own_batch(routes[0, :, 0])
    give_routes = lax.dynamic_index_in_dim(routes[0, :, 0], 1 - section, 0, keepdims=False)
    joined = jnp.concatenate([w_query[0], w_key[0], w_value[0]], axis=1)
    depth = joined.shape[0]

    def column_share(value):
        width = value.shape[1] // replicas
        return lax.dynamic_slice_in_dim(value, replica * width, width, 1)

    def stacked_parts(parts):
        whole = jnp.zeros((folds,) + parts[0].shape, parts[0].dtype)
        for k, part in enumerate(parts):
            whole = lax.dynamic_update_index_in_dim(whole, part, (fold_id - k) % folds, 0)
        return whole.reshape((-1,) + parts[0].shape[1:])

    def stacked_rows(value):
        return stacked_parts(rel_gather(value))

    def of_first(value):
        return jnp.where(is_first, value, swap_section(value))

    def share_back(value):
        whole = jnp.zeros(value.shape, value.dtype)
        for bit in range(replicas):
            got = value[bit] if bit == 0 else swap_xor(value[bit], bit)
            whole = lax.dynamic_update_index_in_dim(whole, got, replica ^ bit, 0)
        return jnp.concatenate([whole[j] for j in range(replicas)], axis=1)

    def group_rows(value):
        parts = []
        for bit in range(0, replicas, 2):
            same = value if bit == 0 else swap_xor(value, bit)
            parts += [same, swap_core(same)]
        return parts

    my_tokens = own_batch(tokens[:, 0])
    token_group = jnp.concatenate(group_rows(my_tokens), axis=0)
    head_own = column_share(joined)
    lin_width = head_own.shape[1]
    head_swap = swap_section(jnp.concatenate([head_own, widened((small, give_routes))], axis=1))
    got_routes = head_swap[:rows, lin_width + routes_at : lin_width + routes_at + top].astype(jnp.int32)
    both_routes = jnp.where(
        is_first,
        jnp.concatenate([my_routes, got_routes], axis=1),
        jnp.concatenate([got_routes, my_routes], axis=1),
    )
    tail_cols = jnp.where(is_first, small, head_swap[:, lin_width : lin_width + small.shape[1]])
    head_got = jnp.concatenate(
        [jnp.where(is_first, head_own, head_swap[:, :lin_width]), widened((tail_cols, both_routes))], axis=1
    )
    part_ff = w_gate.shape[3] // 2
    pieces = []
    for part, axis in ((w_gate, 1), (w_up, 1), (w_down, 0)):
        chosen = lax.dynamic_index_in_dim(part[0], flip, 0, keepdims=False)
        pieces.append(lax.dynamic_slice_in_dim(chosen, core * part_ff, part_ff, axis))
    pieces, head_got = lax.optimization_barrier((pieces, head_got))
    crossed_y = [swap_section(pieces[0]), None, None]
    last_grad = own_batch(cotangent[:, 0])
    head_got, last_blocks = lax.optimization_barrier((head_got, rel_gather(last_grad)))
    head_parts, crossed_y[0] = lax.optimization_barrier((rel_gather(head_got), crossed_y[0]))
    head_block = stacked_parts(head_parts)
    tiles = head_parts
    crossed_y[1:] = [swap_section(value) for value in pieces[1:]]
    first = fold_id * local
    numbers = first + (jnp.arange(local, dtype=jnp.int32) ^ flip)
    scalars = [
        jnp.concatenate([jnp.stack([(section == layer).astype(jnp.int32), flip]), numbers]).astype(jnp.int32)
        for layer in range(2)
    ]
    first_tail = head_block[:, lin_width:]
    out_block = of_first(column_share(w_out[0]))
    head_block, out_block = lax.optimization_barrier((head_block, out_block))
    out_block = stacked_rows(out_block)
    group_in = attention_in(token_group.astype(F32), first_tail[:, expert_count])[2]
    first_lin = share_back(
        mm(group_in, head_block[:, :lin_width]).astype(BF16).reshape(replicas, rows, lin_width)
    )

    def first_out(mixed_low):
        group = jnp.concatenate(group_rows(mixed_low), axis=0)
        made = mm(group, out_block).astype(BF16)
        return share_back(made.reshape(replicas, rows, -1))

    shard = jnp.concatenate([joined, jnp.pad(small, ((0, 0), (0, HEAD - small.shape[1]))), w_out[0]], axis=1)
    share = depth // (2 * replicas)
    keep = lax.dynamic_slice_in_dim(shard, (section * replicas + replica) * share, share, 0)
    give = lax.dynamic_slice_in_dim(shard, ((1 - section) * replicas + replica) * share, share, 0)
    give, _ = lax.optimization_barrier((give, head_got))
    got = swap_section(give)

    def whole_weights(layer, keep, got):
        piece = jnp.where(section == layer, keep, got)
        full = lax.all_gather(piece, (F_AX, S_AX, R_AX), axis=0, tiled=True)
        tail = full[:, split : split + LANES]
        held["full"] = full
        return tail[:, expert_count : expert_count + 2].T, full[:, :split], full[:, split + LANES :], tail

    first_w = (
        first_tail[:, expert_count : expert_count + 2].T, None, None, first_tail
    )
    size = dict(
        folds=folds, local=local, rows=rows, parts=2, width=tokens.shape[3], ff=w_gate.shape[3],
        capacity=capacity, top=top, tile_at=lin_width // LANES,
    )

    lengths = own_batch(seq_lengths[:, 0])
    position = fold_id * rows + jnp.arange(rows, dtype=jnp.int32)
    order = (fold_id - jnp.arange(folds)) % folds
    key_pos = (order[:, None] * rows + jnp.arange(rows)[None, :]).reshape(-1).astype(jnp.int32)
    segment, offset = layout(lengths, position)
    key_seg, _ = layout(lengths, key_pos)
    freq = ROPE_BASE ** (-2.0 * jnp.arange(HEAD // 2, dtype=F32) / HEAD)
    angles = offset[:, None] * freq
    angles = jnp.concatenate([angles, angles], axis=1)[:, None, :]
    common = dict(
        cos=jnp.cos(angles), sin=jnp.sin(angles), groups=kv_width // HEAD, size=size,
        experts=expert_count,
        allowed=(segment[:, None] == key_seg[None, :]) & (key_pos[None, :] <= position[:, None]),
    )

    def first_mixed(tied_lin, tied, attn_in, mixed_low):
        gate_x, up_y = tied
        held["second"] = whole_weights(1, *tied_lin)
        return (crossed_y[0], up_y), (gate_x,)

    def first_moe(moe_in, own, more):
        same, cross = more
        same, cross, moe_in = lax.optimization_barrier(((*same, crossed_y[2]), cross, moe_in))
        cross = [*cross, swap_xor(same[1], 2), swap_xor(same[2], 2)]
        flat = []
        for one, two in zip(same, cross):
            flat += [one, swap_core(one), two, swap_core(two)]
        return moe_in, (own, flat), ()

    held = {}
    first_value, first_kept, experts_w, _ = layer_forward(
        my_tokens, first_w, (w_gate[0], w_up[0], w_down[0]), common, tiles, routes_at, scalars[0],
        dict(router=(head_block, lin_width // LANES), lin=(keep, got), kv=(swap_xor(crossed_y[0], 2), crossed_y[1]), mixed=first_mixed, moe=first_moe),
        first_lin, first_out,
    )
    head_share, out_share, _ = lax.optimization_barrier(
        (head_block[:, :lin_width], out_block, first_kept["moe"][1])
    )
    weights_first = (
        first_w[0], lax.all_gather(head_share, R_AX, axis=0), lax.all_gather(out_share, R_AX, axis=0), first_tail
    )

    second_w = held["second"]

    def left_pair(attn_in, mixed_low):
        pair = (
            jnp.concatenate([first_kept["attn_in"], first_kept["mixed_low"]], axis=1),
            jnp.concatenate([attn_in, mixed_low], axis=1),
        )
        return own_layer(pair), swap_section(other_layer(pair))

    second_value, second_kept, _, tied = layer_forward(
        first_value, second_w, experts_w, common, tiles, routes_at + top, scalars[1],
        dict(
            mixed=lambda one, two, attn_in, mixed_low: (attn_in, mixed_low),
            moe=lambda moe_in, own, more: (moe_in, own, (left_pair(*more), weights_first)),
            last=True, router=(held["full"], split // LANES),
        ),
    )
    left_rows, weights_first = tied
    second_parts, second_finish = second_value
    left_rows = jnp.concatenate(left_rows, axis=0)
    kept, weights = [first_kept, second_kept], [weights_first, second_w]

    half = local // 2

    def chip_rows(pair):
        chip = []
        for value in pair:
            keep = lax.dynamic_slice_in_dim(value, (core ^ flip) * half, half, 0)
            give = lax.dynamic_slice_in_dim(value, (1 - (core ^ flip)) * half, half, 0)
            got = swap_core(give)
            chip.append(jnp.concatenate([keep, got], axis=1))
        return chip

    chips = replicas // 2

    def all_x(value):
        return [swap_xor(value, bit) for bit in range(2, replicas, 2)]

    def by_order(value, others):
        whole = jnp.zeros((chips,) + value.shape, value.dtype)
        for at, part in enumerate([value] + others):
            whole = lax.dynamic_update_index_in_dim(whole, part, (replica // 2) ^ at, 0)
        return whole

    def flat_rows(whole):
        return jnp.moveaxis(whole, 1, 0).reshape(half, -1, whole.shape[-1])

    x_chip = chip_rows([state["moe"][0] for state in kept])
    x_mine, x_give = own_layer(x_chip), other_layer(x_chip)
    def both_rows(pair):
        return jnp.concatenate([own_layer(pair), swap_section(other_layer(pair))], axis=0)

    def own_columns(value):
        width = value.shape[1] // replicas
        parts = []
        for bit in range(replicas):
            piece = lax.dynamic_slice_in_dim(value, (replica ^ bit) * width, width, 1)
            parts.append(piece if bit == 0 else swap_xor(piece, bit))
        return jnp.stack(parts)

    def fold_sum(left, right, extra):
        total = mm_tn(left, right).astype(BF16)
        if extra is not None:
            total = total.reshape(folds, -1, total.shape[1])
            total = jnp.concatenate([total, extra], axis=1).reshape(-1, total.shape[2])
        return total

    def late_part(total, tie):
        if tie == ():
            return lax.psum_scatter(total, F_AX, scatter_dimension=0, tiled=True)
        else:
            step = total.shape[0] // folds
            mine = rel_scatter(
                [
                    lax.dynamic_slice_in_dim(total, ((fold_id - k) % folds) * step, step, 0)
                    for k in range(folds)
                ]
            ).astype(BF16)
        return lax.optimization_barrier((mine, tie))

    def spread_rows(mine):
        whole = jnp.zeros((replicas,) + mine.shape, BF16)
        for bit, part in enumerate(group_rows(mine)):
            whole = lax.dynamic_update_index_in_dim(whole, part, replica ^ bit, 0)
        return whole

    def side_by_side(value):
        return jnp.concatenate([value[j].astype(F32) for j in range(replicas)], axis=1)

    left_whole = group_rows(left_rows)
    model = tokens.shape[3]
    piece = model // (folds * replicas)
    count = expert_count + 1
    tall = -(-count // 16) * 16

    def with_small(grad_attn, small):
        value = small.reshape(count, folds, replicas, piece)
        value = jnp.transpose(value, (0, 2, 1, 3)).reshape(count, model)
        return jnp.concatenate([grad_attn, jnp.pad(value, ((0, tall - count), (0, 0)))], axis=0)

    def last_rows(grad_expert):
        held["rows"] = chip_rows([grad_expert])[0]
        return left_whole, stacked_parts(second_parts)

    def two(value):
        middle_row = value.shape[1] // 2
        return value[:, :middle_row], value[:, middle_row:]

    def joined_rows(one, other):
        return [jnp.concatenate(pair, axis=1) for pair in zip(one, other)]

    def last_attn(grad_attn, small, sent):
        held["attn"] = with_small(grad_attn, small)
        give_one, give_two = two(x_give)
        return swap_section(give_one), give_two, sent[1]

    def last_later(sent, crossed):
        got_one, give_two, stack = crossed
        return sent[0], stack, got_one, swap_section(give_two), all_x(got_one), all_x(x_mine)

    def first_rows(grad_expert):
        chip = (chip_rows([grad_expert])[0], held["rows"])
        mine = own_layer(chip)
        return mine, all_x(mine), swap_section(other_layer(chip)), x_own, second_stack

    def first_attn(grad_attn, small, sent):
        *sent, stack = sent
        held["second_sum"] = lax.psum_scatter(stack, F_AX, scatter_dimension=0, tiled=True)
        return both_rows((with_small(grad_attn, small), held["attn"])), sent

    def first_later(sent, crossed):
        right_out, (mine, mine_x, got, x_own) = crossed
        g_own = by_order(mine, mine_x)
        return x_own, g_own, [expert_middle(x_own[i], flat_rows(g_own)[i], *[w[i] for w in mine_w]) for i in range(half)], got, own_columns(right_out)

    grads, grad_lin = [None, None], [None, None]
    grads[1], grad_lin[1], (left_whole, second_stack, x_got, x_got_two, x_got_x, x_mine_x), _ = layer_backward(
        last_grad, kept[1], weights[1], experts_w, common, scalars[1], (),
        dict(rows=last_rows, attn=last_attn, later=last_later, blocks=last_blocks),
    )
    x_own = flat_rows(by_order(x_mine, x_mine_x))
    x_own = [x_own[i] for i in range(half)]
    mine_w = [lax.dynamic_slice_in_dim(part[0], core * half, half, 0) for part in (w_gate, w_up, w_down)]
    grads[0], grad_lin[0], later, x_got_two_x = layer_backward(
        grads[1], kept[0], weights[0], experts_w, common, scalars[0], all_x(x_got_two),
        dict(rows=first_rows, attn=first_attn, later=first_later),
    )
    x_own, g_own, middle_own, got, right_out = later
    (x_got,) = joined_rows([x_got], [x_got_two])
    x_got_x = joined_rows(x_got_x, x_got_two_x)
    left_whole = jnp.concatenate(left_whole, axis=0)
    right_out = right_out.reshape(replicas, 2, rows + tall, -1)
    extra = jnp.sum(right_out[:, :, rows:].astype(F32), axis=(0, 1)).reshape(tall, folds, piece)
    extra = jnp.pad(
        jnp.transpose(extra, (1, 0, 2)), ((0, 0), (0, 0), (0, right_out.shape[3] - piece))
    ).astype(BF16)
    right_out = right_out[:, :, :rows].reshape(-1, right_out.shape[3])
    out_shard = late_part(fold_sum(left_whole[:, model:], right_out, extra), ())
    lin_rows, second_sum = lax.optimization_barrier((both_rows(grad_lin), held["second_sum"]))
    right, got = lax.optimization_barrier((own_columns(lin_rows), got))
    got_x = all_x(got)
    g_got, x_got = by_order(got, got_x), by_order(x_got, x_got_x)
    shard = fold_sum(left_whole[:, :model], right.reshape(-1, right.shape[2]), None)
    shard, (middle_own, x_own, first_value, grads, second_sum) = lax.optimization_barrier(
        (shard, (middle_own, x_own, first_value, grads, second_sum))
    )
    x_got = [flat_rows(x_got)[i] for i in range(half)]
    g_own, g_got = [[flat_rows(value)[i] for i in range(half)] for value in (g_own, g_got)]
    middle_got = [expert_middle(x_got[i], g_got[i], *[w[i] for w in mine_w]) for i in range(half)]

    shard, (middle_got, out_shard) = late_part(shard, (middle_got, out_shard))
    shard, out_shard = spread_rows(shard), spread_rows(out_shard)
    made = []
    for i in range(half):
        inner, gate, up = zip(middle_own[i], middle_got[i])
        made.append(
            (
                (mm_tn(x_own[i], gate[0]) + mm_tn(x_got[i], gate[1])).astype(BF16),
                (mm_tn(x_own[i], up[0]) + mm_tn(x_got[i], up[1])).astype(BF16),
                (mm_tn(inner[0], g_own[i]) + mm_tn(inner[1], g_got[i])).astype(BF16),
            )
        )
    outs = [first_value, second_finish([second_sum])]
    small = side_by_side(out_shard[:, depth:, :piece])
    out_shard = side_by_side(out_shard[:, :depth])
    shard = side_by_side(shard)
    gain_one = jnp.sum(shard * joined.astype(F32), axis=1) / gains[0, 0].astype(F32)
    expert_out = []
    for slot in range(3):
        keep = made[0][slot]
        got = swap_core(keep)
        both = jnp.broadcast_to(keep.astype(F32)[None], (2,) + keep.shape)
        both = lax.dynamic_update_index_in_dim(both, got.astype(F32), 1 - core, 0)
        expert_out.append(both[None])
    layer_outputs = both_batches(outs)
    input_grads = both_batches(grads)
    return (
        layer_outputs[None, :, None],
        input_grads[None, :, None],
        jnp.stack([gain_one, small[expert_count]])[None],
        shard[None, :, :q_width],
        shard[None, :, q_width : q_width + kv_width],
        shard[None, :, q_width + kv_width : split],
        out_shard[None],
        small[:expert_count].T[None],
        expert_out[0],
        expert_out[1],
        expert_out[2],
    )


def solution(mesh):
    acts = P(None, R_AX, F_AX, None)
    rows = P(S_AX, F_AX, None)
    expert = P(S_AX, F_AX, None, None)
    stacked = P(S_AX, None, R_AX, F_AX, None)
    gain = P(S_AX, None, F_AX)
    return jax.shard_map(
        body,
        mesh=mesh,
        in_specs=(acts, acts, P(None, R_AX, None), stacked, gain)
        + (rows,) * 5
        + (expert,) * 3,
        out_specs=(stacked, stacked, gain) + (rows,) * 5 + (expert,) * 3,
        check_vma=False,
    )
```

```python
import functools

import jax
import jax.numpy as jnp
from jax import lax
from jax.experimental import pallas as pl
from jax.experimental.pallas import tpu as pltpu
from jax.sharding import PartitionSpec as P

HEAD = 128
ROPE_BASE = 1000000.0
EPS = 1e-06
MASKED = -1e30
F32 = jnp.float32
BF16 = jnp.bfloat16
S_AX, F_AX, R_AX = "section", "fsdp", "replica"
HIGHEST = lax.Precision.HIGHEST
LANES = 128
GELU_C = 0.7978845608028654
GELU_A = 0.044715


def dot(a, b):
    return lax.dot_general(a, b, (((1,), (0,)), ((), ())), preferred_element_type=F32)


def dot_nt(a, b):
    return lax.dot_general(a, b, (((1,), (1,)), ((), ())), preferred_element_type=F32)


def dot_tn(a, b):
    return lax.dot_general(a, b, (((0,), (0,)), ((), ())), preferred_element_type=F32)


def gelu_parts(x):
    t = jnp.tanh(GELU_C * (x + GELU_A * x * x * x))
    value = 0.5 * x * (1.0 + t)
    slope = 0.5 * (1.0 + t) + 0.5 * x * (1.0 - t * t) * GELU_C * (1.0 + 3.0 * GELU_A * x * x)
    return value, slope


def lane_is(shape, number):
    return lax.broadcasted_iota(jnp.int32, shape, 1) == number


def masked_mix(logits, mask):
    kept = jnp.where(mask > 0.0, logits, -1e30)
    expo = jnp.exp(kept - jnp.max(kept, axis=1, keepdims=True)) * mask
    return expo / jnp.sum(expo, axis=1, keepdims=True)


def one_hot(slots_ref, block, step, capacity):
    rows = slots_ref.shape[2]
    place = lax.broadcasted_iota(jnp.int32, (capacity, rows), 0)
    return place == slots_ref[block, step : step + 1, :]


def route_mask(tile, at, top):
    lane = lax.broadcasted_iota(jnp.int32, tile.shape, 1).astype(F32)
    named = tile.astype(F32)
    hit = lane == named[:, at : at + 1]
    for k in range(1, top):
        hit = hit | (lane == named[:, at + k : at + k + 1])
    return jnp.where(hit, 1.0, 0.0)


def weight_copies(scalars, own, pieces, buffers, sems):
    own_g, own_u, own_d = own
    parts = len(pieces[0][0])
    ff = own_g.shape[2] // parts
    is_own, flip = scalars[0], scalars[1]
    waits = {}
    for step in range(len(pieces[0])):
        for part in range(parts):
            expert = step ^ flip
            cols = pl.ds(part * ff, ff)
            sources = (own_g.at[expert, :, cols], own_u.at[expert, :, cols], own_d.at[expert, cols, :])
            for kind in range(3):
                target = buffers[kind].at[step, part]
                sem = sems.at[kind, step, part]

                @pl.when(is_own == 1)
                def _(source=sources[kind], target=target, sem=sem):
                    pltpu.make_async_copy(source, target, sem).start()

                @pl.when(is_own == 0)
                def _(source=pieces[kind][step][part], target=target, sem=sem):
                    pltpu.make_async_copy(source, target, sem).start()

                waits[kind, step, part] = pltpu.make_async_copy(
                    pieces[kind][step][part], target, sem
                )
    return waits


def split_refs(refs, counts):
    out, at = [], 0
    for count in counts:
        out.append(refs[at : at + count])
        at += count
    return out


def moe_fwd_kernel(folds, local, parts, capacity, routes_at, top, *refs):
    (scalars, router), tiles, blocks, own, flat, outs, partials, scratch = split_refs(
        refs, (2, folds, folds, 3, 3 * local * parts, 7, folds, 4)
    )
    scalars_ref = scalars
    picked_ref, gate_ref, up_ref, made_ref, grows_ref, slots, mix_ref = outs
    buf_g, buf_u, buf_d, sems = scratch
    pieces = [
        [[flat[(kind * local + step) * parts + part] for part in range(parts)] for step in range(local)]
        for kind in range(3)
    ]
    waits = weight_copies(scalars_ref, own, pieces, (buf_g, buf_u, buf_d), sems)
    rows = blocks[0].shape[0]
    width = blocks[0].shape[1]
    ff = buf_g.shape[3]
    square = (rows, rows)
    earlier = jnp.where(
        lax.broadcasted_iota(jnp.int32, square, 0) < lax.broadcasted_iota(jnp.int32, square, 1), 1.0, 0.0
    ).astype(BF16)
    same = jnp.where(
        lax.broadcasted_iota(jnp.int32, square, 0) == lax.broadcasted_iota(jnp.int32, square, 1), 1.0, 0.0
    ).astype(BF16)
    for k in range(folds):
        mask = route_mask(tiles[k][...], routes_at, top)
        mix = masked_mix(dot(blocks[k][...], router[...]), mask)
        if k == 0:
            mix_ref[...] = mix
        low = mask.astype(BF16)
        rank = dot_tn(low, earlier)
        named = dot_tn(low, same)
        place = jnp.where(named > 0.5, rank, -1.0)
        number = lax.broadcasted_iota(jnp.int32, place.shape, 0)
        for step in range(local):
            row = jnp.sum(jnp.where(number == scalars_ref[2 + step], place, 0.0), axis=0, keepdims=True)
            slots[k, step : step + 1, :] = row.astype(jnp.int32)
        for step in range(local):
            pick = one_hot(slots, k, step, capacity)
            at = pl.ds(k * capacity, capacity)
            picked_ref[step, at, :] = dot(
                jnp.where(pick, 1.0, 0.0).astype(BF16), blocks[k][...]
            ).astype(BF16)
            grows_ref[step, at, :] = lax.dot_general(
                jnp.where(pick, 1.0, 0.0), mix, (((1,), (0,)), ((), ())),
                precision=HIGHEST, preferred_element_type=F32,
            )
    for step in range(local):
        for part in range(parts):
            for kind in range(3):
                waits[kind, step, part].wait()
            cols = pl.ds(part * ff, ff)
            x = picked_ref[step]
            gate = dot(x, buf_g[step, part])
            up = dot(x, buf_u[step, part])
            gate_ref[step, :, cols] = gate
            up_ref[step, :, cols] = up
            inner = (gelu_parts(gate)[0] * up).astype(BF16)
            term = dot(inner, buf_d[step, part])
            made = term if part == 0 else made + term
        made_ref[step] = made.astype(BF16)
    for k in range(folds):
        at = pl.ds(k * capacity, capacity)
        picks, weighted = [], []
        for step in range(local):
            gates = grows_ref[step, at, :]
            own_lane = lane_is(gates.shape, scalars_ref[2 + step])
            factor = jnp.sum(jnp.where(own_lane, gates, 0.0), axis=1, keepdims=True)
            picks.append(jnp.where(one_hot(slots, k, step, capacity), 1.0, 0.0).astype(BF16))
            weighted.append((made_ref[step, at, :].astype(F32) * factor).astype(BF16))
        partials[k][...] = dot_tn(
            jnp.concatenate(picks, axis=0), jnp.concatenate(weighted, axis=0)
        ).astype(BF16)


def moe_bwd_kernel(folds, local, parts, capacity, *refs):
    (scalars, slots, gate_ref, up_ref, made_ref, grows_ref), blocks, own, flat, (ge_ref,), partials, scratch = split_refs(
        refs, (6, folds, 3, 3 * local * parts, 1, folds, 6)
    )
    buf_g, buf_u, buf_d, sems, dx_ref, dots_ref = scratch
    pieces = [
        [[flat[(kind * local + step) * parts + part] for part in range(parts)] for step in range(local)]
        for kind in range(3)
    ]
    waits = weight_copies(scalars, own, pieces, (buf_g, buf_u, buf_d), sems)
    ff = buf_g.shape[3]
    for step in range(local):
        for k in range(folds):
            at = pl.ds(k * capacity, capacity)
            pick = jnp.where(one_hot(slots, k, step, capacity), 1.0, 0.0).astype(BF16)
            dout = dot(pick, blocks[k][...])
            gates = grows_ref[step, at, :]
            own_lane = lane_is(gates.shape, scalars[2 + step])
            factor = jnp.sum(jnp.where(own_lane, gates, 0.0), axis=1, keepdims=True)
            value = jnp.sum(dout * made_ref[step, at, :].astype(F32), axis=1, keepdims=True)
            lane = lax.broadcasted_iota(jnp.int32, gates.shape, 1)
            number = scalars[2 + step]
            dots_ref[step, at, :] = jnp.where(
                (lane == number) | (lane == number + LANES // 2), value, 0.0
            )
            ge_ref[step, at, :] = (dout * factor).astype(BF16)
    for step in range(local):
        ge = ge_ref[step]
        for part in range(parts):
            for kind in range(3):
                waits[kind, step, part].wait()
            cols = pl.ds(part * ff, ff)
            grad_inner = dot_nt(ge, buf_d[step, part])
            gate = gate_ref[step, :, cols]
            up = up_ref[step, :, cols]
            value, slope = gelu_parts(gate)
            grad_gate = (grad_inner * up * slope).astype(BF16)
            grad_up = (grad_inner * value).astype(BF16)
            term = dot_nt(grad_gate, buf_g[step, part]) + dot_nt(grad_up, buf_u[step, part])
            total = term if part == 0 else total + term
        dx_ref[step] = total.astype(BF16)
    for k in range(folds):
        at = pl.ds(k * capacity, capacity)
        hot = [one_hot(slots, k, step, capacity) for step in range(local)]
        picks = jnp.concatenate([jnp.where(one, 1.0, 0.0) for one in hot], axis=0)
        width = ge_ref.shape[2]
        partials[k][:, :width] = dot_tn(
            picks.astype(BF16), jnp.concatenate([dx_ref[step, at, :] for step in range(local)], axis=0)
        ).astype(BF16)
        dots = lax.dot_general(
            picks, jnp.concatenate([dots_ref[step, at, :] for step in range(local)], axis=0),
            (((0,), (0,)), ((), ())), precision=HIGHEST, preferred_element_type=F32,
        )
        high = dots.astype(BF16).astype(F32)
        lane = lax.broadcasted_iota(jnp.int32, dots.shape, 1)
        partials[k][:, width:] = jnp.where(lane < LANES // 2, high, dots - high).astype(BF16)


def vmem(count):
    return [pl.BlockSpec(memory_space=pltpu.VMEM)] * count


def anywhere(count):
    return [pl.BlockSpec(memory_space=pl.ANY)] * count


def weight_scratch(own, local, parts):
    width, ff = own[0].shape[1], own[0].shape[2] // parts
    return [
        pltpu.VMEM((local, parts, width, ff), BF16),
        pltpu.VMEM((local, parts, width, ff), BF16),
        pltpu.VMEM((local, parts, ff, width), BF16),
        pltpu.SemaphoreType.DMA((3, local, parts)),
    ]


def cost(rows, width, ff, products):
    return pl.CostEstimate(
        flops=2 * rows * width * ff * products, bytes_accessed=2 * 3 * width * ff * 2 + 8 * rows * width,
        transcendentals=rows * ff,
    )


def moe_fwd_call(
    scalars, tiles, routes_at, router, blocks, own, flat, folds, local, rows, parts, width, ff, capacity, top, tile_at
):
    router, router_at = router
    picked_rows = folds * capacity
    shapes = [
        jax.ShapeDtypeStruct((local, picked_rows, width), BF16),
        jax.ShapeDtypeStruct((local, picked_rows, ff), F32),
        jax.ShapeDtypeStruct((local, picked_rows, ff), F32),
        jax.ShapeDtypeStruct((local, picked_rows, width), BF16),
        jax.ShapeDtypeStruct((local, picked_rows, LANES), F32),
        jax.ShapeDtypeStruct((folds, local, rows), jnp.int32),
        jax.ShapeDtypeStruct((rows, LANES), F32),
    ] + [jax.ShapeDtypeStruct((rows, width), BF16)] * folds
    out = pl.pallas_call(
        functools.partial(moe_fwd_kernel, folds, local, parts, capacity, routes_at, top),
        out_shape=shapes,
        in_specs=[
            pl.BlockSpec(memory_space=pltpu.SMEM),
            pl.BlockSpec((router.shape[0], LANES), lambda i: (0, router_at)),
        ]
        + [pl.BlockSpec((rows, LANES), lambda i: (0, tile_at))] * folds
        + vmem(folds) + anywhere(3 + len(flat)),
        grid=(1,),
        out_specs=vmem(len(shapes)),
        scratch_shapes=weight_scratch(own, local, parts),
        cost_estimate=cost(local * picked_rows, width, ff, 3),
        compiler_params=pltpu.CompilerParams(vmem_limit_bytes=56 << 20),
    )(scalars, router, *tiles, *blocks, *own, *flat)
    return out[:7], out[7:]


def moe_bwd_call(scalars, kept, blocks, own, flat, folds, local, rows, parts, width, ff, capacity, top, tile_at):
    _, gate_pre, up_pre, made, gate_rows, slots, _ = kept
    picked_rows = folds * capacity
    shapes = [jax.ShapeDtypeStruct((local, picked_rows, width), BF16)] + [
        jax.ShapeDtypeStruct((rows, width + LANES), BF16)
    ] * folds
    out = pl.pallas_call(
        functools.partial(moe_bwd_kernel, folds, local, parts, capacity),
        out_shape=shapes,
        in_specs=[pl.BlockSpec(memory_space=pltpu.SMEM)]
        + vmem(5 + folds) + anywhere(3 + len(flat)),
        out_specs=vmem(len(shapes)),
        scratch_shapes=weight_scratch(own, local, parts)
        + [pltpu.VMEM((local, picked_rows, width), BF16), pltpu.VMEM((local, picked_rows, LANES), F32)],
        cost_estimate=cost(local * picked_rows, width, ff, 3),
        compiler_params=pltpu.CompilerParams(vmem_limit_bytes=56 << 20),
    )(scalars, slots, gate_pre, up_pre, made, gate_rows, *blocks, *own, *flat)
    return out[0], out[1:]


def mm(a, b):
    return jnp.dot(a, b, preferred_element_type=F32)


def mm_nt(a, b):
    return lax.dot_general(a, b, (((1,), (1,)), ((), ())), preferred_element_type=F32)


def mm_shares(a, shares):
    if shares.ndim == 2:
        return mm_nt(a, shares)
    width = shares.shape[2]
    return sum(mm_nt(a[:, j * width : (j + 1) * width], shares[j]) for j in range(shares.shape[0]))


def mm_tn(a, b):
    return lax.dot_general(a, b, (((0,), (0,)), ((), ())), preferred_element_type=F32)


def ein(spec, a, b):
    return jnp.einsum(spec, a, b, preferred_element_type=F32)


def rel_gather(value):
    folds = lax.axis_size(F_AX)
    parts = [value]
    for k in range(1, folds):
        parts.append(lax.ppermute(value, F_AX, [(i, (i + k) % folds) for i in range(folds)]))
    return parts


def rel_scatter(parts):
    folds = lax.axis_size(F_AX)
    total = parts[0].astype(F32)
    for k in range(1, folds):
        got = lax.ppermute(parts[k], F_AX, [(i, (i - k) % folds) for i in range(folds)])
        total = total + got.astype(F32)
    return total


def send_back(parts):
    folds = lax.axis_size(F_AX)
    return [parts[0]] + [
        lax.ppermute(parts[k], F_AX, [(i, (i - k) % folds) for i in range(folds)]) for k in range(1, folds)
    ]


def add_up(parts):
    total = parts[0].astype(F32)
    for part in parts[1:]:
        total = total + part.astype(F32)
    return total


def swap_section(value):
    return lax.ppermute(value, S_AX, [(0, 1), (1, 0)])


def swap_core(value):
    count = lax.axis_size(R_AX)
    return lax.ppermute(value, R_AX, [(i, i ^ 1) for i in range(count)])


def rope_turn(values, cos, sin):
    half = HEAD // 2
    turned = jnp.concatenate([-values[..., half:], values[..., :half]], axis=-1)
    return values * cos + turned * sin


def rope_back(grads, cos, sin):
    half = HEAD // 2
    scaled = grads * sin
    turned = jnp.concatenate([scaled[..., half:], -scaled[..., :half]], axis=-1)
    return grads * cos + turned


def layout(lengths, position):
    bounds = jnp.cumsum(lengths)
    passed = (position[:, None] >= bounds[None, :]).astype(jnp.int32)
    segment = jnp.sum(passed, axis=1)
    start = jnp.sum(passed * lengths[None, :], axis=1)
    return segment, (position - start).astype(F32)


def gated(gate, up):
    return jax.nn.gelu(gate) * up


def attention_in(hidden, gain):
    scale = lax.rsqrt(jnp.mean(hidden * hidden, axis=1, keepdims=True) + EPS)
    normed = hidden * scale
    return scale, normed, (normed * gain.astype(F32)).astype(BF16)


def turn_heads(lin, common, kv_width):
    rows = lin.shape[0]
    q_width = lin.shape[1] - 2 * kv_width
    turned = rope_turn(
        lin[:, : q_width + kv_width].astype(F32).reshape(rows, -1, HEAD), common["cos"], common["sin"]
    ).astype(BF16).reshape(rows, -1)
    kv = jnp.concatenate([turned[:, q_width:], lin[:, q_width + kv_width :].astype(BF16)], axis=1)
    return turned[:, :q_width], kv


def grouped_heads(value, groups):
    rows = value.shape[0]
    return value.reshape(rows, groups, -1, HEAD)


def attend(query, kv_all, allowed, groups):
    keys = kv_all[:, : groups * HEAD].reshape(-1, groups, HEAD)
    values = kv_all[:, groups * HEAD :].reshape(-1, groups, HEAD)
    raw = ein("tgha,sga->ghts", grouped_heads(query, groups), keys) * HEAD ** (-0.5)
    scores = jnp.where(allowed[None, None], raw, MASKED)
    top = jnp.max(scores, axis=3, keepdims=True)
    expo = jnp.exp(scores - top)
    probs = expo / jnp.sum(expo, axis=3, keepdims=True)
    mixed = ein("ghts,sga->tgha", probs.astype(BF16), values)
    return mixed.reshape(query.shape), probs


def attend_back(grad_mixed, mixed, probs, query, kv_all, groups):
    rows = query.shape[0]
    keys = kv_all[:, : groups * HEAD].reshape(-1, groups, HEAD)
    values = kv_all[:, groups * HEAD :].reshape(-1, groups, HEAD)
    grad_grouped = grouped_heads(grad_mixed, groups)
    delta = jnp.sum(
        grad_grouped.astype(F32) * grouped_heads(mixed, groups), axis=3
    )
    delta = jnp.transpose(delta, (1, 2, 0))[..., None]
    grad_probs = ein("tgha,sga->ghts", grad_grouped, values)
    grad_scores = (probs * (grad_probs - delta)).astype(BF16)
    score_scale = HEAD ** (-0.5)
    grad_query = (ein("ghts,sga->tgha", grad_scores, keys) * score_scale).reshape(rows, -1, HEAD)
    grad_key = ein("ghts,tgha->sga", grad_scores, grouped_heads(query, groups)) * score_scale
    grad_value = ein("ghts,tgha->sga", probs.astype(BF16), grad_grouped)
    count = kv_all.shape[0]
    grad_kv = jnp.concatenate(
        [grad_key.reshape(count, -1), grad_value.reshape(count, -1)], axis=1
    ).astype(BF16)
    return grad_query, grad_kv


def moe_forward(router, tiles, routes_at, scalars, experts_w, size, blocks):
    outs, partials = moe_fwd_call(
        scalars, tiles, routes_at, router, blocks, *experts_w, **size
    )
    return partials, outs


def moe_backward(blocks, kept, scalars, experts_w, size, tie, hooks):
    blocks, tied = lax.optimization_barrier((blocks, tie))
    grad_expert, partials = moe_bwd_call(scalars, kept, blocks, *experts_w, **size)
    sent = hooks["rows"](grad_expert)
    summed, sent = lax.optimization_barrier((rel_scatter(partials), sent))
    width = blocks[0].shape[1]
    tail = summed[:, width:]
    half = LANES // 2
    dots = tail[:, :half] + tail[:, half:]
    return summed[:, :width], jnp.pad(dots, ((0, 0), (0, half))), sent, tied


def layer_forward(layer_in, weights, experts_w, common, tiles, routes_at, scalars, tie, projected=None, out_product=None):
    gains, w_qkv, w_out, router = weights
    groups = common["groups"]
    hidden = layer_in.astype(F32)
    scale, normed, attn_in = attention_in(hidden, gains[0])
    lin = mm(attn_in, w_qkv) if projected is None else projected
    lin, tied_lin = lax.optimization_barrier((lin, tie.get("lin", ())))
    query, kv = turn_heads(lin, common, groups * HEAD)
    kv_all, tied_kv = lax.optimization_barrier(
        (jnp.concatenate(rel_gather(kv), axis=0), tie.get("kv", ()))
    )
    mixed, probs = attend(query, kv_all, common["allowed"], groups)
    mixed_low = mixed.astype(BF16)
    more = tie["mixed"](tied_lin, tied_kv, attn_in, mixed_low) if "mixed" in tie else ()
    mixed_low, more = lax.optimization_barrier((mixed_low, more))
    if out_product is None:
        residual = hidden + mm(mixed_low, w_out)
    else:
        residual = hidden + out_product(mixed_low).astype(F32)
    scale_two = lax.rsqrt(jnp.mean(residual * residual, axis=1, keepdims=True) + EPS)
    normed_two = residual * scale_two
    moe_in = (normed_two * gains[1].astype(F32)).astype(BF16)
    if "moe" in tie:
        moe_in, experts_w, more = tie["moe"](moe_in, experts_w, more)
    blocks, tied = lax.optimization_barrier((rel_gather(moe_in), more))
    parts, moe_kept = moe_forward(tie["router"], tiles, routes_at, scalars, experts_w, common["size"], blocks)
    finish = lambda got: (residual + add_up(got)).astype(BF16)
    out = finish(send_back(parts)) if "last" not in tie else (parts, finish)
    kept = dict(
        scale=scale, normed=normed, attn_in=attn_in, query=query, kv=kv,
        kv_all=kv_all, mixed=mixed, probs=probs, mixed_low=mixed_low, scale_two=scale_two,
        normed_two=normed_two, moe_in=moe_in, mix=moe_kept[6], moe=moe_kept,
    )
    return out, kept, experts_w, tied


def layer_backward(grad_low, kept, weights, experts_w, common, scalars, tie, hooks):
    gains, w_qkv, w_out, router = weights
    groups = common["groups"]
    grad_out = grad_low.astype(F32)
    rows = grad_out.shape[0]
    blocks = hooks["blocks"] if "blocks" in hooks else rel_gather(grad_low)
    grad_moe_in, dots, sent, tied = moe_backward(
        blocks, kept["moe"], scalars, experts_w, common["size"], tie, hooks
    )
    mix = kept["mix"]
    grad_logits = mix * (dots - jnp.sum(mix * dots, axis=1, keepdims=True))
    moe_in = kept["moe_in"]
    count = common["experts"]
    high = grad_logits.astype(BF16)
    rest = (grad_logits - high.astype(F32)).astype(BF16)
    both = mm_tn(jnp.concatenate([high[:, :count], rest[:, :count]], axis=1), moe_in)
    grad_router = both[:count] + both[count:]
    grad_moe_in = grad_moe_in + mm_nt(high, router) + mm_nt(rest, router)
    normed_two = kept["normed_two"]
    grad_norm = grad_moe_in * gains[1].astype(F32)
    grad_gain_two = jnp.sum(grad_moe_in * normed_two, axis=0)
    grad_mid = grad_out + kept["scale_two"] * (
        grad_norm - normed_two * jnp.mean(grad_norm * normed_two, axis=1, keepdims=True)
    )
    grad_attn = grad_mid.astype(BF16)
    small = jnp.concatenate([grad_router, grad_gain_two[None]], axis=0).astype(BF16)
    crossed = hooks["attn"](grad_attn, small, sent)
    grad_mixed = mm_shares(grad_attn, w_out).astype(BF16)
    grad_query, grad_kv = attend_back(
        grad_mixed, kept["mixed"], kept["probs"], kept["query"], kept["kv_all"], groups
    )
    grad_kv, crossed = lax.optimization_barrier((grad_kv, crossed))
    later = hooks["later"](sent, crossed)
    own = rel_scatter([grad_kv[k * rows : (k + 1) * rows] for k in range(lax.axis_size(F_AX))])
    own, later = lax.optimization_barrier((own, later))
    cos, sin = common["cos"], common["sin"]
    kv_width = groups * HEAD
    grad_lin = jnp.concatenate(
        [
            rope_back(grad_query, cos, sin).reshape(rows, -1),
            rope_back(own[:, :kv_width].reshape(rows, -1, HEAD), cos, sin).reshape(rows, -1),
            own[:, kv_width:],
        ],
        axis=1,
    ).astype(BF16)
    grad_attn_in = mm_shares(grad_lin, w_qkv)
    normed = kept["normed"]
    grad_norm = grad_attn_in * gains[0].astype(F32)
    grad_in = grad_mid + kept["scale"] * (
        grad_norm - normed * jnp.mean(grad_norm * normed, axis=1, keepdims=True)
    )
    return grad_in.astype(BF16), grad_lin, later, tied


def expert_middle(rows_in, grad_rows, gate_w, up_w, down_w):
    value, slope = gelu_parts(mm(rows_in, gate_w))
    up_pre = mm(rows_in, up_w)
    grad_inner = mm_nt(grad_rows, down_w)
    return (
        (value * up_pre).astype(BF16),
        (grad_inner * up_pre * slope).astype(BF16),
        (grad_inner * value).astype(BF16),
    )


def body(
    tokens, cotangent, seq_lengths, routes, gains, w_query, w_key, w_value, w_out, w_router, w_gate, w_up, w_down
):
    section = lax.axis_index(S_AX)
    is_first = section == 0
    fold_id = lax.axis_index(F_AX)
    replica = lax.axis_index(R_AX)
    core = replica % 2
    flip = (replica // 2) % 2
    folds, replicas = lax.axis_size(F_AX), lax.axis_size(R_AX)
    rows = tokens.shape[2]
    top = routes.shape[4]
    local = w_gate.shape[1]
    expert_count = w_router.shape[2]
    kv_width = w_key.shape[2]
    q_width = w_query.shape[2]
    capacity = rows * top // expert_count

    def own_batch(value):
        return lax.dynamic_index_in_dim(value, section, 0, keepdims=False)

    def swap_xor(value, bit):
        return lax.ppermute(value, R_AX, [(i, i ^ bit) for i in range(replicas)])

    def own_layer(pair):
        return jnp.where(is_first, pair[0], pair[1])

    def other_layer(pair):
        return jnp.where(is_first, pair[1], pair[0])

    def by_section(keep, got):
        return jnp.stack([jnp.where(is_first, keep, got), jnp.where(is_first, got, keep)])

    def both_batches(pair):
        return by_section(own_layer(pair), swap_section(other_layer(pair)))

    split = q_width + 2 * kv_width
    routes_at = HEAD // 4

    def widened(pieces):
        weights_part, routes_part = pieces
        routes_part = jnp.pad(routes_part.astype(BF16), ((0, weights_part.shape[0] - rows), (0, 0)))
        gap = jnp.zeros((weights_part.shape[0], routes_at - weights_part.shape[1]), BF16)
        whole = jnp.concatenate([weights_part, gap, routes_part], axis=1)
        return jnp.pad(whole, ((0, 0), (0, HEAD - whole.shape[1])))

    small = jnp.concatenate([w_router[0], gains[0].T], axis=1)
    my_routes = own_batch(routes[0, :, 0])
    give_routes = lax.dynamic_index_in_dim(routes[0, :, 0], 1 - section, 0, keepdims=False)
    joined = jnp.concatenate([w_query[0], w_key[0], w_value[0]], axis=1)
    depth = joined.shape[0]

    def column_share(value):
        width = value.shape[1] // replicas
        return lax.dynamic_slice_in_dim(value, replica * width, width, 1)

    def stacked_parts(parts):
        whole = jnp.zeros((folds,) + parts[0].shape, parts[0].dtype)
        for k, part in enumerate(parts):
            whole = lax.dynamic_update_index_in_dim(whole, part, (fold_id - k) % folds, 0)
        return whole.reshape((-1,) + parts[0].shape[1:])

    def stacked_rows(value):
        return stacked_parts(rel_gather(value))

    def of_first(value):
        return jnp.where(is_first, value, swap_section(value))

    def share_back(value):
        whole = jnp.zeros(value.shape, value.dtype)
        for bit in range(replicas):
            got = value[bit] if bit == 0 else swap_xor(value[bit], bit)
            whole = lax.dynamic_update_index_in_dim(whole, got, replica ^ bit, 0)
        return jnp.concatenate([whole[j] for j in range(replicas)], axis=1)

    def group_rows(value):
        parts = []
        for bit in range(0, replicas, 2):
            same = value if bit == 0 else swap_xor(value, bit)
            parts += [same, swap_core(same)]
        return parts

    my_tokens = own_batch(tokens[:, 0])
    token_group = jnp.concatenate(group_rows(my_tokens), axis=0)
    head_own = column_share(joined)
    lin_width = head_own.shape[1]
    head_swap = swap_section(jnp.concatenate([head_own, widened((small, give_routes))], axis=1))
    got_routes = head_swap[:rows, lin_width + routes_at : lin_width + routes_at + top].astype(jnp.int32)
    both_routes = jnp.where(
        is_first,
        jnp.concatenate([my_routes, got_routes], axis=1),
        jnp.concatenate([got_routes, my_routes], axis=1),
    )
    tail_cols = jnp.where(is_first, small, head_swap[:, lin_width : lin_width + small.shape[1]])
    head_got = jnp.concatenate(
        [jnp.where(is_first, head_own, head_swap[:, :lin_width]), widened((tail_cols, both_routes))], axis=1
    )
    part_ff = w_gate.shape[3] // 2
    pieces = []
    for part, axis in ((w_gate, 1), (w_up, 1), (w_down, 0)):
        chosen = lax.dynamic_index_in_dim(part[0], flip, 0, keepdims=False)
        pieces.append(lax.dynamic_slice_in_dim(chosen, core * part_ff, part_ff, axis))
    pieces, head_got = lax.optimization_barrier((pieces, head_got))
    crossed_y = [swap_section(pieces[0]), None, None]
    last_grad = own_batch(cotangent[:, 0])
    head_got, last_blocks = lax.optimization_barrier((head_got, rel_gather(last_grad)))
    head_parts, crossed_y[0] = lax.optimization_barrier((rel_gather(head_got), crossed_y[0]))
    head_block = stacked_parts(head_parts)
    tiles = head_parts
    crossed_y[1:] = [swap_section(value) for value in pieces[1:]]
    first = fold_id * local
    numbers = first + (jnp.arange(local, dtype=jnp.int32) ^ flip)
    scalars = [
        jnp.concatenate([jnp.stack([(section == layer).astype(jnp.int32), flip]), numbers]).astype(jnp.int32)
        for layer in range(2)
    ]
    first_tail = head_block[:, lin_width:]
    out_block = of_first(column_share(w_out[0]))
    head_block, out_block = lax.optimization_barrier((head_block, out_block))
    out_parts = rel_gather(out_block)
    group_in = attention_in(token_group.astype(F32), first_tail[:, expert_count])[2]
    first_lin = share_back(
        mm(group_in, head_block[:, :lin_width]).astype(BF16).reshape(replicas, rows, lin_width)
    )

    def first_out(mixed_low):
        out_block = held["out_block"]
        group = jnp.concatenate(group_rows(mixed_low), axis=0)
        made = mm(group, out_block).astype(BF16)
        return share_back(made.reshape(replicas, rows, -1))

    shard = jnp.concatenate([joined, jnp.pad(small, ((0, 0), (0, HEAD - small.shape[1]))), w_out[0]], axis=1)
    share = depth // (2 * replicas)
    keep = lax.dynamic_slice_in_dim(shard, (section * replicas + replica) * share, share, 0)
    give = lax.dynamic_slice_in_dim(shard, ((1 - section) * replicas + replica) * share, share, 0)
    give, _ = lax.optimization_barrier((give, head_got))
    got = swap_section(give)

    def whole_weights(layer, keep, got):
        piece = jnp.where(section == layer, keep, got)
        full = lax.all_gather(piece, (F_AX, S_AX, R_AX), axis=0, tiled=True)
        tail = full[:, split : split + LANES]
        held["full"] = full
        return tail[:, expert_count : expert_count + 2].T, full[:, :split], full[:, split + LANES :], tail

    first_w = (
        first_tail[:, expert_count : expert_count + 2].T, None, None, first_tail
    )
    size = dict(
        folds=folds, local=local, rows=rows, parts=2, width=tokens.shape[3], ff=w_gate.shape[3],
        capacity=capacity, top=top, tile_at=lin_width // LANES,
    )

    lengths = own_batch(seq_lengths[:, 0])
    position = fold_id * rows + jnp.arange(rows, dtype=jnp.int32)
    order = (fold_id - jnp.arange(folds)) % folds
    key_pos = (order[:, None] * rows + jnp.arange(rows)[None, :]).reshape(-1).astype(jnp.int32)
    segment, offset = layout(lengths, position)
    key_seg, _ = layout(lengths, key_pos)
    freq = ROPE_BASE ** (-2.0 * jnp.arange(HEAD // 2, dtype=F32) / HEAD)
    angles = offset[:, None] * freq
    angles = jnp.concatenate([angles, angles], axis=1)[:, None, :]
    common = dict(
        cos=jnp.cos(angles), sin=jnp.sin(angles), groups=kv_width // HEAD, size=size,
        experts=expert_count,
        allowed=(segment[:, None] == key_seg[None, :]) & (key_pos[None, :] <= position[:, None]),
    )

    def first_mixed(tied_lin, tied, attn_in, mixed_low):
        gate_x, up_y, parts = tied
        held["out_block"] = stacked_parts(parts)
        held["second"] = whole_weights(1, *tied_lin)
        return (crossed_y[0], up_y), (gate_x,)

    def first_moe(moe_in, own, more):
        same, cross = more
        same, cross, moe_in = lax.optimization_barrier(((*same, crossed_y[2]), cross, moe_in))
        cross = [*cross, swap_xor(same[1], 2), swap_xor(same[2], 2)]
        flat = []
        for one, two in zip(same, cross):
            flat += [one, swap_core(one), two, swap_core(two)]
        return moe_in, (own, flat), ()

    held = {}
    first_value, first_kept, experts_w, _ = layer_forward(
        my_tokens, first_w, (w_gate[0], w_up[0], w_down[0]), common, tiles, routes_at, scalars[0],
        dict(router=(head_block, lin_width // LANES), lin=(keep, got), kv=(swap_xor(crossed_y[0], 2), crossed_y[1], out_parts), mixed=first_mixed, moe=first_moe),
        first_lin, first_out,
    )
    head_share, out_share, _ = lax.optimization_barrier(
        (head_block[:, :lin_width], held["out_block"], first_kept["moe"][1])
    )
    weights_first = (
        first_w[0], lax.all_gather(head_share, R_AX, axis=0), lax.all_gather(out_share, R_AX, axis=0), first_tail
    )

    second_w = held["second"]

    def left_pair(attn_in, mixed_low):
        pair = (
            jnp.concatenate([first_kept["attn_in"], first_kept["mixed_low"]], axis=1),
            jnp.concatenate([attn_in, mixed_low], axis=1),
        )
        return own_layer(pair), swap_section(other_layer(pair))

    second_value, second_kept, _, tied = layer_forward(
        first_value, second_w, experts_w, common, tiles, routes_at + top, scalars[1],
        dict(
            mixed=lambda one, two, attn_in, mixed_low: (attn_in, mixed_low),
            moe=lambda moe_in, own, more: (moe_in, own, (left_pair(*more), weights_first)),
            last=True, router=(held["full"], split // LANES),
        ),
    )
    left_rows, weights_first = tied
    second_parts, second_finish = second_value
    left_rows = jnp.concatenate(left_rows, axis=0)
    kept, weights = [first_kept, second_kept], [weights_first, second_w]

    half = local // 2

    def chip_rows(pair):
        chip = []
        for value in pair:
            keep = lax.dynamic_slice_in_dim(value, (core ^ flip) * half, half, 0)
            give = lax.dynamic_slice_in_dim(value, (1 - (core ^ flip)) * half, half, 0)
            got = swap_core(give)
            chip.append(jnp.concatenate([keep, got], axis=1))
        return chip

    chips = replicas // 2

    def all_x(value):
        return [swap_xor(value, bit) for bit in range(2, replicas, 2)]

    def by_order(value, others):
        whole = jnp.zeros((chips,) + value.shape, value.dtype)
        for at, part in enumerate([value] + others):
            whole = lax.dynamic_update_index_in_dim(whole, part, (replica // 2) ^ at, 0)
        return whole

    def flat_rows(whole):
        return jnp.moveaxis(whole, 1, 0).reshape(half, -1, whole.shape[-1])

    x_chip = chip_rows([state["moe"][0] for state in kept])
    x_mine, x_give = own_layer(x_chip), other_layer(x_chip)
    def both_rows(pair):
        return jnp.concatenate([own_layer(pair), swap_section(other_layer(pair))], axis=0)

    def own_columns(value):
        width = value.shape[1] // replicas
        parts = []
        for bit in range(replicas):
            piece = lax.dynamic_slice_in_dim(value, (replica ^ bit) * width, width, 1)
            parts.append(piece if bit == 0 else swap_xor(piece, bit))
        return jnp.stack(parts)

    def fold_sum(left, right, extra):
        total = mm_tn(left, right).astype(BF16)
        if extra is not None:
            total = total.reshape(folds, -1, total.shape[1])
            total = jnp.concatenate([total, extra], axis=1).reshape(-1, total.shape[2])
        return total

    def late_part(total, tie):
        if tie == ():
            return lax.psum_scatter(total, F_AX, scatter_dimension=0, tiled=True)
        else:
            step = total.shape[0] // folds
            mine = rel_scatter(
                [
                    lax.dynamic_slice_in_dim(total, ((fold_id - k) % folds) * step, step, 0)
                    for k in range(folds)
                ]
            ).astype(BF16)
        return lax.optimization_barrier((mine, tie))

    def spread_rows(mine):
        whole = jnp.zeros((replicas,) + mine.shape, BF16)
        for bit, part in enumerate(group_rows(mine)):
            whole = lax.dynamic_update_index_in_dim(whole, part, replica ^ bit, 0)
        return whole

    def side_by_side(value):
        return jnp.concatenate([value[j].astype(F32) for j in range(replicas)], axis=1)

    left_whole = group_rows(left_rows)
    model = tokens.shape[3]
    piece = model // (folds * replicas)
    count = expert_count + 1
    tall = -(-count // 16) * 16

    def with_small(grad_attn, small):
        value = small.reshape(count, folds, replicas, piece)
        value = jnp.transpose(value, (0, 2, 1, 3)).reshape(count, model)
        return jnp.concatenate([grad_attn, jnp.pad(value, ((0, tall - count), (0, 0)))], axis=0)

    def last_rows(grad_expert):
        held["rows"] = chip_rows([grad_expert])[0]
        return left_whole, stacked_parts(second_parts)

    def two(value):
        middle_row = value.shape[1] // 2
        return value[:, :middle_row], value[:, middle_row:]

    def joined_rows(one, other):
        return [jnp.concatenate(pair, axis=1) for pair in zip(one, other)]

    def last_attn(grad_attn, small, sent):
        held["attn"] = with_small(grad_attn, small)
        give_one, give_two = two(x_give)
        return swap_section(give_one), give_two, sent[1]

    def last_later(sent, crossed):
        got_one, give_two, stack = crossed
        return sent[0], stack, got_one, swap_section(give_two), all_x(got_one), all_x(x_mine)

    def first_rows(grad_expert):
        chip = (chip_rows([grad_expert])[0], held["rows"])
        mine = own_layer(chip)
        return mine, all_x(mine), swap_section(other_layer(chip)), x_own, second_stack

    def first_attn(grad_attn, small, sent):
        *sent, stack = sent
        held["second_sum"] = lax.psum_scatter(stack, F_AX, scatter_dimension=0, tiled=True)
        return both_rows((with_small(grad_attn, small), held["attn"])), sent

    def first_later(sent, crossed):
        right_out, (mine, mine_x, got, x_own) = crossed
        g_own = by_order(mine, mine_x)
        return x_own, g_own, [expert_middle(x_own[i], flat_rows(g_own)[i], *[w[i] for w in mine_w]) for i in range(half)], got, own_columns(right_out)

    grads, grad_lin = [None, None], [None, None]
    grads[1], grad_lin[1], (left_whole, second_stack, x_got, x_got_two, x_got_x, x_mine_x), _ = layer_backward(
        last_grad, kept[1], weights[1], experts_w, common, scalars[1], (),
        dict(rows=last_rows, attn=last_attn, later=last_later, blocks=last_blocks),
    )
    x_own = flat_rows(by_order(x_mine, x_mine_x))
    x_own = [x_own[i] for i in range(half)]
    mine_w = [lax.dynamic_slice_in_dim(part[0], core * half, half, 0) for part in (w_gate, w_up, w_down)]
    grads[0], grad_lin[0], later, x_got_two_x = layer_backward(
        grads[1], kept[0], weights[0], experts_w, common, scalars[0], all_x(x_got_two),
        dict(rows=first_rows, attn=first_attn, later=first_later),
    )
    x_own, g_own, middle_own, got, right_out = later
    (x_got,) = joined_rows([x_got], [x_got_two])
    x_got_x = joined_rows(x_got_x, x_got_two_x)
    left_whole = jnp.concatenate(left_whole, axis=0)
    right_out = right_out.reshape(replicas, 2, rows + tall, -1)
    extra = jnp.sum(right_out[:, :, rows:].astype(F32), axis=(0, 1)).reshape(tall, folds, piece)
    extra = jnp.pad(
        jnp.transpose(extra, (1, 0, 2)), ((0, 0), (0, 0), (0, right_out.shape[3] - piece))
    ).astype(BF16)
    right_out = right_out[:, :, :rows].reshape(-1, right_out.shape[3])
    out_shard = late_part(fold_sum(left_whole[:, model:], right_out, extra), ())
    lin_rows, second_sum = lax.optimization_barrier((both_rows(grad_lin), held["second_sum"]))
    right, got = lax.optimization_barrier((own_columns(lin_rows), got))
    got_x = all_x(got)
    g_got, x_got = by_order(got, got_x), by_order(x_got, x_got_x)
    shard = fold_sum(left_whole[:, :model], right.reshape(-1, right.shape[2]), None)
    shard, (middle_own, x_own, first_value, grads, second_sum) = lax.optimization_barrier(
        (shard, (middle_own, x_own, first_value, grads, second_sum))
    )
    x_got = [flat_rows(x_got)[i] for i in range(half)]
    g_own, g_got = [[flat_rows(value)[i] for i in range(half)] for value in (g_own, g_got)]
    middle_got = [expert_middle(x_got[i], g_got[i], *[w[i] for w in mine_w]) for i in range(half)]

    shard, (middle_got, out_shard) = late_part(shard, (middle_got, out_shard))
    shard, out_shard = spread_rows(shard), spread_rows(out_shard)
    made = []
    for i in range(half):
        inner, gate, up = zip(middle_own[i], middle_got[i])
        made.append(
            (
                (mm_tn(x_own[i], gate[0]) + mm_tn(x_got[i], gate[1])).astype(BF16),
                (mm_tn(x_own[i], up[0]) + mm_tn(x_got[i], up[1])).astype(BF16),
                (mm_tn(inner[0], g_own[i]) + mm_tn(inner[1], g_got[i])).astype(BF16),
            )
        )
    outs = [first_value, second_finish([second_sum])]
    small = side_by_side(out_shard[:, depth:, :piece])
    out_shard = side_by_side(out_shard[:, :depth])
    shard = side_by_side(shard)
    gain_one = jnp.sum(shard * joined.astype(F32), axis=1) / gains[0, 0].astype(F32)
    expert_out = []
    for slot in range(3):
        keep = jnp.stack([one[slot] for one in made])
        got = swap_core(keep)
        both = jnp.concatenate(
            [jnp.where(core == 0, keep, got), jnp.where(core == 0, got, keep)], axis=0
        )
        expert_out.append(both.astype(F32)[None])
    layer_outputs = both_batches(outs)
    input_grads = both_batches(grads)
    return (
        layer_outputs[None, :, None],
        input_grads[None, :, None],
        jnp.stack([gain_one, small[expert_count]])[None],
        shard[None, :, :q_width],
        shard[None, :, q_width : q_width + kv_width],
        shard[None, :, q_width + kv_width : split],
        out_shard[None],
        small[:expert_count].T[None],
        expert_out[0],
        expert_out[1],
        expert_out[2],
    )


def solution(mesh):
    acts = P(None, R_AX, F_AX, None)
    rows = P(S_AX, F_AX, None)
    expert = P(S_AX, F_AX, None, None)
    stacked = P(S_AX, None, R_AX, F_AX, None)
    gain = P(S_AX, None, F_AX)
    return jax.shard_map(
        body,
        mesh=mesh,
        in_specs=(acts, acts, P(None, R_AX, None), stacked, gain)
        + (rows,) * 5
        + (expert,) * 3,
        out_specs=(stacked, stacked, gain) + (rows,) * 5 + (expert,) * 3,
        check_vma=False,
    )
```
